32 devices in a mesh: grp: 2 (over x), vir: 16 (over z, y, core).
Axes of the slice: x: 2, y: 2, z: 4, core: 2. Of those that a mesh axis runs over, the one named last changes fastest.
Arguments:
- amplitudes: bfloat16 [32, 1024, 1024], P(('grp', 'vir')), parts along dimension 0, may hold values from -6 to 6
- couplings: bfloat16 [4096, 16, 2048], P(('grp', 'vir')), parts along dimension 0, may hold values from -0.125 to 0.125
- occ_irrep: int32 [32], P('grp'), parts along dimension 0, may hold values from 0 to 7
- pair_irrep: int32 [1], replicated, may hold values from 0 to 7
- j_irrep: int32 [2], replicated, may hold values from 0 to 7
- block_sizes: int32 [16], P('grp'), parts along dimension 0, may hold values from 1 to 256, 1024 in all
- owner: int32 [512, 1], P('grp'), parts along dimension 0, may hold values from 0 to 15; in each aligned block of 256 rows (0 to 255, 256 to 511, ...) at most 32 rows name the same one
Outputs:
- cycle: float32 [2048, 2048], P(('grp', 'vir')), parts along dimension 0
The draws below stay inside these ranges and needn't reach their ends.
There are 2 independent parts, one for each index of `grp`. The reference program is written for one: setup_inputs(seed, part) draws one part's arguments, and reference() takes and returns one part's arrays. A program takes and returns all parts, laid end to end along the dimension named above; an argument that names none is the same for every part. Nothing has to cross between parts.
Inputs may be any that keep to these rules, and one draw needn't show every extreme that they name: `block_sizes`: the eight blocks are consecutive in virtual order and sum to 1024; the largest holds exactly 256 virtuals. `owner`: no device owns more than 32 blocks, and some device owns exactly 32.
All inputs are finite; a program needn't handle non-finite values.
Results may differ from the reference program's by a relative error of at most 0.0003.
Values may be sent and summed in bfloat16 or wider, within the bound.
No kernel may reach another device: no remote copies, remote signals or barrier semaphores. Data moves between devices by JAX's collectives and lax.ppermute only.
A program may use at most 128 MiB of HBM per device.

```python
import math
import jax
import jax.numpy as jnp
import numpy as np

V = 1024
J = 2
BS = 4
MOST = 256
O = 16
VB = 256
CAP = 32
N_VIR = 16


def place_ends(values, own_key, low, high):
    longest = values.shape.index(max(values.shape))
    spots = []
    for shift in (0, 1):
        where = [jax.random.randint(jax.random.fold_in(own_key, axis), (), 0, length) for axis, length in enumerate(values.shape)]
        where[longest] = (where[longest] + shift) % values.shape[longest]
        spots.append(tuple(where))
    return values.at[spots[0]].set(low).at[spots[1]].set(high)


def shard_levels(stream_key, shape, pieces, smallest, largest):
    gain = 1.0
    for dim, parts in pieces:
        draws = jax.random.uniform(jax.random.fold_in(jax.random.fold_in(stream_key, 6), dim), (parts,), jnp.float32, smallest / len(pieces), largest / len(pieces))
        gain = gain * jnp.repeat(jnp.exp(draws), shape[dim] // parts).reshape((-1,) + (1,) * (len(shape) - 1 - dim))
    return gain


def profile(count, total, most, slope):
    weights = [(1 << 20) // math.isqrt(grade ** slope) + 1 for grade in range(2, count + 1)]
    rest, holding = total - most - (count - 1), [1] * (count - 1)
    while rest > 0:
        free = [i for i in range(count - 1) if holding[i] < most]
        whole, left = sum([weights[i] for i in free]), rest
        for i in free:
            addition = min(most - holding[i], max(1, left * weights[i] // whole), rest)
            holding[i] = holding[i] + addition
            rest = rest - addition
    return np.array([most] + holding)


def uneven(key, amount, total, limit, slope):
    if amount == 2:
        one = jax.random.randint(key, (), max(1, total - limit), min(limit, total - 1) + 1)
        return jnp.stack([one, total - one])
    tallies = jnp.asarray(profile(amount, total, limit, slope), jnp.int32)
    twos = (amount - 1) // 2
    donor, taker = tallies[1:1 + 2 * twos:2], tallies[2:2 + 2 * twos:2]
    room = jnp.minimum(donor - 1, limit - taker)
    moved = jax.random.randint(jax.random.fold_in(key, 1), (twos,), 0, 1 << 20) % (room + 1)
    tallies = tallies.at[1:1 + 2 * twos:2].set(donor - moved).at[2:2 + 2 * twos:2].set(taker + moved)
    return tallies[jax.random.permutation(jax.random.fold_in(key, 2), amount)]


def routed_block(stream_key, own, number, rows, amount, top, limit, lean):
    sequence = jax.random.permutation(stream_key, amount)
    packed, usual = load_shares(amount, rows * top, limit, lean, True), load_shares(amount, rows * top, limit, lean, False)
    places = jnp.arange(amount)

    def named(tallies, turn):
        used = int((tallies > 0).sum())
        fixed = max(1, used // 4)
        shifted = fixed + (places - fixed + turn * (used - fixed)) % max(1, amount - fixed)
        return jnp.zeros((amount,), jnp.int32).at[sequence[jnp.where(places < fixed, places, shifted)]].set(jnp.asarray(tallies, jnp.int32))

    tallies = jnp.where(number % 4 == 0, named(packed, number // 4), named(usual, number - number // 4 - 1))
    mixed = jax.random.permutation(jax.random.fold_in(own, 3), amount)
    giver, taker = mixed[0:amount // 2 * 2:2], mixed[1:amount // 2 * 2:2]
    margin = jnp.minimum(tallies[giver] - 1, limit - tallies[taker]) // 2
    margin = jnp.where((giver == sequence[0]) | (taker == sequence[0]) | (tallies[taker] == 0), 0, jnp.maximum(margin, 0))
    shifted = jax.random.randint(jax.random.fold_in(own, 4), (amount // 2,), 0, 1 << 20) % (margin + 1)
    tallies = tallies.at[giver].add(-shifted).at[taker].add(shifted)
    items = jnp.searchsorted(jnp.cumsum(tallies), jnp.arange(rows * top), side="right").astype(jnp.int32)
    table = items.reshape(top, rows).T
    table = table[jax.random.permutation(jax.random.fold_in(own, 1), rows)]
    turn = jax.random.randint(jax.random.fold_in(own, 2), (rows, 1), 0, top)
    return jnp.take_along_axis(table, (jnp.arange(top)[None, :] + turn) % top, axis=1)


def load_shares(amount, total, most, skew, full):
    loads = [(1 << 20) // math.isqrt(grade ** skew) + 1 for grade in range(1, amount + 1)]
    largest = most if full else min(most, max(-(-total // amount), total * loads[0] // sum(loads)))
    least = 1 if total - largest >= amount - 1 else 0
    holding, spare = [largest] + [least] * (amount - 1), total - largest - least * (amount - 1)
    while spare > 0:
        candidates = [i for i in range(1, amount) if holding[i] < largest] or [i for i in range(1, amount) if holding[i] < most]
        pool, left = sum([loads[i] for i in candidates]), spare
        for i in candidates:
            addition = min(most - holding[i], max(1, left * loads[i] // pool), spare)
            holding[i] = holding[i] + addition
            spare = spare - addition
    return np.array(holding)


def noise(own_key, dims, spread, limit, cuts=(), held_as=jnp.bfloat16):
    gain = shard_levels(own_key, dims, cuts, -0.22, 0.18) if cuts else 1.0
    entries = jax.random.normal(own_key, dims, jnp.float32) * spread * gain
    return jnp.minimum(jnp.maximum(entries, -limit), limit).astype(held_as)


def setup_inputs(seed: int = 0, part: int = 0) -> dict:
    streams_of = jax.random.split(jax.random.key(seed), 8)
    part_keys = jax.random.split(jax.random.fold_in(streams_of[7], part), 8)
    amplitudes = noise(part_keys[0], (O, V, V), 1.0, 6.0, ((0, 16),))
    couplings = noise(part_keys[1], (N_VIR * CAP * BS, O, V * J), (O * V // 8) ** -0.5, 0.125, ((0, 16),))
    occ_irrep = place_ends(jax.random.randint(part_keys[2], (O,), 0, 8), jax.random.fold_in(part_keys[2], 1), 0, 7).astype(jnp.int32)
    pair_irrep = jax.random.randint(streams_of[3], (1,), 0, 8).astype(jnp.int32)
    j_irrep = jax.random.randint(streams_of[4], (J,), 0, 8).astype(jnp.int32)
    block_sizes = uneven(part_keys[5], 8, V, MOST, 1).astype(jnp.int32)
    owner_keys = jax.random.split(jax.random.fold_in(part_keys[6], 1), VB // VB)
    owner_turns = jax.random.permutation(jax.random.fold_in(part_keys[6], 3), VB // VB)
    owner = jax.vmap(lambda own, number: routed_block(jax.random.fold_in(part_keys[6], 2), own, number, VB, N_VIR, 1, CAP, 2))(owner_keys, owner_turns).reshape((VB, 1))
    return dict(amplitudes=amplitudes, couplings=couplings, occ_irrep=occ_irrep, pair_irrep=pair_irrep, j_irrep=j_irrep, block_sizes=block_sizes, owner=owner)


def orbital_labels(block_sizes):
    ends = jnp.cumsum(block_sizes).astype(jnp.int32)
    virtual = jnp.arange(V, dtype=jnp.int32)
    return jnp.sum((virtual[:, None] >= ends[None, :]).astype(jnp.int32), axis=1).astype(jnp.int32)


def slot_of_block(owners):
    blocks = jnp.arange(VB, dtype=jnp.int32)
    same_owner = owners[:, None] == owners[None, :]
    earlier = blocks[None, :] < blocks[:, None]
    ranking = jnp.sum((same_owner & earlier).astype(jnp.int32), axis=1).astype(jnp.int32)
    return (owners * CAP + ranking).astype(jnp.int32)


def reference(amplitudes, couplings, occ_irrep, pair_irrep, j_irrep, block_sizes, owner):
    labels = orbital_labels(block_sizes)
    slot_index = slot_of_block(owner[:, 0])
    virtual = jnp.arange(V, dtype=jnp.int32)
    row_of_e = (slot_index[virtual // BS] * BS + virtual % BS).astype(jnp.int32)
    wanted = jnp.bitwise_xor(pair_irrep[0], occ_irrep)
    t_allowed = jnp.bitwise_xor(labels[:, None], labels[None, :])[None] == wanted[:, None, None]
    masked_t = jnp.where(t_allowed, amplitudes, jnp.zeros((), amplitudes.dtype))
    w_rows = jnp.take(couplings, row_of_e, axis=0)
    column_irrep = jnp.bitwise_xor(labels[:, None], j_irrep[None, :]).reshape(V * J)
    w_allowed = jnp.bitwise_xor(labels[:, None], occ_irrep[None, :])[:, :, None] == column_irrep[None, None, :]
    masked_w = jnp.where(w_allowed, w_rows, jnp.zeros((), couplings.dtype))
    left_side = masked_t.reshape(O * V, V)
    right_side = jnp.transpose(masked_w, (1, 0, 2)).reshape(O * V, V * J)
    return jnp.dot(left_side.T, right_side, preferred_element_type=jnp.float32)
```

```python
import functools

import jax
import jax.numpy as jnp
from jax import lax
from jax.experimental import pallas as pl
from jax.experimental.pallas import tpu as pltpu
from jax.sharding import PartitionSpec as P

BS = 4
MOST = 256
LIMIT = 48 * 1024 * 1024
F32, BF16, I32 = jnp.float32, jnp.bfloat16, jnp.int32


def irrep_of(index, sizes):
    label = jnp.zeros_like(index)
    end = jnp.int32(0)
    for h in range(sizes.shape[0]):
        end = end + sizes[h]
        label = label + (index >= end).astype(I32)
    return label


def iota(shape, dim):
    return lax.broadcasted_iota(I32, shape, dim)


def column_keys(columns, sizes, j_irrep):
    count = j_irrep.shape[0]
    column = iota((1, columns), 1)
    j = column % count
    j_label = jnp.zeros_like(column)
    for i in range(count):
        j_label = jnp.where(j == i, j_irrep[i], j_label)
    return irrep_of(column // count, sizes) ^ j_label


def coupling_row(owner_row, virtuals, rows):
    blocks = owner_row.shape[1]
    first, second = iota((blocks, blocks), 0), iota((blocks, blocks), 1)
    owner_col = jnp.sum(jnp.where(first == second, owner_row, 0), axis=1, keepdims=True)
    earlier = (owner_col == owner_row) & (first < second)
    rank = jnp.sum(earlier.astype(I32), axis=0, keepdims=True)
    place = owner_row * rows + rank * BS
    e, block = iota((virtuals, blocks), 0), iota((virtuals, blocks), 1)
    start = jnp.sum(jnp.where(e // BS == block, place, 0), axis=1, keepdims=True)
    return start + iota((virtuals, 1), 0) % BS


def pack_kernel(
    rows, rows_out, sizes, occ, pair, owner_row, t_hbm, out, t_vmem, folded_t, target, sem
):
    virtuals = t_hbm.shape[1]
    lanes = 2 * rows

    @pl.when(pl.program_id(0) == 0)
    def _():
        copy = pltpu.make_async_copy(t_hbm.at[0], t_vmem, sem)
        copy.start()
        target[...] = jnp.broadcast_to(
            coupling_row(owner_row[...], virtuals, rows), target.shape
        )
        wanted = pair[0] ^ occ[lax.axis_index("vir")]
        label_e = irrep_of(iota((virtuals, 1), 0), sizes) ^ wanted
        label_a = irrep_of(iota((1, virtuals), 1), sizes)
        copy.wait()
        folded = jnp.zeros((virtuals, MOST), F32)
        for k in range(virtuals // MOST):
            part = slice(k * MOST, (k + 1) * MOST)
            folded = folded + jnp.where(
                label_e == label_a[:, part], t_vmem[:, part].astype(F32), 0.0
            )
        folded_t[...] = folded.T.astype(BF16)

    chips = out.shape[0] // 2
    for chip in range(chips):
        lane = iota((virtuals, lanes), 1)
        offset = (pl.program_id(0) * chips + chip) * lanes
        place = target[:, :1] - offset

        def moved(flip):
            hot = jnp.where(place == lane ^ flip, 1.0, 0.0).astype(BF16)
            return jnp.dot(folded_t[...], hot, preferred_element_type=F32)

        def half(values, core):
            return jnp.concatenate(
                [
                    values[start : start + rows_out]
                    for start in range(core * rows_out, MOST, 2 * rows_out)
                ],
                axis=0,
            )

        here = moved(0)
        out[2 * chip] = half(here, 0).astype(BF16)
        if rows % 128 == 0:
            there = half(here, 1)
            out[2 * chip + 1, :, :rows] = there[:, rows:].astype(BF16)
            out[2 * chip + 1, :, rows:] = there[:, :rows].astype(BF16)
        else:
            out[2 * chip + 1] = half(moved(rows), 1).astype(BF16)


def fold_kernel(
    rows, sizes, occ, pair, j_irrep, owner, owner_row, w, out, label_k, blocks, keys, folded
):
    here = lax.axis_index("vir")
    step, part = pl.program_id(0), pl.program_id(1)
    row_block, m_block, columns = w.shape
    wide = out.shape[2]

    @pl.when((step == 0) & (part == 0))
    def _():
        keys[...] = jnp.broadcast_to(column_keys(columns, sizes, j_irrep), keys.shape)

        def clear(s, _):
            blocks[s] = 0
            return 0

        lax.fori_loop(0, blocks.shape[0], clear, 0)

        def visit(k, seen):
            mine = owner[k] == here

            @pl.when(mine)
            def _():
                blocks[seen] = k

            return seen + mine.astype(I32)

        lax.fori_loop(0, owner.shape[0], visit, jnp.int32(0))
        virtuals = owner.shape[0] * BS
        lanes = label_k.shape[1]
        target = coupling_row(owner_row[...], virtuals, rows)
        lane = iota((virtuals, lanes), 1)
        own = here * rows
        mate = (here ^ 1) * rows
        source = jnp.where(lane < rows, lane + own, lane - rows + mate)
        label_e = irrep_of(iota((virtuals, 1), 0), sizes)
        label = jnp.sum(jnp.where(target == source, label_e, 0), axis=0, keepdims=True)
        label_k[...] = jnp.broadcast_to(label, label_k.shape)

    m_row = iota((m_block, 1), 0)
    occ_col = jnp.zeros((m_block, 1), I32)
    for i in range(m_block):
        occ_col = jnp.where(m_row == i, occ[part * m_block + i], occ_col)
    for i in range(row_block):
        row = step * row_block + i
        label = irrep_of(blocks[row // BS] * BS + row % BS, sizes)
        allowed = (occ_col ^ label) == keys[:1, :]
        kept = jnp.where(allowed, w[i].astype(F32), 0.0)
        total = kept[:, :wide]
        for k in range(1, columns // wide):
            total = total + kept[:, k * wide : (k + 1) * wide]
        for k in range(wide // 128):
            folded[k, i * m_block : (i + 1) * m_block, :] = total[:, k * 128 : (k + 1) * 128]
    for i in range(m_block):
        for k in range(wide // 128):
            out[i, :, k * 128 : (k + 1) * 128] = folded[
                k, pl.ds(i, row_block, stride=m_block), :
            ].astype(BF16)


def product_kernel(rows_out, sizes, occ, pair, label_k, t, w_own, w_mate, out):
    step = pl.program_id(0)
    m_block, half, lanes = t.shape
    virtuals = out.shape[0] * 2
    kept_row = iota((out.shape[0], 1), 0)
    core = lax.axis_index("vir") % 2
    a = kept_row // rows_out * (2 * rows_out) + core * rows_out + kept_row % rows_out
    label_a = irrep_of(a, sizes)
    left, right = [], []
    for i in range(m_block):
        wanted = label_k[:1, :] ^ (pair[0] ^ occ[step * m_block + i])
        values = t[i].astype(F32)
        left.append(
            jnp.concatenate(
                [
                    jnp.where(label_a[k : k + half] == wanted, values, 0.0).astype(BF16)
                    for k in range(0, virtuals // 2, half)
                ],
                axis=0,
            )
        )
        right += [w_own[i], w_mate[i]]
    if lanes % 128 == 0:
        total = jnp.dot(
            jnp.concatenate(left, axis=1),
            jnp.concatenate(right, axis=0),
            preferred_element_type=F32,
        )
    else:
        total = jnp.zeros(out.shape, F32)
        for i in range(m_block):
            total = total + jnp.dot(
                left[i],
                jnp.concatenate(right[2 * i : 2 * i + 2], axis=0),
                preferred_element_type=F32,
            )

    @pl.when(step == 0)
    def _():
        out[...] = total

    @pl.when(step > 0)
    def _():
        out[...] += total


def finish_kernel(sizes, pair, j_irrep, parts, out):
    chips, rows_out, wide = parts.shape
    total = parts[0]
    for q in range(1, chips):
        total = total + parts[q]
    columns = out.shape[1]
    a = iota((rows_out, 1), 0) + lax.axis_index("vir") * rows_out
    label_a = irrep_of(a, sizes) ^ pair[0]
    keys = column_keys(columns, sizes, j_irrep)
    for k in range(0, columns, wide):
        out[:, k : k + wide] = jnp.where(label_a == keys[:, k : k + wide], total, 0.0)


def per_device(amplitudes, couplings, occ_irrep, pair_irrep, j_irrep, block_sizes, owner):
    devices = lax.axis_size("vir")
    chips = devices // 2
    virtuals = amplitudes.shape[2]
    rows, occupied, columns = couplings.shape
    wide = columns // virtuals * MOST
    rows_out = virtuals // devices
    lanes = 2 * rows
    blocks = owner.shape[0]
    owner_row = owner.reshape(1, blocks)
    owner_flat = owner.reshape(blocks)
    smem = pl.BlockSpec(memory_space=pltpu.SMEM)
    vmem = pl.BlockSpec(memory_space=pltpu.VMEM)
    params = pltpu.CompilerParams(vmem_limit_bytes=LIMIT)

    chips_step = max(1, 256 // lanes)
    outgoing = pl.pallas_call(
        functools.partial(pack_kernel, rows, rows_out),
        out_shape=jax.ShapeDtypeStruct((devices, MOST // 2, lanes), BF16),
        grid=(chips // chips_step,),
        in_specs=[smem, smem, smem, vmem, pl.BlockSpec(memory_space=pl.ANY)],
        out_specs=pl.BlockSpec((2 * chips_step, MOST // 2, lanes), lambda i: (i, 0, 0)),
        scratch_shapes=[
            pltpu.VMEM((virtuals, virtuals), BF16),
            pltpu.VMEM((MOST, virtuals), BF16),
            pltpu.VMEM((virtuals, 128), I32),
            pltpu.SemaphoreType.DMA,
        ],
        compiler_params=params,
        name="pack_amplitudes",
    )(block_sizes, occ_irrep, pair_irrep, owner_row, amplitudes)
    received = lax.all_to_all(outgoing, "vir", 0, 0)

    row_block, m_block = 16, 16
    w_own, label_k = pl.pallas_call(
        functools.partial(fold_kernel, rows),
        out_shape=(
            jax.ShapeDtypeStruct((occupied, rows, wide), BF16),
            jax.ShapeDtypeStruct((8, lanes), I32),
        ),
        grid=(rows // row_block, occupied // m_block),
        in_specs=[smem, smem, smem, smem, smem, vmem]
        + [pl.BlockSpec((row_block, m_block, columns), lambda i, j: (i, j, 0))],
        out_specs=(
            pl.BlockSpec((m_block, row_block, wide), lambda i, j: (j, i, 0)),
            pl.BlockSpec((8, lanes), lambda i, j: (0, 0)),
        ),
        scratch_shapes=[
            pltpu.SMEM((rows // BS,), I32),
            pltpu.VMEM((8, columns), I32),
            pltpu.VMEM((wide // 128, row_block * m_block, 128), F32),
        ],
        compiler_params=params,
        cost_estimate=pl.CostEstimate(
            flops=4 * rows * occupied * columns,
            bytes_accessed=3 * rows * occupied * columns,
            transcendentals=0,
        ),
        name="fold_couplings",
    )(block_sizes, occ_irrep, pair_irrep, j_irrep, owner_flat, owner_row, couplings)
    w_mate = lax.ppermute(w_own, "vir", [(d, d ^ 1) for d in range(devices)])

    m_step = 4
    kept = virtuals // 2
    partial = pl.pallas_call(
        functools.partial(product_kernel, rows_out),
        out_shape=jax.ShapeDtypeStruct((kept, wide), F32),
        grid=(occupied // m_step,),
        in_specs=[smem, smem, smem, vmem]
        + [pl.BlockSpec((m_step, MOST // 2, lanes), lambda i: (i, 0, 0))]
        + [pl.BlockSpec((m_step, rows, wide), lambda i: (i, 0, 0))] * 2,
        out_specs=pl.BlockSpec((kept, wide), lambda i: (0, 0)),
        compiler_params=params,
        name="multiply",
    )(block_sizes, occ_irrep, pair_irrep, label_k, received, w_own, w_mate)
    sides = [[d for d in range(devices) if d % 2 == core] for core in (0, 1)]
    parts = lax.all_to_all(
        partial.reshape(chips, rows_out, wide), "vir", 0, 0, axis_index_groups=sides
    )
    return pl.pallas_call(
        finish_kernel,
        out_shape=jax.ShapeDtypeStruct((rows_out, columns), F32),
        in_specs=[smem, smem, smem, vmem],
        out_specs=vmem,
        compiler_params=params,
        name="unfold",
    )(block_sizes, pair_irrep, j_irrep, parts)


def solution(mesh):
    return jax.shard_map(
        per_device,
        mesh=mesh,
        in_specs=(
            P(("grp", "vir"), None, None),
            P(("grp", "vir"), None, None),
            P("grp"),
            P(),
            P(),
            P("grp"),
            P("grp", None),
        ),
        out_specs=P(("grp", "vir"), None),
        check_vma=False,
    )
```

```python
import functools

import jax
import jax.numpy as jnp
from jax import lax
from jax.experimental import pallas as pl
from jax.experimental.pallas import tpu as pltpu
from jax.sharding import PartitionSpec as P

BS = 4
MOST = 256
LIMIT = 24 * 1024 * 1024
MOST_LIMIT = 60 * 1024 * 1024
F32, BF16, I32 = jnp.float32, jnp.bfloat16, jnp.int32


def irrep_of(index, sizes):
    label = jnp.zeros_like(index)
    end = jnp.int32(0)
    for h in range(sizes.shape[0]):
        end = end + sizes[h]
        label = label + (index >= end).astype(I32)
    return label


def iota(shape, dim):
    return lax.broadcasted_iota(I32, shape, dim)


def column_keys(columns, sizes, j_irrep):
    count = j_irrep.shape[0]
    column = iota((1, columns), 1)
    j = column % count
    j_label = jnp.zeros_like(column)
    for i in range(count):
        j_label = jnp.where(j == i, j_irrep[i], j_label)
    return irrep_of(column // count, sizes) ^ j_label


def block_place(owner_row, rows):
    blocks = owner_row.shape[1]
    first, second = iota((blocks, blocks), 0), iota((blocks, blocks), 1)
    owner_col = jnp.sum(jnp.where(first == second, owner_row, 0), axis=1, keepdims=True)
    earlier = (owner_col == owner_row) & (first < second)
    rank = jnp.sum(earlier.astype(I32), axis=0, keepdims=True)
    return owner_row * rows + rank * BS


def virtual_place(place, virtuals):
    blocks = place.shape[1]
    e, block = iota((virtuals, blocks), 0), iota((virtuals, blocks), 1)
    start = jnp.sum(jnp.where(e // BS == block, place, 0), axis=1, keepdims=True)
    return start + iota((virtuals, 1), 0) % BS


def pack_kernel(
    rows,
    rows_out,
    sizes_hbm,
    occ_hbm,
    pair_hbm,
    owner_hbm,
    t_hbm,
    out,
    place,
    sizes,
    occ,
    pair,
    owner_row,
    t_vmem,
    folded_t,
    target,
    sems,
):
    virtuals = t_hbm.shape[1]
    lanes = 2 * rows

    @pl.when(pl.program_id(0) == 0)
    def _():
        pairs = (
            (owner_hbm, owner_row),
            (sizes_hbm, sizes),
            (occ_hbm, occ),
            (pair_hbm, pair),
            (t_hbm.at[0], t_vmem),
        )
        copies = [
            pltpu.make_async_copy(source, here, sems.at[i])
            for i, (source, here) in enumerate(pairs)
        ]
        for copy in copies:
            copy.start()
        copies[0].wait()
        where = block_place(owner_row[...], rows)
        place[...] = jnp.broadcast_to(where, place.shape)
        target[...] = jnp.broadcast_to(virtual_place(where, virtuals), target.shape)
        for copy in copies[1:4]:
            copy.wait()
        wanted = pair[0] ^ occ[lax.axis_index("vir")]
        label_e = irrep_of(iota((virtuals, 1), 0), sizes) ^ wanted
        label_a = irrep_of(iota((1, virtuals), 1), sizes)
        copies[4].wait()
        folded = jnp.zeros((virtuals, MOST), F32)
        for k in range(virtuals // MOST):
            part = slice(k * MOST, (k + 1) * MOST)
            folded = folded + jnp.where(
                label_e == label_a[:, part], t_vmem[:, part].astype(F32), 0.0
            )
        folded_t[...] = folded.T.astype(BF16)

    chips = out.shape[0] // 2
    for chip in range(chips):
        lane = iota((virtuals, lanes), 1)
        offset = (pl.program_id(0) * chips + chip) * lanes
        place = target[:, :1] - offset

        def moved(flip):
            hot = jnp.where(place == lane ^ flip, 1.0, 0.0).astype(BF16)
            return jnp.dot(folded_t[...], hot, preferred_element_type=F32)

        def half(values, core):
            return jnp.concatenate(
                [
                    values[start : start + rows_out]
                    for start in range(core * rows_out, MOST, 2 * rows_out)
                ],
                axis=0,
            )

        here = moved(0)
        out[2 * chip] = half(here, 0).astype(BF16)
        if rows % 128 == 0:
            there = half(here, 1)
            out[2 * chip + 1, :, :rows] = there[:, rows:].astype(BF16)
            out[2 * chip + 1, :, rows:] = there[:, :rows].astype(BF16)
        else:
            out[2 * chip + 1] = half(moved(rows), 1).astype(BF16)


def label_kernel(
    rows,
    rows_out,
    sizes,
    occ,
    pair,
    j_irrep,
    place,
    label_row,
    label_k,
    label_kept,
    label_out,
    keys,
):
    here = lax.axis_index("vir")
    occupied, lanes = label_k.shape
    virtuals = place.shape[1] * BS
    target = virtual_place(place[:1, :], virtuals)
    lane = iota((virtuals, lanes), 1)
    source = jnp.where(lane < rows, lane + here * rows, lane - rows + (here ^ 1) * rows)
    label_e = irrep_of(iota((virtuals, 1), 0), sizes)
    label = jnp.sum(jnp.where(target == source, label_e, 0), axis=0, keepdims=True)
    label_row[...] = label[:, :rows]
    for m in range(occupied):
        label_k[m : m + 1, :] = label ^ (pair[0] ^ occ[m])
    row = iota(label_kept.shape, 0)
    a = row // rows_out * (2 * rows_out) + here % 2 * rows_out + row % rows_out
    label_kept[...] = irrep_of(a, sizes)
    label_out[...] = irrep_of(iota(label_out.shape, 0) + here * rows_out, sizes) ^ pair[0]
    keys[...] = jnp.broadcast_to(column_keys(keys.shape[1], sizes, j_irrep), keys.shape)


def fold_kernel(first, occ, label_row, keys, w, out, folded):
    step, part = pl.program_id(0), pl.program_id(1)
    row_block, m_block, columns = w.shape
    wide = out.shape[2]
    m_row = iota((m_block, 1), 0)
    occ_col = jnp.zeros((m_block, 1), I32)
    for i in range(m_block):
        occ_col = jnp.where(m_row == i, occ[part * m_block + i], occ_col)
    for i in range(row_block):
        label = label_row[first + step * row_block + i]
        allowed = (occ_col ^ label) == keys[:1, :]
        kept = jnp.where(allowed, w[i].astype(F32), 0.0)
        total = kept[:, :wide]
        for k in range(1, columns // wide):
            total = total + kept[:, k * wide : (k + 1) * wide]
        for k in range(wide // 128):
            folded[k, i * m_block : (i + 1) * m_block, :] = total[:, k * 128 : (k + 1) * 128]
    for i in range(m_block):
        for k in range(wide // 128):
            out[i, :, k * 128 : (k + 1) * 128] = folded[
                k, pl.ds(i, row_block, stride=m_block), :
            ].astype(BF16)


def product_kernel(label_k_hbm, label_kept_hbm, t_hbm, *refs):
    *pieces, out, label_k, label_kept, t, w, sems = refs
    occupied, half, lanes = t.shape
    kept = out.shape[0]
    size = pieces[0].shape[1]
    m_block = max(1, min(occupied, 1024 // lanes))
    steps = occupied // m_block

    def fetches(step):
        part = pl.ds(step * m_block, m_block)
        pairs = [(t_hbm.at[part], t.at[part])] + [
            (piece.at[part], w.at[part, pl.ds(i * size, size)])
            for i, piece in enumerate(pieces)
        ]
        return [
            pltpu.make_async_copy(source, here, sems.at[2 + step * len(pairs) + i])
            for i, (source, here) in enumerate(pairs)
        ]

    tables = [
        pltpu.make_async_copy(label_k_hbm, label_k, sems.at[0]),
        pltpu.make_async_copy(label_kept_hbm, label_kept, sems.at[1]),
    ]
    for copy in tables:
        copy.start()
    for step in range(steps):
        for copy in fetches(step):
            copy.start()
    out[...] = jnp.zeros(out.shape, F32)
    for copy in tables:
        copy.wait()
    wide_label = jnp.broadcast_to(label_kept[:, :1], (kept, lanes))

    @pl.loop(0, steps)
    def _(step):
        for copy in fetches(step):
            copy.wait()
        left, right = [], []
        for i in range(m_block):
            m = step * m_block + i
            wanted = label_k[pl.ds(m, 1), :]
            values = t[m].astype(F32)
            left.append(
                jnp.concatenate(
                    [
                        jnp.where(wide_label[k : k + half] == wanted, values, 0.0).astype(BF16)
                        for k in range(0, kept, half)
                    ],
                    axis=0,
                )
            )
            right.append(w[m])
        if lanes % 128 == 0:
            left = [jnp.concatenate(left, axis=1)]
            right = [jnp.concatenate(right, axis=0)]
        total = jnp.dot(left[0], right[0], preferred_element_type=F32)
        for x, y in zip(left[1:], right[1:]):
            total = total + jnp.dot(x, y, preferred_element_type=F32)
        out[...] += total


def finish_kernel(label_out, keys, parts, out):
    chips, rows_out, wide = parts.shape
    total = parts[0]
    for q in range(1, chips):
        total = total + parts[q]
    for k in range(0, out.shape[1], wide):
        out[:, k : k + wide] = jnp.where(
            label_out[:, :1] == keys[:1, k : k + wide], total, 0.0
        )


def per_device(amplitudes, couplings, occ_irrep, pair_irrep, j_irrep, block_sizes, owner):
    devices = lax.axis_size("vir")
    chips = devices // 2
    virtuals = amplitudes.shape[2]
    rows, occupied, columns = couplings.shape
    wide = columns // virtuals * MOST
    rows_out = virtuals // devices
    kept = virtuals // 2
    lanes = 2 * rows
    blocks = owner.shape[0]
    smem = pl.BlockSpec(memory_space=pltpu.SMEM)
    vmem = pl.BlockSpec(memory_space=pltpu.VMEM)
    hbm = pl.BlockSpec(memory_space=pltpu.HBM)
    params = pltpu.CompilerParams(vmem_limit_bytes=LIMIT)
    alone = pltpu.CompilerParams(vmem_limit_bytes=MOST_LIMIT)

    chips_step = max(1, 256 // lanes)
    outgoing, place = pl.pallas_call(
        functools.partial(pack_kernel, rows, rows_out),
        out_shape=(
            jax.ShapeDtypeStruct((devices, MOST // 2, lanes), BF16),
            jax.ShapeDtypeStruct((8, blocks), I32),
        ),
        grid=(chips // chips_step,),
        in_specs=[hbm] * 5,
        out_specs=(
            pl.BlockSpec((2 * chips_step, MOST // 2, lanes), lambda i: (i, 0, 0)),
            pl.BlockSpec((8, blocks), lambda i: (0, 0)),
        ),
        scratch_shapes=[
            pltpu.SMEM(block_sizes.shape, I32),
            pltpu.SMEM(occ_irrep.shape, I32),
            pltpu.SMEM(pair_irrep.shape, I32),
            pltpu.VMEM((1, blocks), I32),
            pltpu.VMEM((virtuals, virtuals), BF16),
            pltpu.VMEM((MOST, virtuals), BF16),
            pltpu.VMEM((virtuals, 128), I32),
            pltpu.SemaphoreType.DMA((5,)),
        ],
        compiler_params=alone,
        name="pack_amplitudes",
    )(block_sizes, occ_irrep, pair_irrep, owner.reshape(1, blocks), amplitudes)
    received = lax.all_to_all(outgoing, "vir", 0, 0)

    label_row, label_k, label_kept, label_out, keys = pl.pallas_call(
        functools.partial(label_kernel, rows, rows_out),
        out_shape=(
            jax.ShapeDtypeStruct((1, rows), I32),
            jax.ShapeDtypeStruct((occupied, lanes), I32),
            jax.ShapeDtypeStruct((kept, 128), I32),
            jax.ShapeDtypeStruct((rows_out, 128), I32),
            jax.ShapeDtypeStruct((8, columns), I32),
        ),
        in_specs=[smem] * 4 + [vmem],
        out_specs=(vmem,) * 5,
        compiler_params=params,
        name="labels",
    )(block_sizes, occ_irrep, pair_irrep, j_irrep, place)

    row_block, m_block = 16, 16
    pieces = max(1, rows // 32)
    piece_rows = rows // pieces
    w_own, w_mate = [], []
    for piece in range(pieces):
        first = piece * piece_rows
        w_own.append(
            pl.pallas_call(
                functools.partial(fold_kernel, first),
                out_shape=jax.ShapeDtypeStruct((occupied, piece_rows, wide), BF16),
                grid=(piece_rows // row_block, occupied // m_block),
                in_specs=[smem, smem, vmem]
                + [
                    pl.BlockSpec(
                        (row_block, m_block, columns),
                        lambda i, j, skip=first // row_block: (skip + i, j, 0),
                    )
                ],
                out_specs=pl.BlockSpec((m_block, row_block, wide), lambda i, j: (j, i, 0)),
                scratch_shapes=[pltpu.VMEM((wide // 128, row_block * m_block, 128), F32)],
                compiler_params=params,
                cost_estimate=pl.CostEstimate(
                    flops=4 * piece_rows * occupied * columns,
                    bytes_accessed=3 * piece_rows * occupied * columns,
                    transcendentals=0,
                ),
                name="fold_couplings",
            )(occ_irrep, label_row.reshape(rows), keys, couplings)
        )
        w_mate.append(lax.ppermute(w_own[-1], "vir", [(d, d ^ 1) for d in range(devices)]))

    partial = pl.pallas_call(
        product_kernel,
        out_shape=jax.ShapeDtypeStruct((kept, wide), F32),
        in_specs=[hbm] * (3 + 2 * pieces),
        out_specs=vmem,
        scratch_shapes=[
            pltpu.VMEM((occupied, lanes), I32),
            pltpu.VMEM((kept, 128), I32),
            pltpu.VMEM(received.shape, BF16),
            pltpu.VMEM((occupied, lanes, wide), BF16),
            pltpu.SemaphoreType.DMA((2 + occupied * (1 + 2 * pieces),)),
        ],
        compiler_params=alone,
        name="multiply",
    )(label_k, label_kept, received, *w_own, *w_mate)
    sides = [[d for d in range(devices) if d % 2 == core] for core in (0, 1)]
    parts = lax.all_to_all(
        partial.reshape(chips, rows_out, wide), "vir", 0, 0, axis_index_groups=sides
    )
    return pl.pallas_call(
        finish_kernel,
        out_shape=jax.ShapeDtypeStruct((rows_out, columns), F32),
        in_specs=[vmem] * 3,
        out_specs=vmem,
        compiler_params=params,
        name="unfold",
    )(label_out, keys, parts)


def solution(mesh):
    return jax.shard_map(
        per_device,
        mesh=mesh,
        in_specs=(
            P(("grp", "vir"), None, None),
            P(("grp", "vir"), None, None),
            P("grp"),
            P(),
            P(),
            P("grp"),
            P("grp", None),
        ),
        out_specs=P(("grp", "vir"), None),
        check_vma=False,
    )
```

```python
import functools

import jax
import jax.numpy as jnp
from jax import lax
from jax.experimental import pallas as pl
from jax.experimental.pallas import tpu as pltpu
from jax.sharding import PartitionSpec as P

BS = 4
MOST = 256
LIMIT = 24 * 1024 * 1024
F32, BF16, I32 = jnp.float32, jnp.bfloat16, jnp.int32


def irrep_of(index, sizes):
    label = jnp.zeros_like(index)
    end = jnp.int32(0)
    for h in range(sizes.shape[0]):
        end = end + sizes[h]
        label = label + (index >= end).astype(I32)
    return label


def iota(shape, dim):
    return lax.broadcasted_iota(I32, shape, dim)


def column_keys(columns, sizes, j_irrep):
    count = j_irrep.shape[0]
    column = iota((1, columns), 1)
    j = column % count
    j_label = jnp.zeros_like(column)
    for i in range(count):
        j_label = jnp.where(j == i, j_irrep[i], j_label)
    return irrep_of(column // count, sizes) ^ j_label


def block_place(owner_row, rows):
    blocks = owner_row.shape[1]
    first, second = iota((blocks, blocks), 0), iota((blocks, blocks), 1)
    owner_col = jnp.sum(jnp.where(first == second, owner_row, 0), axis=1, keepdims=True)
    earlier = (owner_col == owner_row) & (first < second)
    rank = jnp.sum(earlier.astype(I32), axis=0, keepdims=True)
    return owner_row * rows + rank * BS


def virtual_place(place, virtuals):
    blocks = place.shape[1]
    e, block = iota((virtuals, blocks), 0), iota((virtuals, blocks), 1)
    start = jnp.sum(jnp.where(e // BS == block, place, 0), axis=1, keepdims=True)
    return start + iota((virtuals, 1), 0) % BS


def pack_kernel(
    rows,
    rows_out,
    sizes_hbm,
    occ_hbm,
    pair,
    owner_hbm,
    t_hbm,
    out_hbm,
    place,
    sizes,
    occ,
    owner_row,
    t_vmem,
    out,
    in_sems,
    out_sems,
):
    virtuals = t_hbm.shape[1]
    lanes = 2 * rows
    pairs = (
        (owner_hbm, owner_row),
        (sizes_hbm, sizes),
        (occ_hbm, occ),
        (t_hbm.at[0], t_vmem),
    )
    copies = [
        pltpu.make_async_copy(source, here, in_sems.at[i])
        for i, (source, here) in enumerate(pairs)
    ]
    for copy in copies:
        copy.start()
    copies[0].wait()
    where = block_place(owner_row[...], rows)
    place[...] = jnp.broadcast_to(where, place.shape)
    target = jnp.broadcast_to(virtual_place(where, virtuals), (virtuals, lanes))
    for copy in copies[1:3]:
        copy.wait()
    wanted = pair[0] ^ occ[lax.axis_index("vir")]
    label_e = irrep_of(iota((virtuals, 1), 0), sizes) ^ wanted
    label_a = irrep_of(iota((1, virtuals), 1), sizes)
    copies[3].wait()
    folded = jnp.zeros((virtuals, MOST), F32)
    for k in range(virtuals // MOST):
        part = slice(k * MOST, (k + 1) * MOST)
        folded = folded + jnp.where(
            label_e == label_a[:, part], t_vmem[:, part].astype(F32), 0.0
        )
    folded_t = folded.T.astype(BF16)
    lane = iota((1, lanes), 1)

    def half(values, core):
        return jnp.concatenate(
            [
                values[start : start + rows_out]
                for start in range(core * rows_out, MOST, 2 * rows_out)
            ],
            axis=0,
        )

    sends = []
    for chip in range(out.shape[0] // 2):

        def moved(flip):
            hot = jnp.where(target == (lane ^ flip) + chip * lanes, 1.0, 0.0).astype(BF16)
            return jnp.dot(folded_t, hot, preferred_element_type=F32)

        here = moved(0)
        out[2 * chip] = half(here, 0).astype(BF16)
        if rows % 128 == 0:
            there = half(here, 1)
            out[2 * chip + 1, :, :rows] = there[:, rows:].astype(BF16)
            out[2 * chip + 1, :, rows:] = there[:, :rows].astype(BF16)
        else:
            out[2 * chip + 1] = half(moved(rows), 1).astype(BF16)
        both = pl.ds(2 * chip, 2)
        sends.append(pltpu.make_async_copy(out.at[both], out_hbm.at[both], out_sems.at[chip]))
        sends[-1].start()
    for copy in sends:
        copy.wait()


def label_kernel(
    rows,
    rows_out,
    sizes,
    occ,
    pair,
    j_irrep,
    place,
    label_row,
    label_k,
    label_kept,
    label_out,
    keys,
):
    here = lax.axis_index("vir")
    occupied, lanes = label_k.shape
    virtuals = place.shape[1] * BS
    target = virtual_place(place[:1, :], virtuals)
    lane = iota((virtuals, lanes), 1)
    source = jnp.where(lane < rows, lane + here * rows, lane - rows + (here ^ 1) * rows)
    label_e = irrep_of(iota((virtuals, 1), 0), sizes)
    label = jnp.sum(jnp.where(target == source, label_e, 0), axis=0, keepdims=True)
    label_row[...] = label[:, :rows]
    for m in range(occupied):
        label_k[m : m + 1, :] = label ^ (pair[0] ^ occ[m])
    row = iota(label_kept.shape, 0)
    a = row // rows_out * (2 * rows_out) + here % 2 * rows_out + row % rows_out
    label_kept[...] = irrep_of(a, sizes)
    label_out[...] = irrep_of(iota(label_out.shape, 0) + here * rows_out, sizes) ^ pair[0]
    keys[...] = jnp.broadcast_to(column_keys(keys.shape[1], sizes, j_irrep), keys.shape)


def fold_kernel(first, occ, label_row, keys, w, out, folded):
    step, part = pl.program_id(0), pl.program_id(1)
    row_block, m_block, columns = w.shape
    wide = out.shape[2]
    m_row = iota((m_block, 1), 0)
    occ_col = jnp.zeros((m_block, 1), I32)
    for i in range(m_block):
        occ_col = jnp.where(m_row == i, occ[part * m_block + i], occ_col)
    for i in range(row_block):
        label = label_row[first + step * row_block + i]
        allowed = (occ_col ^ label) == keys[:1, :]
        kept = jnp.where(allowed, w[i].astype(F32), 0.0)
        total = kept[:, :wide]
        for k in range(1, columns // wide):
            total = total + kept[:, k * wide : (k + 1) * wide]
        for k in range(wide // 128):
            folded[k, i * m_block : (i + 1) * m_block, :] = total[:, k * 128 : (k + 1) * 128]
    for i in range(m_block):
        for k in range(wide // 128):
            out[i, :, k * 128 : (k + 1) * 128] = folded[
                k, pl.ds(i, row_block, stride=m_block), :
            ].astype(BF16)


def product_kernel(pieces, label_k, label_kept, t, *refs):
    own, mate_hbm, (out, mate, sems) = refs[:pieces], refs[pieces : 2 * pieces], refs[2 * pieces :]
    occupied, half, lanes = t.shape
    rows = lanes // 2
    kept = out.shape[0]
    size = rows // pieces
    copies = [
        pltpu.make_async_copy(mate_hbm[i], mate.at[:, i * size : (i + 1) * size], sems.at[i])
        for i in range(pieces)
    ]
    for copy in copies:
        copy.start()
    wide_label = jnp.broadcast_to(label_kept[:, :1], (kept, rows))
    out[...] = jnp.zeros(out.shape, F32)
    m_block = max(1, min(occupied, 1024 // rows))

    def accumulate(side, couplings):
        lane = slice(side * rows, (side + 1) * rows)

        @pl.loop(0, occupied // m_block)
        def _(step):
            left, right = [], []
            for i in range(m_block):
                m = step * m_block + i
                wanted = label_k[pl.ds(m, 1), :][:, lane]
                values = t[m][:, lane].astype(F32)
                left.append(
                    jnp.concatenate(
                        [
                            jnp.where(wide_label[k : k + half] == wanted, values, 0.0).astype(BF16)
                            for k in range(0, kept, half)
                        ],
                        axis=0,
                    )
                )
                right.append(couplings(m))
            if rows % 128 == 0:
                left = [jnp.concatenate(left, axis=1)]
                right = [jnp.concatenate(right, axis=0)]
            total = jnp.dot(left[0], right[0], preferred_element_type=F32)
            for x, y in zip(left[1:], right[1:]):
                total = total + jnp.dot(x, y, preferred_element_type=F32)
            out[...] += total

    accumulate(0, lambda m: jnp.concatenate([piece[m] for piece in own], axis=0))
    for copy in copies:
        copy.wait()
    accumulate(1, lambda m: mate[m])


def finish_kernel(label_out, keys, parts, out):
    chips, rows_out, wide = parts.shape
    total = parts[0]
    for q in range(1, chips):
        total = total + parts[q]
    for k in range(0, out.shape[1], wide):
        out[:, k : k + wide] = jnp.where(
            label_out[:, :1] == keys[:1, k : k + wide], total, 0.0
        )


in_hbm = functools.partial(pltpu.with_memory_space_constraint, memory_space=pltpu.HBM)
in_vmem = functools.partial(pltpu.with_memory_space_constraint, memory_space=pltpu.VMEM)


def per_device(amplitudes, couplings, occ_irrep, pair_irrep, j_irrep, block_sizes, owner):
    devices = lax.axis_size("vir")
    chips = devices // 2
    virtuals = amplitudes.shape[2]
    rows, occupied, columns = couplings.shape
    wide = columns // virtuals * MOST
    rows_out = virtuals // devices
    kept = virtuals // 2
    lanes = 2 * rows
    blocks = owner.shape[0]
    smem = pl.BlockSpec(memory_space=pltpu.SMEM)
    vmem = pl.BlockSpec(memory_space=pltpu.VMEM)
    hbm = pl.BlockSpec(memory_space=pltpu.HBM)
    params = pltpu.CompilerParams(vmem_limit_bytes=LIMIT)

    outgoing, place = pl.pallas_call(
        functools.partial(pack_kernel, rows, rows_out),
        out_shape=(
            pltpu.HBM((devices, MOST // 2, lanes), BF16),
            jax.ShapeDtypeStruct((8, blocks), I32),
        ),
        in_specs=[hbm, hbm, smem, hbm, hbm],
        out_specs=(hbm, vmem),
        scratch_shapes=[
            pltpu.SMEM(block_sizes.shape, I32),
            pltpu.SMEM(occ_irrep.shape, I32),
            pltpu.VMEM((1, blocks), I32),
            pltpu.VMEM((virtuals, virtuals), BF16),
            pltpu.VMEM((devices, MOST // 2, lanes), BF16),
            pltpu.SemaphoreType.DMA((4,)),
            pltpu.SemaphoreType.DMA((chips,)),
        ],
        compiler_params=params,
        name="pack_amplitudes",
    )(
        in_hbm(block_sizes),
        in_hbm(occ_irrep),
        pair_irrep,
        in_hbm(owner.reshape(1, blocks)),
        in_hbm(amplitudes),
    )
    received = lax.all_to_all(outgoing, "vir", 0, 0)

    label_row, label_k, label_kept, label_out, keys = pl.pallas_call(
        functools.partial(label_kernel, rows, rows_out),
        out_shape=(
            jax.ShapeDtypeStruct((1, rows), I32),
            jax.ShapeDtypeStruct((occupied, lanes), I32),
            jax.ShapeDtypeStruct((kept, 128), I32),
            jax.ShapeDtypeStruct((rows_out, 128), I32),
            jax.ShapeDtypeStruct((8, columns), I32),
        ),
        in_specs=[smem] * 4 + [vmem],
        out_specs=(vmem,) * 5,
        compiler_params=params,
        name="labels",
    )(block_sizes, occ_irrep, pair_irrep, j_irrep, place)

    row_block, m_block = 16, 16
    pieces = max(1, rows // 32)
    piece_rows = rows // pieces
    w_own, w_mate = [], []
    for piece in range(pieces):
        first = piece * piece_rows
        w_own.append(
            pl.pallas_call(
                functools.partial(fold_kernel, first),
                out_shape=jax.ShapeDtypeStruct((occupied, piece_rows, wide), BF16),
                grid=(piece_rows // row_block, occupied // m_block),
                in_specs=[smem, smem, vmem]
                + [
                    pl.BlockSpec(
                        (row_block, m_block, columns),
                        lambda i, j, skip=first // row_block: (skip + i, j, 0),
                    )
                ],
                out_specs=pl.BlockSpec((m_block, row_block, wide), lambda i, j: (j, i, 0)),
                scratch_shapes=[pltpu.VMEM((wide // 128, row_block * m_block, 128), F32)],
                compiler_params=params,
                cost_estimate=pl.CostEstimate(
                    flops=4 * piece_rows * occupied * columns,
                    bytes_accessed=3 * piece_rows * occupied * columns,
                    transcendentals=0,
                ),
                name="fold_couplings",
            )(occ_irrep, label_row.reshape(rows), keys, in_hbm(couplings))
        )
        w_mate.append(lax.ppermute(w_own[-1], "vir", [(d, d ^ 1) for d in range(devices)]))

    partial = pl.pallas_call(
        functools.partial(product_kernel, pieces),
        out_shape=jax.ShapeDtypeStruct((kept, wide), F32),
        in_specs=[vmem] * (3 + pieces) + [hbm] * pieces,
        out_specs=vmem,
        scratch_shapes=[
            pltpu.VMEM((occupied, rows, wide), BF16),
            pltpu.SemaphoreType.DMA((pieces,)),
        ],
        compiler_params=params,
        name="multiply",
    )(
        *[in_vmem(x) for x in (label_k, label_kept, received, *w_own)],
        *[in_hbm(x) for x in w_mate],
    )
    sides = [[d for d in range(devices) if d % 2 == core] for core in (0, 1)]
    parts = lax.all_to_all(
        partial.reshape(chips, rows_out, wide), "vir", 0, 0, axis_index_groups=sides
    )
    return pl.pallas_call(
        finish_kernel,
        out_shape=jax.ShapeDtypeStruct((rows_out, columns), F32),
        in_specs=[vmem] * 3,
        out_specs=vmem,
        compiler_params=params,
        name="unfold",
    )(label_out, keys, parts)


def solution(mesh):
    return jax.shard_map(
        per_device,
        mesh=mesh,
        in_specs=(
            P(("grp", "vir"), None, None),
            P(("grp", "vir"), None, None),
            P("grp"),
            P(),
            P(),
            P("grp"),
            P("grp", None),
        ),
        out_specs=P(("grp", "vir"), None),
        check_vma=False,
    )
```

```python
import functools

import jax
import jax.numpy as jnp
from jax import lax
from jax.experimental import pallas as pl
from jax.experimental.pallas import tpu as pltpu
from jax.sharding import PartitionSpec as P

BS = 4
MOST = 256
LIMIT = 24 * 1024 * 1024
F32, BF16, I32, I16 = jnp.float32, jnp.bfloat16, jnp.int32, jnp.int16
TOP = 32767.0
STEPS = 256.0
SMALL = 2.0**-126
PAD = 16


def irrep_of(index, sizes):
    label = jnp.zeros_like(index)
    end = jnp.int32(0)
    for h in range(sizes.shape[0]):
        end = end + sizes[h]
        label = label + (index >= end).astype(I32)
    return label


def iota(shape, dim):
    return lax.broadcasted_iota(I32, shape, dim)


def column_keys(columns, sizes, j_irrep):
    count = j_irrep.shape[0]
    column = iota((1, columns), 1)
    j = column % count
    j_label = jnp.zeros_like(column)
    for i in range(count):
        j_label = jnp.where(j == i, j_irrep[i], j_label)
    return irrep_of(column // count, sizes) ^ j_label


def block_place(owner_row, rows):
    blocks = owner_row.shape[1]
    first, second = iota((blocks, blocks), 0), iota((blocks, blocks), 1)
    owner_col = jnp.sum(jnp.where(first == second, owner_row, 0), axis=1, keepdims=True)
    earlier = (owner_col == owner_row) & (first < second)
    rank = jnp.sum(earlier.astype(I32), axis=0, keepdims=True)
    return owner_row * rows + rank * BS


def virtual_place(place, virtuals):
    blocks = place.shape[1]
    e, block = iota((virtuals, blocks), 0), iota((virtuals, blocks), 1)
    start = jnp.sum(jnp.where(e // BS == block, place, 0), axis=1, keepdims=True)
    return start + iota((virtuals, 1), 0) % BS


def pack_kernel(
    rows,
    rows_out,
    sizes_hbm,
    occ_hbm,
    pair,
    owner_hbm,
    t_hbm,
    out_hbm,
    place,
    sizes,
    occ,
    owner_row,
    t_vmem,
    out,
    in_sems,
    out_sems,
):
    virtuals = t_hbm.shape[1]
    lanes = 2 * rows
    pairs = (
        (owner_hbm, owner_row),
        (sizes_hbm, sizes),
        (occ_hbm, occ),
        (t_hbm.at[0], t_vmem),
    )
    copies = [
        pltpu.make_async_copy(source, here, in_sems.at[i])
        for i, (source, here) in enumerate(pairs)
    ]
    for copy in copies:
        copy.start()
    copies[0].wait()
    where = block_place(owner_row[...], rows)
    place[...] = jnp.broadcast_to(where, place.shape)
    target = jnp.broadcast_to(virtual_place(where, virtuals), (virtuals, lanes))
    for copy in copies[1:3]:
        copy.wait()
    wanted = pair[0] ^ occ[lax.axis_index("vir")]
    label_e = irrep_of(iota((virtuals, 1), 0), sizes) ^ wanted
    label_a = irrep_of(iota((1, virtuals), 1), sizes)
    copies[3].wait()
    folded = jnp.zeros((virtuals, MOST), F32)
    for k in range(virtuals // MOST):
        part = slice(k * MOST, (k + 1) * MOST)
        folded = folded + jnp.where(
            label_e == label_a[:, part], t_vmem[:, part].astype(F32), 0.0
        )
    folded_t = folded.T.astype(BF16)
    lane = iota((1, lanes), 1)

    def half(values, core):
        return jnp.concatenate(
            [
                values[start : start + rows_out]
                for start in range(core * rows_out, MOST, 2 * rows_out)
            ],
            axis=0,
        )

    sends = []
    for chip in range(out.shape[0] // 2):

        def moved(flip):
            hot = jnp.where(target == (lane ^ flip) + chip * lanes, 1.0, 0.0).astype(BF16)
            return jnp.dot(folded_t, hot, preferred_element_type=F32)

        here = moved(0)
        out[2 * chip] = half(here, 0).astype(BF16)
        if rows % 128 == 0:
            there = half(here, 1)
            out[2 * chip + 1, :, :rows] = there[:, rows:].astype(BF16)
            out[2 * chip + 1, :, rows:] = there[:, :rows].astype(BF16)
        else:
            out[2 * chip + 1] = half(moved(rows), 1).astype(BF16)
        both = pl.ds(2 * chip, 2)
        sends.append(pltpu.make_async_copy(out.at[both], out_hbm.at[both], out_sems.at[chip]))
        sends[-1].start()
    for copy in sends:
        copy.wait()


def label_kernel(
    rows,
    rows_out,
    sizes,
    occ,
    pair,
    j_irrep,
    place,
    label_row,
    label_k,
    label_kept,
    label_out,
    keys,
):
    here = lax.axis_index("vir")
    occupied, lanes = label_k.shape
    virtuals = place.shape[1] * BS
    target = virtual_place(place[:1, :], virtuals)
    lane = iota((virtuals, lanes), 1)
    source = jnp.where(lane < rows, lane + here * rows, lane - rows + (here ^ 1) * rows)
    label_e = irrep_of(iota((virtuals, 1), 0), sizes)
    label = jnp.sum(jnp.where(target == source, label_e, 0), axis=0, keepdims=True)
    label_row[...] = label[:, :rows]
    for m in range(occupied):
        label_k[m : m + 1, :] = label ^ (pair[0] ^ occ[m])
    row = iota(label_kept.shape, 0)
    a = row // rows_out * (2 * rows_out) + here % 2 * rows_out + row % rows_out
    label_kept[...] = irrep_of(a, sizes)
    label_out[...] = irrep_of(iota(label_out.shape, 0) + here * rows_out, sizes) ^ pair[0]
    keys[...] = jnp.broadcast_to(column_keys(keys.shape[1], sizes, j_irrep), keys.shape)


def fold_kernel(first, occ, label_row, keys, w, out, folded):
    step, part = pl.program_id(0), pl.program_id(1)
    row_block, m_block, columns = w.shape
    wide = out.shape[2]
    m_row = iota((m_block, 1), 0)
    occ_col = jnp.zeros((m_block, 1), I32)
    for i in range(m_block):
        occ_col = jnp.where(m_row == i, occ[part * m_block + i], occ_col)
    for i in range(row_block):
        label = label_row[first + step * row_block + i]
        allowed = (occ_col ^ label) == keys[:1, :]
        kept = jnp.where(allowed, w[i].astype(F32), 0.0)
        total = kept[:, :wide]
        for k in range(1, columns // wide):
            total = total + kept[:, k * wide : (k + 1) * wide]
        for k in range(wide // 128):
            folded[k, i * m_block : (i + 1) * m_block, :] = total[:, k * 128 : (k + 1) * 128]
    for i in range(m_block):
        for k in range(wide // 128):
            out[i, :, k * 128 : (k + 1) * 128] = folded[
                k, pl.ds(i, row_block, stride=m_block), :
            ].astype(BF16)


def product_kernel(pieces, label_k, label_kept, t, *refs):
    own, mate_hbm = refs[:pieces], refs[pieces : 2 * pieces]
    coded, out, mate, sems = refs[2 * pieces :]
    occupied, half, lanes = t.shape
    rows = lanes // 2
    kept = out.shape[0]
    size = rows // pieces
    copies = [
        pltpu.make_async_copy(mate_hbm[i], mate.at[:, i * size : (i + 1) * size], sems.at[i])
        for i in range(pieces)
    ]
    for copy in copies:
        copy.start()
    wide_label = jnp.broadcast_to(label_kept[:, :1], (kept, rows))
    out[...] = jnp.zeros(out.shape, F32)
    m_block = max(1, min(occupied, 1024 // rows))

    def accumulate(side, couplings):
        lane = slice(side * rows, (side + 1) * rows)

        @pl.loop(0, occupied // m_block)
        def _(step):
            left, right = [], []
            for i in range(m_block):
                m = step * m_block + i
                wanted = label_k[pl.ds(m, 1), :][:, lane]
                values = t[m][:, lane].astype(F32)
                left.append(
                    jnp.concatenate(
                        [
                            jnp.where(wide_label[k : k + half] == wanted, values, 0.0).astype(BF16)
                            for k in range(0, kept, half)
                        ],
                        axis=0,
                    )
                )
                right.append(couplings(m))
            if rows % 128 == 0:
                left = [jnp.concatenate(left, axis=1)]
                right = [jnp.concatenate(right, axis=0)]
            total = jnp.dot(left[0], right[0], preferred_element_type=F32)
            for x, y in zip(left[1:], right[1:]):
                total = total + jnp.dot(x, y, preferred_element_type=F32)
            out[...] += total

    accumulate(0, lambda m: jnp.concatenate([piece[m] for piece in own], axis=0))
    for copy in copies:
        copy.wait()
    accumulate(1, lambda m: mate[m])
    rows_out = kept // coded.shape[0]
    for chip in range(coded.shape[0]):
        coded[chip] = encode(out[chip * rows_out : (chip + 1) * rows_out, :])


def encode(values):
    row = iota((PAD, 128), 0)
    scales = jnp.zeros((PAD, 128), I32)
    blocks = []
    for i in range(values.shape[1] // 128):
        part = values[:, i * 128 : (i + 1) * 128]
        largest = jnp.maximum(jnp.max(jnp.abs(part), axis=0, keepdims=True), SMALL)
        scale = jnp.floor(jnp.log2(largest) * STEPS) + 2.0
        factor = jnp.exp2(scale * (-0.5 / STEPS))
        blocks.append(jnp.floor(part * factor * (factor * TOP) + 0.5).astype(I32))
        scales = jnp.where(row == i, scale.astype(I32), scales)
    return jnp.concatenate(blocks + [scales], axis=0).astype(I16)


def decode(coded, rows_out):
    values = coded.astype(I32)
    blocks = []
    for i in range((coded.shape[0] - PAD) // rows_out):
        scale = values[coded.shape[0] - PAD + i :][:1].astype(F32)
        factor = jnp.exp2(scale * (0.5 / STEPS))
        part = values[i * rows_out : (i + 1) * rows_out].astype(F32)
        blocks.append(part * (factor * (1.0 / TOP)) * factor)
    return blocks


def finish_kernel(label_out, keys, parts, out):
    chips = parts.shape[0]
    rows_out = out.shape[0]
    total = decode(parts[0], rows_out)
    for q in range(1, chips):
        total = [x + y for x, y in zip(total, decode(parts[q], rows_out))]
    total = jnp.concatenate(total, axis=1)
    wide = total.shape[1]
    for k in range(0, out.shape[1], wide):
        out[:, k : k + wide] = jnp.where(
            label_out[:, :1] == keys[:1, k : k + wide], total, 0.0
        )


in_hbm = functools.partial(pltpu.with_memory_space_constraint, memory_space=pltpu.HBM)
in_vmem = functools.partial(pltpu.with_memory_space_constraint, memory_space=pltpu.VMEM)


def per_device(amplitudes, couplings, occ_irrep, pair_irrep, j_irrep, block_sizes, owner):
    devices = lax.axis_size("vir")
    chips = devices // 2
    virtuals = amplitudes.shape[2]
    rows, occupied, columns = couplings.shape
    wide = columns // virtuals * MOST
    rows_out = virtuals // devices
    kept = virtuals // 2
    lanes = 2 * rows
    blocks = owner.shape[0]
    smem = pl.BlockSpec(memory_space=pltpu.SMEM)
    vmem = pl.BlockSpec(memory_space=pltpu.VMEM)
    hbm = pl.BlockSpec(memory_space=pltpu.HBM)
    params = pltpu.CompilerParams(vmem_limit_bytes=LIMIT)

    outgoing, place = pl.pallas_call(
        functools.partial(pack_kernel, rows, rows_out),
        out_shape=(
            pltpu.HBM((devices, MOST // 2, lanes), BF16),
            jax.ShapeDtypeStruct((8, blocks), I32),
        ),
        in_specs=[hbm, hbm, smem, hbm, hbm],
        out_specs=(hbm, vmem),
        scratch_shapes=[
            pltpu.SMEM(block_sizes.shape, I32),
            pltpu.SMEM(occ_irrep.shape, I32),
            pltpu.VMEM((1, blocks), I32),
            pltpu.VMEM((virtuals, virtuals), BF16),
            pltpu.VMEM((devices, MOST // 2, lanes), BF16),
            pltpu.SemaphoreType.DMA((4,)),
            pltpu.SemaphoreType.DMA((chips,)),
        ],
        compiler_params=params,
        name="pack_amplitudes",
    )(
        in_hbm(block_sizes),
        in_hbm(occ_irrep),
        pair_irrep,
        in_hbm(owner.reshape(1, blocks)),
        in_hbm(amplitudes),
    )
    received = lax.all_to_all(outgoing, "vir", 0, 0)

    label_row, label_k, label_kept, label_out, keys = pl.pallas_call(
        functools.partial(label_kernel, rows, rows_out),
        out_shape=(
            jax.ShapeDtypeStruct((1, rows), I32),
            jax.ShapeDtypeStruct((occupied, lanes), I32),
            jax.ShapeDtypeStruct((kept, 128), I32),
            jax.ShapeDtypeStruct((rows_out, 128), I32),
            jax.ShapeDtypeStruct((8, columns), I32),
        ),
        in_specs=[smem] * 4 + [vmem],
        out_specs=(vmem,) * 5,
        compiler_params=params,
        name="labels",
    )(block_sizes, occ_irrep, pair_irrep, j_irrep, place)

    row_block, m_block = 16, 16
    pieces = max(1, rows // 32)
    piece_rows = rows // pieces
    w_own, w_mate = [], []
    for piece in range(pieces):
        first = piece * piece_rows
        w_own.append(
            pl.pallas_call(
                functools.partial(fold_kernel, first),
                out_shape=jax.ShapeDtypeStruct((occupied, piece_rows, wide), BF16),
                grid=(piece_rows // row_block, occupied // m_block),
                in_specs=[smem, smem, vmem]
                + [
                    pl.BlockSpec(
                        (row_block, m_block, columns),
                        lambda i, j, skip=first // row_block: (skip + i, j, 0),
                    )
                ],
                out_specs=pl.BlockSpec((m_block, row_block, wide), lambda i, j: (j, i, 0)),
                scratch_shapes=[pltpu.VMEM((wide // 128, row_block * m_block, 128), F32)],
                compiler_params=params,
                cost_estimate=pl.CostEstimate(
                    flops=4 * piece_rows * occupied * columns,
                    bytes_accessed=3 * piece_rows * occupied * columns,
                    transcendentals=0,
                ),
                name="fold_couplings",
            )(occ_irrep, label_row.reshape(rows), keys, in_hbm(couplings))
        )
        w_mate.append(lax.ppermute(w_own[-1], "vir", [(d, d ^ 1) for d in range(devices)]))

    partial = pl.pallas_call(
        functools.partial(product_kernel, pieces),
        out_shape=jax.ShapeDtypeStruct((chips, wide // 128 * rows_out + PAD, 128), I16),
        in_specs=[vmem] * (3 + pieces) + [hbm] * pieces,
        out_specs=vmem,
        scratch_shapes=[
            pltpu.VMEM((kept, wide), F32),
            pltpu.VMEM((occupied, rows, wide), BF16),
            pltpu.SemaphoreType.DMA((pieces,)),
        ],
        compiler_params=params,
        name="multiply",
    )(
        *[in_vmem(x) for x in (label_k, label_kept, received, *w_own)],
        *[in_hbm(x) for x in w_mate],
    )
    sides = [[d for d in range(devices) if d % 2 == core] for core in (0, 1)]
    parts = lax.all_to_all(partial, "vir", 0, 0, axis_index_groups=sides)
    return pl.pallas_call(
        finish_kernel,
        out_shape=jax.ShapeDtypeStruct((rows_out, columns), F32),
        in_specs=[vmem] * 3,
        out_specs=vmem,
        compiler_params=params,
        name="unfold",
    )(label_out, keys, parts)


def solution(mesh):
    return jax.shard_map(
        per_device,
        mesh=mesh,
        in_specs=(
            P(("grp", "vir"), None, None),
            P(("grp", "vir"), None, None),
            P("grp"),
            P(),
            P(),
            P("grp"),
            P("grp", None),
        ),
        out_specs=P(("grp", "vir"), None),
        check_vma=False,
    )
```

```python
import functools

import jax
import jax.numpy as jnp
from jax import lax
from jax.experimental import pallas as pl
from jax.experimental.pallas import tpu as pltpu
from jax.sharding import PartitionSpec as P

BS = 4
MOST = 256
LIMIT = 24 * 1024 * 1024
F32, BF16, I32, I16 = jnp.float32, jnp.bfloat16, jnp.int32, jnp.int16
TOP = 32767.0
STEPS = 256.0
SMALL = 2.0**-126
HALF = MOST // 2
ALIGN = 16
PAD = 16


def irrep_of(index, sizes):
    label = jnp.zeros_like(index)
    end = jnp.int32(0)
    for h in range(sizes.shape[0]):
        end = end + sizes[h]
        label = label + (index >= end).astype(I32)
    return label


def iota(shape, dim):
    return lax.broadcasted_iota(I32, shape, dim)


def column_keys(columns, sizes, j_irrep):
    count = j_irrep.shape[0]
    column = iota((1, columns), 1)
    j = column % count
    j_label = jnp.zeros_like(column)
    for i in range(count):
        j_label = jnp.where(j == i, j_irrep[i], j_label)
    return irrep_of(column // count, sizes) ^ j_label


def block_place(owner_row, rows):
    blocks = owner_row.shape[1]
    first, second = iota((blocks, blocks), 0), iota((blocks, blocks), 1)
    owner_col = jnp.sum(jnp.where(first == second, owner_row, 0), axis=1, keepdims=True)
    earlier = (owner_col == owner_row) & (first < second)
    rank = jnp.sum(earlier.astype(I32), axis=0, keepdims=True)
    return owner_row * rows + rank * BS


def virtual_place(place, virtuals):
    blocks = place.shape[1]
    e, block = iota((virtuals, blocks), 0), iota((virtuals, blocks), 1)
    start = jnp.sum(jnp.where(e // BS == block, place, 0), axis=1, keepdims=True)
    return start + iota((virtuals, 1), 0) % BS


def wide_flags(partner, sizes):
    wide = jnp.zeros_like(partner)
    for h in range(sizes.shape[0]):
        wide = jnp.where(partner == h, (sizes[h] > HALF).astype(I32), wide)
    return wide


def wide_block(block, wanted, sizes):
    wide = jnp.zeros_like(block ^ wanted)
    for r in range(BS):
        wide = wide | wide_flags(irrep_of(block * BS + r, sizes) ^ wanted, sizes)
    return wide


def slots_needed(wide, owned):
    return wide + (owned - wide + 1) // 2


def slots_of(wide, rank, rank_wide, count_wide):
    rank_narrow = rank - rank_wide
    slot = jnp.where(wide == 1, rank_wide, count_wide + rank_narrow // 2)
    return slot, jnp.where(wide == 1, 0, 1 + rank_narrow % 2)


def pack_kernel(
    rows_out,
    classes,
    sizes_hbm,
    occ_hbm,
    pair,
    owner_hbm,
    t_hbm,
    *refs,
):
    outs, choice = refs[: len(classes)], refs[len(classes)]
    sizes, occ, owner_row, t_vmem, folds, filled, out, in_sems, out_sems = refs[len(classes) + 1 :]
    virtuals = t_hbm.shape[1]
    blocks = owner_row.shape[1]
    chips = outs[0].shape[0] // 2
    quarter = HALF // 2
    pairs = (
        (owner_hbm, owner_row),
        (sizes_hbm, sizes),
        (occ_hbm, occ),
        (t_hbm.at[0], t_vmem),
    )
    copies = [
        pltpu.make_async_copy(source, here, in_sems.at[i])
        for i, (source, here) in enumerate(pairs)
    ]
    for copy in copies:
        copy.start()
    copies[0].wait()
    chip_row = owner_row[...] // 2
    first, second = iota((blocks, blocks), 0), iota((blocks, blocks), 1)
    chip_col = jnp.sum(jnp.where(first == second, chip_row, 0), axis=1, keepdims=True)
    same = chip_col == chip_row
    before = jnp.where(same & (first < second), 1.0, 0.0).astype(BF16)
    same = jnp.where(same, 1.0, 0.0).astype(BF16)
    for copy in copies[1:3]:
        copy.wait()
    wanted = pair[0] ^ occ[lax.axis_index("vir")]
    row = iota((8, blocks), 0)
    wide_all = wide_block(iota((1, blocks), 1), row, sizes)
    own = jnp.sum(jnp.where(row == wanted, wide_all, 0), axis=0, keepdims=True)
    rest = jnp.where(row == 0, own, jnp.where(row == 1, 1, 0))
    tallies = jnp.concatenate([wide_all, rest], axis=0).astype(F32).astype(BF16)
    ahead = jnp.dot(tallies, before, preferred_element_type=F32).astype(I32)
    total = jnp.dot(tallies, same, preferred_element_type=F32).astype(I32)
    owned = total[9:10]

    index = jnp.int32(0)
    if len(classes) > 1:
        used = jnp.int32(0)
        for m in range(occ.shape[0]):
            used = used | (jnp.int32(1) << (pair[0] ^ occ[m]))
        need = slots_needed(total[:8], owned) * ((used >> row) & 1)
        need = jnp.max(need) * BS
        for size in classes[:-1]:
            index = index + (need > size).astype(I32)
    choice[0] = index

    step = ALIGN // BS
    chip = iota((chips, 1), 0)
    lengths = jnp.where(chip == chip_row, slots_needed(total[8:9], owned), 0)
    lengths = (jnp.max(lengths, axis=1, keepdims=True) + (step - 1)) // step
    starts_row = jnp.sum(jnp.where(chip < chip_row, lengths, 0), axis=0, keepdims=True)
    starts = [jnp.sum(jnp.where(chip < q, lengths, 0)) for q in range(chips)]
    slot, kind = slots_of(own, ahead[9:10], ahead[8:9], total[8:9])
    place = starts_row * step + slot
    targets = [jnp.where(kind == 2, -1, place), jnp.where(kind == 1, -1, place)]

    partner = irrep_of(iota((virtuals, 1), 0), sizes) ^ wanted
    label_a = irrep_of(iota((1, virtuals), 1), sizes)
    copies[3].wait()
    halves = [jnp.zeros((virtuals, HALF), F32) for _ in range(2)]
    for i, k in enumerate(range(0, virtuals, HALF)):
        kept = jnp.where(partner == label_a[:, k : k + HALF], t_vmem[:, k : k + HALF].astype(F32), 0.0)
        halves[i % 2] = halves[i % 2] + kept
    for h in range(2):
        folds[h] = halves[h]
    first, second = iota((blocks, blocks), 0), iota((blocks, blocks), 1)
    narrow = jnp.sum(jnp.where(first == second, own, 0), axis=1, keepdims=True) == 0
    blank = jnp.zeros((blocks, quarter), F32)
    sources = [[], []]
    for r in range(BS):
        both = [folds[h, pl.ds(r, blocks, stride=BS), :] for h in range(2)]
        for h in range(2):
            source = both[h] + jnp.where(narrow, both[1 - h], 0.0)
            if rows_out < quarter:
                old, new = iota((HALF, HALF), 0), iota((HALF, HALF), 1)
                core, x = new // quarter, new % quarter
                lane = x // rows_out * (2 * rows_out) + core * rows_out + x % rows_out
                order = jnp.where(old == lane, 1.0, 0.0).astype(BF16)
                source = jnp.dot(source.astype(BF16), order, preferred_element_type=F32)
            for core in range(2):
                side = source[:, core * quarter : (core + 1) * quarter]
                sources[h] += [blank, side] if h else [side, blank]
    sources = jnp.concatenate([jnp.concatenate(x, axis=1) for x in sources], axis=0).astype(BF16)
    count = filled.shape[1] // BS
    slot = iota((count, 1), 0)
    hot = jnp.concatenate([jnp.where(x == slot, 1.0, 0.0) for x in targets], axis=1).astype(BF16)
    moved = jnp.dot(hot, sources, preferred_element_type=F32)
    for r in range(BS):
        for core in range(2):
            part = slice((2 * r + core) * HALF, (2 * r + core + 1) * HALF)
            filled[core, pl.ds(r, count, stride=BS), :] = moved[:, part]
    for core in range(2):
        out[core, : filled.shape[1]] = filled[core].astype(BF16)
        rest = out.shape[1] - filled.shape[1]
        out[core, filled.shape[1] :] = jnp.zeros((rest, HALF), BF16)

    def send(k, device):
        start = pl.multiple_of(starts[device // 2] * ALIGN, ALIGN)
        return pltpu.make_async_copy(
            out.at[device % 2, pl.ds(start, classes[k])],
            outs[k].at[device],
            out_sems.at[device],
        )

    for k in range(len(classes)):

        @pl.when(index == k)
        def _(k=k):
            for device in range(2 * chips):
                send(k, device).start()
            for device in range(2 * chips):
                send(k, device).wait()


def label_kernel(
    rows,
    rows_out,
    sizes,
    occ,
    pair,
    j_irrep,
    owner_row,
    label_row,
    label_k,
    slots,
    kinds,
    label_kept,
    label_out,
    keys,
):
    here = lax.axis_index("vir")
    occupied, lanes = label_k.shape
    virtuals = owner_row.shape[1] * BS
    target = virtual_place(block_place(owner_row[...], rows), virtuals)
    lane = iota((virtuals, lanes), 1)
    source = jnp.where(lane < rows, lane + here * rows, lane - rows + (here ^ 1) * rows)
    virtual = iota((virtuals, lanes), 0)
    e_row = jnp.sum(jnp.where(target == source, virtual + 1, 0), axis=0, keepdims=True) - 1
    label = irrep_of(e_row, sizes)
    label_row[...] = label[:, :rows]
    m_row = iota((occupied, 1), 0)
    wanted = jnp.zeros((occupied, 1), I32)
    for m in range(occupied):
        wanted = jnp.where(m_row == m, pair[0] ^ occ[m], wanted)
    partner = label ^ wanted
    label_k[...] = partner
    first, second = iota((lanes, lanes), 0), iota((lanes, lanes), 1)
    e_col = jnp.sum(jnp.where(first == second, e_row, 0), axis=1, keepdims=True)
    ahead = (e_col >= 0) & (e_col % BS == 0) & (e_col // BS < e_row // BS)
    wide = jnp.where(e_row >= 0, wide_block(jnp.maximum(e_row, 0) // BS, wanted, sizes), 0)
    rank_wide = jnp.dot(
        wide.astype(F32).astype(BF16),
        jnp.where(ahead, 1.0, 0.0).astype(BF16),
        preferred_element_type=F32,
    ).astype(I32)
    rank = jnp.sum(ahead.astype(I32), axis=0, keepdims=True)
    count_wide = jnp.sum(wide, axis=1, keepdims=True) // BS
    slot, kind = slots_of(wide, rank, rank_wide, count_wide)
    slots[...] = jnp.where(e_row >= 0, slot * BS + e_row % BS, -1)
    kinds[...] = kind
    row = iota(label_kept.shape, 0)
    a = row // rows_out * (2 * rows_out) + here % 2 * rows_out + row % rows_out
    label_kept[...] = irrep_of(a, sizes)
    label_out[...] = irrep_of(iota(label_out.shape, 0) + here * rows_out, sizes) ^ pair[0]
    keys[...] = jnp.broadcast_to(column_keys(keys.shape[1], sizes, j_irrep), keys.shape)


def fold_kernel(first, occ, label_row, keys, w, out, folded):
    step, part = pl.program_id(0), pl.program_id(1)
    row_block, m_block, columns = w.shape
    wide = out.shape[2]
    m_row = iota((m_block, 1), 0)
    occ_col = jnp.zeros((m_block, 1), I32)
    for i in range(m_block):
        occ_col = jnp.where(m_row == i, occ[part * m_block + i], occ_col)
    for i in range(row_block):
        label = label_row[first + step * row_block + i]
        allowed = (occ_col ^ label) == keys[:1, :]
        kept = jnp.where(allowed, w[i].astype(F32), 0.0)
        total = kept[:, :wide]
        for k in range(1, columns // wide):
            total = total + kept[:, k * wide : (k + 1) * wide]
        for k in range(wide // 128):
            folded[k, i * m_block : (i + 1) * m_block, :] = total[:, k * 128 : (k + 1) * 128]
    for i in range(m_block):
        for k in range(wide // 128):
            out[i, :, k * 128 : (k + 1) * 128] = folded[
                k, pl.ds(i, row_block, stride=m_block), :
            ].astype(BF16)


def product_kernel(pieces, label_k, slots, kinds, label_kept, packed, *refs):
    own, mate_hbm = refs[:pieces], refs[pieces : 2 * pieces]
    coded, out, t, mate, sems = refs[2 * pieces :]
    occupied, half, lanes = t.shape
    rows = lanes // 2
    kept = out.shape[0]
    size = rows // pieces
    copies = [
        pltpu.make_async_copy(mate_hbm[i], mate.at[:, i * size : (i + 1) * size], sems.at[i])
        for i in range(pieces)
    ]
    for copy in copies:
        copy.start()
    slot = iota((packed.shape[1], 1), 0)
    unpacked = max(1, min(occupied, 8))

    @pl.loop(0, occupied // unpacked)
    def _(step):
        for i in range(unpacked):
            m = step * unpacked + i
            hot = jnp.where(slots[pl.ds(m, 1), :] == slot, 1.0, 0.0).astype(BF16)
            both = lax.dot_general(
                packed[m], hot, (((0,), (0,)), ((), ())), preferred_element_type=F32
            )
            low, high = both[: half // 2], both[half // 2 :]
            kind = kinds[pl.ds(m, 1), :]
            t[m] = jnp.concatenate(
                [jnp.where(kind == 2, high, low), jnp.where(kind == 1, low, high)], axis=0
            ).astype(BF16)

    wide_label = jnp.broadcast_to(label_kept[:, :1], (kept, rows))
    out[...] = jnp.zeros(out.shape, F32)
    m_block = max(1, min(occupied, 1024 // rows))

    def accumulate(side, couplings):
        lane = slice(side * rows, (side + 1) * rows)

        @pl.loop(0, occupied // m_block)
        def _(step):
            left, right = [], []
            for i in range(m_block):
                m = step * m_block + i
                wanted = label_k[pl.ds(m, 1), :][:, lane]
                values = t[m][:, lane].astype(F32)
                left.append(
                    jnp.concatenate(
                        [
                            jnp.where(wide_label[k : k + half] == wanted, values, 0.0).astype(BF16)
                            for k in range(0, kept, half)
                        ],
                        axis=0,
                    )
                )
                right.append(couplings(m))
            if rows % 128 == 0:
                left = [jnp.concatenate(left, axis=1)]
                right = [jnp.concatenate(right, axis=0)]
            total = jnp.dot(left[0], right[0], preferred_element_type=F32)
            for x, y in zip(left[1:], right[1:]):
                total = total + jnp.dot(x, y, preferred_element_type=F32)
            out[...] += total

    accumulate(0, lambda m: jnp.concatenate([piece[m] for piece in own], axis=0))
    for copy in copies:
        copy.wait()
    accumulate(1, lambda m: mate[m])
    rows_out = kept // coded.shape[0]
    for chip in range(coded.shape[0]):
        coded[chip] = encode(out[chip * rows_out : (chip + 1) * rows_out, :])


def encode(values):
    row = iota((PAD, 128), 0)
    scales = jnp.zeros((PAD, 128), I32)
    blocks = []
    for i in range(values.shape[1] // 128):
        part = values[:, i * 128 : (i + 1) * 128]
        largest = jnp.maximum(jnp.max(jnp.abs(part), axis=0, keepdims=True), SMALL)
        scale = jnp.floor(jnp.log2(largest) * STEPS) + 2.0
        factor = jnp.exp2(scale * (-0.5 / STEPS))
        blocks.append(jnp.floor(part * factor * (factor * TOP) + 0.5).astype(I32))
        scales = jnp.where(row == i, scale.astype(I32), scales)
    return jnp.concatenate(blocks + [scales], axis=0).astype(I16)


def decode(coded, rows_out):
    values = coded.astype(I32)
    blocks = []
    for i in range((coded.shape[0] - PAD) // rows_out):
        scale = values[coded.shape[0] - PAD + i :][:1].astype(F32)
        factor = jnp.exp2(scale * (0.5 / STEPS))
        part = values[i * rows_out : (i + 1) * rows_out].astype(F32)
        blocks.append(part * (factor * (1.0 / TOP)) * factor)
    return blocks


def finish_kernel(label_out, keys, parts, out):
    chips = parts.shape[0]
    rows_out = out.shape[0]
    total = decode(parts[0], rows_out)
    for q in range(1, chips):
        total = [x + y for x, y in zip(total, decode(parts[q], rows_out))]
    total = jnp.concatenate(total, axis=1)
    wide = total.shape[1]
    for k in range(0, out.shape[1], wide):
        out[:, k : k + wide] = jnp.where(
            label_out[:, :1] == keys[:1, k : k + wide], total, 0.0
        )


in_hbm = functools.partial(pltpu.with_memory_space_constraint, memory_space=pltpu.HBM)
in_vmem = functools.partial(pltpu.with_memory_space_constraint, memory_space=pltpu.VMEM)


def per_device(amplitudes, couplings, occ_irrep, pair_irrep, j_irrep, block_sizes, owner):
    devices = lax.axis_size("vir")
    chips = devices // 2
    virtuals = amplitudes.shape[2]
    rows, occupied, columns = couplings.shape
    wide = columns // virtuals * MOST
    rows_out = virtuals // devices
    kept = virtuals // 2
    lanes = 2 * rows
    blocks = owner.shape[0]
    smem = pl.BlockSpec(memory_space=pltpu.SMEM)
    vmem = pl.BlockSpec(memory_space=pltpu.VMEM)
    hbm = pl.BlockSpec(memory_space=pltpu.HBM)
    params = pltpu.CompilerParams(vmem_limit_bytes=LIMIT)

    classes = [lanes]
    if lanes % 256 == 0:
        classes = [lanes // 16 * part for part in (10, 11, 12, 13, 16)]
    owner_row = owner.reshape(1, blocks)
    *outgoing, choice = pl.pallas_call(
        functools.partial(pack_kernel, rows_out, classes),
        out_shape=[jax.ShapeDtypeStruct((devices, size, HALF), BF16) for size in classes]
        + [jax.ShapeDtypeStruct((1,), I32)],
        in_specs=[hbm, hbm, smem, hbm, hbm],
        out_specs=[hbm] * len(classes) + [smem],
        scratch_shapes=[
            pltpu.SMEM(block_sizes.shape, I32),
            pltpu.SMEM(occ_irrep.shape, I32),
            pltpu.VMEM((1, blocks), I32),
            pltpu.VMEM((virtuals, virtuals), BF16),
            pltpu.VMEM((2, virtuals, HALF), F32),
            pltpu.VMEM((2, virtuals + chips * ALIGN, HALF), F32),
            pltpu.VMEM((2, virtuals + chips * ALIGN + lanes, HALF), BF16),
            pltpu.SemaphoreType.DMA((4,)),
            pltpu.SemaphoreType.DMA((devices,)),
        ],
        compiler_params=params,
        name="pack_amplitudes",
    )(
        in_hbm(block_sizes),
        in_hbm(occ_irrep),
        pair_irrep,
        in_hbm(owner_row),
        in_hbm(amplitudes),
    )

    def contract(packed):
        received = lax.all_to_all(packed, "vir", 0, 0)

        label_row, label_k, slots, kinds, label_kept, label_out, keys = pl.pallas_call(
            functools.partial(label_kernel, rows, rows_out),
            out_shape=(
                jax.ShapeDtypeStruct((1, rows), I32),
                jax.ShapeDtypeStruct((occupied, lanes), I32),
                jax.ShapeDtypeStruct((occupied, lanes), I32),
                jax.ShapeDtypeStruct((occupied, lanes), I32),
                jax.ShapeDtypeStruct((kept, 128), I32),
                jax.ShapeDtypeStruct((rows_out, 128), I32),
                jax.ShapeDtypeStruct((8, columns), I32),
            ),
            in_specs=[smem] * 4 + [vmem],
            out_specs=(vmem,) * 7,
            compiler_params=params,
            name="labels",
        )(block_sizes, occ_irrep, pair_irrep, j_irrep, owner_row)

        row_block, m_block = 16, 16
        pieces = max(1, rows // 32)
        piece_rows = rows // pieces
        w_own, w_mate = [], []
        for piece in range(pieces):
            first = piece * piece_rows
            w_own.append(
                pl.pallas_call(
                    functools.partial(fold_kernel, first),
                    out_shape=jax.ShapeDtypeStruct((occupied, piece_rows, wide), BF16),
                    grid=(piece_rows // row_block, occupied // m_block),
                    in_specs=[smem, smem, vmem]
                    + [
                        pl.BlockSpec(
                            (row_block, m_block, columns),
                            lambda i, j, skip=first // row_block: (skip + i, j, 0),
                        )
                    ],
                    out_specs=pl.BlockSpec((m_block, row_block, wide), lambda i, j: (j, i, 0)),
                    scratch_shapes=[pltpu.VMEM((wide // 128, row_block * m_block, 128), F32)],
                    compiler_params=params,
                    cost_estimate=pl.CostEstimate(
                        flops=4 * piece_rows * occupied * columns,
                        bytes_accessed=3 * piece_rows * occupied * columns,
                        transcendentals=0,
                    ),
                    name="fold_couplings",
                )(occ_irrep, label_row.reshape(rows), keys, in_hbm(couplings))
            )
            w_mate.append(lax.ppermute(w_own[-1], "vir", [(d, d ^ 1) for d in range(devices)]))

        partial = pl.pallas_call(
            functools.partial(product_kernel, pieces),
            out_shape=jax.ShapeDtypeStruct((chips, wide // 128 * rows_out + PAD, 128), I16),
            in_specs=[vmem] * (5 + pieces) + [hbm] * pieces,
            out_specs=vmem,
            scratch_shapes=[
                pltpu.VMEM((kept, wide), F32),
                pltpu.VMEM((occupied, HALF, lanes), BF16),
                pltpu.VMEM((occupied, rows, wide), BF16),
                pltpu.SemaphoreType.DMA((pieces,)),
            ],
            compiler_params=params,
            name="multiply",
        )(
            *[in_vmem(x) for x in (label_k, slots, kinds, label_kept, received, *w_own)],
            *[in_hbm(x) for x in w_mate],
        )
        sides = [[d for d in range(devices) if d % 2 == core] for core in (0, 1)]
        parts = lax.all_to_all(partial, "vir", 0, 0, axis_index_groups=sides)
        return pl.pallas_call(
            finish_kernel,
            out_shape=pltpu.HBM((rows_out, columns), F32),
            in_specs=[vmem] * 3,
            out_specs=vmem,
            compiler_params=params,
            name="unfold",
        )(label_out, keys, parts)

    if len(classes) == 1:
        return contract(outgoing[0])
    branches = [lambda *packed, k=k: contract(packed[k]) for k in range(len(classes))]
    return lax.switch(choice[0], branches, *outgoing)


def solution(mesh):
    return jax.shard_map(
        per_device,
        mesh=mesh,
        in_specs=(
            P(("grp", "vir"), None, None),
            P(("grp", "vir"), None, None),
            P("grp"),
            P(),
            P(),
            P("grp"),
            P("grp", None),
        ),
        out_specs=P(("grp", "vir"), None),
        check_vma=False,
    )
```

```python
import functools

import jax
import jax.numpy as jnp
from jax import lax
from jax.experimental import pallas as pl
from jax.experimental.pallas import tpu as pltpu
from jax.sharding import PartitionSpec as P

BS = 4
MOST = 256
LIMIT = 24 * 1024 * 1024
F32, BF16, I32, I16 = jnp.float32, jnp.bfloat16, jnp.int32, jnp.int16
TOP = 32767.0
STEPS = 256.0
SMALL = 2.0**-126
HALF = MOST // 2
ALIGN = 16
PAD = 16


def irrep_of(index, sizes):
    label = jnp.zeros_like(index)
    end = jnp.int32(0)
    for h in range(sizes.shape[0] - 1):
        end = end + sizes[h]
        label = jnp.where(index >= end, h + 1, label)
    return label


def iota(shape, dim):
    return lax.broadcasted_iota(I32, shape, dim)


def column_keys(columns, sizes, j_irrep):
    count = j_irrep.shape[0]
    column = iota((1, columns), 1)
    j = column % count
    j_label = jnp.zeros_like(column)
    for i in range(count):
        j_label = jnp.where(j == i, j_irrep[i], j_label)
    return irrep_of(column // count, sizes) ^ j_label


def block_place(owner_row, rows):
    blocks = owner_row.shape[1]
    first, second = iota((blocks, blocks), 0), iota((blocks, blocks), 1)
    owner_col = jnp.sum(jnp.where(first == second, owner_row, 0), axis=1, keepdims=True)
    earlier = (owner_col == owner_row) & (first < second)
    rank = jnp.sum(earlier.astype(I32), axis=0, keepdims=True)
    return owner_row * rows + rank * BS


def virtual_place(place, virtuals):
    blocks = place.shape[1]
    e, block = iota((virtuals, blocks), 0), iota((virtuals, blocks), 1)
    start = jnp.sum(jnp.where(e // BS == block, place, 0), axis=1, keepdims=True)
    return start + iota((virtuals, 1), 0) % BS


def wide_flags(partner, sizes):
    wide = jnp.zeros_like(partner)
    for h in range(sizes.shape[0]):
        wide = jnp.where(partner == h, (sizes[h] > HALF).astype(I32), wide)
    return wide


def wide_block(block, wanted, sizes):
    wide = jnp.zeros_like(block ^ wanted)
    for r in range(BS):
        wide = wide | wide_flags(irrep_of(block * BS + r, sizes) ^ wanted, sizes)
    return wide


def slots_needed(wide, owned):
    return wide + (owned - wide + 1) // 2


def slots_of(wide, rank, rank_wide, count_wide):
    rank_narrow = rank - rank_wide
    slot = jnp.where(wide == 1, rank_wide, count_wide + rank_narrow // 2)
    return slot, jnp.where(wide == 1, 0, 1 + rank_narrow % 2)


def pack_kernel(
    rows_out,
    classes,
    sizes_hbm,
    occ_hbm,
    pair,
    owner_hbm,
    t_hbm,
    *refs,
):
    outs, choice = refs[: len(classes)], refs[len(classes)]
    sizes, occ, owner_row, t_vmem, folds, filled, out, in_sems, out_sems = refs[len(classes) + 1 :]
    virtuals = t_hbm.shape[1]
    blocks = owner_row.shape[1]
    chips = outs[0].shape[0] // 2
    quarter = HALF // 2
    pairs = (
        (owner_hbm, owner_row),
        (sizes_hbm, sizes),
        (occ_hbm, occ),
        (t_hbm.at[0], t_vmem),
    )
    copies = [
        pltpu.make_async_copy(source, here, in_sems.at[i])
        for i, (source, here) in enumerate(pairs)
    ]
    for copy in copies:
        copy.start()
    copies[0].wait()
    chip_row = owner_row[...] // 2
    first, second = iota((blocks, blocks), 0), iota((blocks, blocks), 1)
    chip_col = jnp.sum(jnp.where(first == second, chip_row, 0), axis=1, keepdims=True)
    same = chip_col == chip_row
    before = jnp.where(same & (first < second), 1.0, 0.0).astype(BF16)
    same = jnp.where(same, 1.0, 0.0).astype(BF16)
    for copy in copies[1:3]:
        copy.wait()
    wanted = pair[0] ^ occ[lax.axis_index("vir")]
    row = iota((8, blocks), 0)
    wide_all = wide_block(iota((1, blocks), 1), row, sizes)
    own = jnp.sum(jnp.where(row == wanted, wide_all, 0), axis=0, keepdims=True)
    rest = jnp.where(row == 0, own, jnp.where(row == 1, 1, 0))
    tallies = jnp.concatenate([wide_all, rest], axis=0).astype(F32).astype(BF16)
    ahead = jnp.dot(tallies, before, preferred_element_type=F32).astype(I32)
    total = jnp.dot(tallies, same, preferred_element_type=F32).astype(I32)
    owned = total[9:10]

    index = jnp.int32(0)
    if len(classes) > 1:
        used = jnp.int32(0)
        for m in range(occ.shape[0]):
            used = used | (jnp.int32(1) << (pair[0] ^ occ[m]))
        need = slots_needed(total[:8], owned) * ((used >> row) & 1)
        need = jnp.max(need) * BS
        for size in classes[:-1]:
            index = index + (need > size).astype(I32)
    choice[0] = index

    step = ALIGN // BS
    chip = iota((chips, 1), 0)
    lengths = jnp.where(chip == chip_row, slots_needed(total[8:9], owned), 0)
    lengths = (jnp.max(lengths, axis=1, keepdims=True) + (step - 1)) // step
    starts_row = jnp.sum(jnp.where(chip < chip_row, lengths, 0), axis=0, keepdims=True)
    starts = [jnp.sum(jnp.where(chip < q, lengths, 0)) for q in range(chips)]
    slot, kind = slots_of(own, ahead[9:10], ahead[8:9], total[8:9])
    place = starts_row * step + slot
    targets = [jnp.where(kind == 2, -1, place), jnp.where(kind == 1, -1, place)]

    partner = irrep_of(iota((virtuals, 1), 0), sizes) ^ wanted
    partner = jnp.broadcast_to(partner, (virtuals, HALF)).astype(I16)
    label_a = irrep_of(iota((1, virtuals), 1), sizes).astype(I16)
    copies[3].wait()
    halves = [jnp.zeros((virtuals, HALF), BF16) for _ in range(2)]
    for i, k in enumerate(range(0, virtuals, HALF)):
        here = partner == label_a[:, k : k + HALF]
        kept = jnp.where(here, t_vmem[:, k : k + HALF], jnp.zeros((), BF16))
        halves[i % 2] = halves[i % 2] + kept
    for h in range(2):
        folds[h] = halves[h].astype(F32)
    first, second = iota((blocks, blocks), 0), iota((blocks, blocks), 1)
    narrow = jnp.sum(jnp.where(first == second, own, 0), axis=1, keepdims=True) == 0
    blank = jnp.zeros((blocks, quarter), F32)
    sources = [[[], []], [[], []]]
    for r in range(BS):
        both = [folds[h, pl.ds(r, blocks, stride=BS), :] for h in range(2)]
        for h in range(2):
            source = both[h] + jnp.where(narrow, both[1 - h], 0.0)
            if rows_out < quarter:
                old, new = iota((HALF, HALF), 0), iota((HALF, HALF), 1)
                core, x = new // quarter, new % quarter
                lane = x // rows_out * (2 * rows_out) + core * rows_out + x % rows_out
                order = jnp.where(old == lane, 1.0, 0.0).astype(BF16)
                source = jnp.dot(source.astype(BF16), order, preferred_element_type=F32)
            for core in range(2):
                side = source[:, core * quarter : (core + 1) * quarter]
                sources[core][h] += [blank, side] if h else [side, blank]
    count = filled.shape[1] // BS
    slot = iota((count, 1), 0)
    hot = jnp.concatenate([jnp.where(x == slot, 1.0, 0.0) for x in targets], axis=1).astype(BF16)

    def send(k, device):
        start = pl.multiple_of(starts[device // 2] * ALIGN, ALIGN)
        return pltpu.make_async_copy(
            out.at[device % 2, pl.ds(start, classes[k])],
            outs[k].at[device],
            out_sems.at[device],
        )

    def each(core, act):
        for k in range(len(classes)):

            @pl.when(index == k)
            def _(k=k):
                for device in range(core, 2 * chips, 2):
                    act(send(k, device))

    for core in range(2):
        source = [jnp.concatenate(x, axis=1) for x in sources[core]]
        source = jnp.concatenate(source, axis=0).astype(BF16)
        moved = jnp.dot(hot, source, preferred_element_type=F32)
        for r in range(BS):
            part = slice(r * HALF, (r + 1) * HALF)
            filled[core, pl.ds(r, count, stride=BS), :] = moved[:, part]
        out[core, : filled.shape[1]] = filled[core].astype(BF16)
        rest = out.shape[1] - filled.shape[1]
        out[core, filled.shape[1] :] = jnp.zeros((rest, HALF), BF16)
        each(core, lambda copy: copy.start())
    for core in range(2):
        each(core, lambda copy: copy.wait())


def label_kernel(
    rows,
    rows_out,
    sizes,
    occ,
    pair,
    j_irrep,
    owner_row,
    label_row,
    label_k,
    slots,
    kinds,
    label_kept,
    label_out,
    keys,
):
    here = lax.axis_index("vir")
    occupied, lanes = label_k.shape
    virtuals = owner_row.shape[1] * BS
    target = virtual_place(block_place(owner_row[...], rows), virtuals)
    lane = iota((virtuals, lanes), 1)
    source = jnp.where(lane < rows, lane + here * rows, lane - rows + (here ^ 1) * rows)
    virtual = iota((virtuals, lanes), 0)
    e_row = jnp.sum(jnp.where(target == source, virtual + 1, 0), axis=0, keepdims=True) - 1
    label = irrep_of(e_row, sizes)
    label_row[...] = label[:, :rows]
    m_row = iota((occupied, 1), 0)
    wanted = jnp.zeros((occupied, 1), I32)
    for m in range(occupied):
        wanted = jnp.where(m_row == m, pair[0] ^ occ[m], wanted)
    partner = label ^ wanted
    label_k[...] = partner
    first, second = iota((lanes, lanes), 0), iota((lanes, lanes), 1)
    e_col = jnp.sum(jnp.where(first == second, e_row, 0), axis=1, keepdims=True)
    ahead = (e_col >= 0) & (e_col % BS == 0) & (e_col // BS < e_row // BS)
    wide = jnp.where(e_row >= 0, wide_block(jnp.maximum(e_row, 0) // BS, wanted, sizes), 0)
    rank_wide = jnp.dot(
        wide.astype(F32).astype(BF16),
        jnp.where(ahead, 1.0, 0.0).astype(BF16),
        preferred_element_type=F32,
    ).astype(I32)
    rank = jnp.sum(ahead.astype(I32), axis=0, keepdims=True)
    count_wide = jnp.sum(wide, axis=1, keepdims=True) // BS
    slot, kind = slots_of(wide, rank, rank_wide, count_wide)
    slots[...] = jnp.where(e_row >= 0, slot * BS + e_row % BS, -1)
    kinds[...] = kind
    row = iota(label_kept.shape, 0)
    a = row // rows_out * (2 * rows_out) + here % 2 * rows_out + row % rows_out
    label_kept[...] = irrep_of(a, sizes)
    label_out[...] = irrep_of(iota(label_out.shape, 0) + here * rows_out, sizes) ^ pair[0]
    keys[...] = jnp.broadcast_to(column_keys(keys.shape[1], sizes, j_irrep), keys.shape)


def fold_kernel(first, occ, label_row, keys, w, out, folded):
    step, part = pl.program_id(0), pl.program_id(1)
    row_block, m_block, columns = w.shape
    wide = out.shape[2]
    m_row = iota((m_block, 1), 0)
    occ_col = jnp.zeros((m_block, 1), I32)
    for i in range(m_block):
        occ_col = jnp.where(m_row == i, occ[part * m_block + i], occ_col)

    @pl.loop(0, row_block // 4)
    def _(quad):
        for i in range(4):
            row = quad * 4 + i
            label = label_row[first + step * row_block + row]
            allowed = (occ_col ^ label) == keys[:1, :]
            kept = jnp.where(allowed, w[row].astype(F32), 0.0)
            total = kept[:, :wide]
            for k in range(1, columns // wide):
                total = total + kept[:, k * wide : (k + 1) * wide]
            here = pl.ds(pl.multiple_of(row * m_block, m_block), m_block)
            for k in range(wide // 128):
                folded[k, here, :] = total[:, k * 128 : (k + 1) * 128]

    for i in range(m_block):
        for k in range(wide // 128):
            out[i, :, k * 128 : (k + 1) * 128] = folded[
                k, pl.ds(i, row_block, stride=m_block), :
            ].astype(BF16)


def product_kernel(pieces, label_k, slots, kinds, label_kept, packed, *refs):
    own, mate_hbm = refs[:pieces], refs[pieces : 2 * pieces]
    coded, out, t, mate, sems = refs[2 * pieces :]
    occupied, half, lanes = t.shape
    rows = lanes // 2
    kept = out.shape[0]
    size = rows // pieces
    copies = [
        pltpu.make_async_copy(mate_hbm[i], mate.at[:, i * size : (i + 1) * size], sems.at[i])
        for i in range(pieces)
    ]
    for copy in copies:
        copy.start()
    slot = iota((packed.shape[1], 1), 0)
    unpacked = max(1, min(occupied, 8))

    @pl.loop(0, occupied // unpacked)
    def _(step):
        for i in range(unpacked):
            m = step * unpacked + i
            hot = jnp.where(slots[pl.ds(m, 1), :] == slot, 1.0, 0.0).astype(BF16)
            both = lax.dot_general(
                packed[m], hot, (((0,), (0,)), ((), ())), preferred_element_type=F32
            )
            low, high = both[: half // 2], both[half // 2 :]
            kind = kinds[pl.ds(m, 1), :]
            t[m] = jnp.concatenate(
                [jnp.where(kind == 2, high, low), jnp.where(kind == 1, low, high)], axis=0
            ).astype(BF16)

    wide_label = jnp.broadcast_to(label_kept[:, :1], (kept, rows))

    def expand(m, side):
        lane = slice(side * rows, (side + 1) * rows)
        wanted = label_k[pl.ds(m, 1), :][:, lane]
        values = t[m][:, lane].astype(F32)
        return jnp.concatenate(
            [
                jnp.where(wide_label[k : k + half] == wanted, values, 0.0).astype(BF16)
                for k in range(0, kept, half)
            ],
            axis=0,
        )

    def couplings(m, side):
        return mate[m] if side else jnp.concatenate([piece[m] for piece in own], axis=0)

    def arrived(side):
        for copy in copies if side else ():
            copy.wait()

    if rows % 128 == 0:
        for side in range(2):
            arrived(side)
            left = jnp.concatenate([expand(m, side) for m in range(occupied)], axis=1)
            right = jnp.concatenate([couplings(m, side) for m in range(occupied)], axis=0)
            total = jnp.dot(left, right, preferred_element_type=F32)
            out[...] = out[...] + total if side else total
    else:
        arrived(1)
        out[...] = jnp.zeros(out.shape, F32)

        @pl.loop(0, occupied)
        def _(m):
            for side in range(2):
                out[...] += jnp.dot(
                    expand(m, side), couplings(m, side), preferred_element_type=F32
                )

    rows_out = kept // coded.shape[0]
    for chip in range(coded.shape[0]):
        coded[chip] = encode(out[chip * rows_out : (chip + 1) * rows_out, :])


def encode(values):
    row = iota((PAD, 128), 0)
    scales = jnp.zeros((PAD, 128), I32)
    blocks = []
    for i in range(values.shape[1] // 128):
        part = values[:, i * 128 : (i + 1) * 128]
        largest = jnp.maximum(jnp.max(jnp.abs(part), axis=0, keepdims=True), SMALL)
        scale = jnp.floor(jnp.log2(largest) * STEPS) + 2.0
        factor = jnp.exp2(scale * (-0.5 / STEPS))
        blocks.append(jnp.floor(part * factor * (factor * TOP) + 0.5).astype(I32))
        scales = jnp.where(row == i, scale.astype(I32), scales)
    return jnp.concatenate(blocks + [scales], axis=0).astype(I16)


def decode(coded, rows_out):
    values = coded.astype(I32)
    blocks = []
    for i in range((coded.shape[0] - PAD) // rows_out):
        scale = values[coded.shape[0] - PAD + i :][:1].astype(F32)
        factor = jnp.exp2(scale * (0.5 / STEPS))
        part = values[i * rows_out : (i + 1) * rows_out].astype(F32)
        blocks.append(part * (factor * (1.0 / TOP)) * factor)
    return blocks


def finish_kernel(label_out, keys, parts, out):
    chips = parts.shape[0]
    rows_out = out.shape[0]
    total = decode(parts[0], rows_out)
    for q in range(1, chips):
        total = [x + y for x, y in zip(total, decode(parts[q], rows_out))]
    total = jnp.concatenate(total, axis=1)
    wide = total.shape[1]
    for k in range(0, out.shape[1], wide):
        out[:, k : k + wide] = jnp.where(
            label_out[:, :1] == keys[:1, k : k + wide], total, 0.0
        )


in_hbm = functools.partial(pltpu.with_memory_space_constraint, memory_space=pltpu.HBM)
in_vmem = functools.partial(pltpu.with_memory_space_constraint, memory_space=pltpu.VMEM)


def per_device(amplitudes, couplings, occ_irrep, pair_irrep, j_irrep, block_sizes, owner):
    devices = lax.axis_size("vir")
    chips = devices // 2
    virtuals = amplitudes.shape[2]
    rows, occupied, columns = couplings.shape
    wide = columns // virtuals * MOST
    rows_out = virtuals // devices
    kept = virtuals // 2
    lanes = 2 * rows
    blocks = owner.shape[0]
    smem = pl.BlockSpec(memory_space=pltpu.SMEM)
    vmem = pl.BlockSpec(memory_space=pltpu.VMEM)
    hbm = pl.BlockSpec(memory_space=pltpu.HBM)
    params = pltpu.CompilerParams(vmem_limit_bytes=LIMIT)

    classes = [lanes]
    if lanes % 256 == 0:
        classes = [lanes // 16 * part for part in (10, 11, 12, 13, 14, 16)]
    owner_row = owner.reshape(1, blocks)
    *outgoing, choice = pl.pallas_call(
        functools.partial(pack_kernel, rows_out, classes),
        out_shape=[jax.ShapeDtypeStruct((devices, size, HALF), BF16) for size in classes]
        + [jax.ShapeDtypeStruct((1,), I32)],
        in_specs=[hbm, hbm, smem, hbm, hbm],
        out_specs=[hbm] * len(classes) + [smem],
        scratch_shapes=[
            pltpu.SMEM(block_sizes.shape, I32),
            pltpu.SMEM(occ_irrep.shape, I32),
            pltpu.VMEM((1, blocks), I32),
            pltpu.VMEM((virtuals, virtuals), BF16),
            pltpu.VMEM((2, virtuals, HALF), F32),
            pltpu.VMEM((2, virtuals + chips * ALIGN, HALF), F32),
            pltpu.VMEM((2, virtuals + chips * ALIGN + lanes, HALF), BF16),
            pltpu.SemaphoreType.DMA((4,)),
            pltpu.SemaphoreType.DMA((devices,)),
        ],
        compiler_params=params,
        name="pack_amplitudes",
    )(
        in_hbm(block_sizes),
        in_hbm(occ_irrep),
        pair_irrep,
        in_hbm(owner_row),
        in_hbm(amplitudes),
    )

    def contract(packed):
        received = lax.all_to_all(packed, "vir", 0, 0)

        label_row, label_k, slots, kinds, label_kept, label_out, keys = pl.pallas_call(
            functools.partial(label_kernel, rows, rows_out),
            out_shape=(
                jax.ShapeDtypeStruct((1, rows), I32),
                jax.ShapeDtypeStruct((occupied, lanes), I32),
                jax.ShapeDtypeStruct((occupied, lanes), I32),
                jax.ShapeDtypeStruct((occupied, lanes), I32),
                jax.ShapeDtypeStruct((kept, 128), I32),
                jax.ShapeDtypeStruct((rows_out, 128), I32),
                jax.ShapeDtypeStruct((8, columns), I32),
            ),
            in_specs=[smem] * 4 + [vmem],
            out_specs=(vmem,) * 7,
            compiler_params=params,
            name="labels",
        )(block_sizes, occ_irrep, pair_irrep, j_irrep, owner_row)

        row_block, m_block = 16, 16
        pieces = max(1, rows // 32)
        piece_rows = rows // pieces
        w_own, w_mate = [], []
        for piece in range(pieces):
            first = piece * piece_rows
            w_own.append(
                pl.pallas_call(
                    functools.partial(fold_kernel, first),
                    out_shape=jax.ShapeDtypeStruct((occupied, piece_rows, wide), BF16),
                    grid=(piece_rows // row_block, occupied // m_block),
                    in_specs=[smem, smem, vmem]
                    + [
                        pl.BlockSpec(
                            (row_block, m_block, columns),
                            lambda i, j, skip=first // row_block: (skip + i, j, 0),
                        )
                    ],
                    out_specs=pl.BlockSpec((m_block, row_block, wide), lambda i, j: (j, i, 0)),
                    scratch_shapes=[pltpu.VMEM((wide // 128, row_block * m_block, 128), F32)],
                    compiler_params=params,
                    cost_estimate=pl.CostEstimate(
                        flops=4 * piece_rows * occupied * columns,
                        bytes_accessed=3 * piece_rows * occupied * columns,
                        transcendentals=0,
                    ),
                    name="fold_couplings",
                )(occ_irrep, label_row.reshape(rows), keys, in_hbm(couplings))
            )
            w_mate.append(lax.ppermute(w_own[-1], "vir", [(d, d ^ 1) for d in range(devices)]))

        partial = pl.pallas_call(
            functools.partial(product_kernel, pieces),
            out_shape=jax.ShapeDtypeStruct((chips, wide // 128 * rows_out + PAD, 128), I16),
            in_specs=[vmem] * (5 + pieces) + [hbm] * pieces,
            out_specs=vmem,
            scratch_shapes=[
                pltpu.VMEM((kept, wide), F32),
                pltpu.VMEM((occupied, HALF, lanes), BF16),
                pltpu.VMEM((occupied, rows, wide), BF16),
                pltpu.SemaphoreType.DMA((pieces,)),
            ],
            compiler_params=params,
            name="multiply",
        )(
            *[in_vmem(x) for x in (label_k, slots, kinds, label_kept, received, *w_own)],
            *[in_hbm(x) for x in w_mate],
        )
        sides = [[d for d in range(devices) if d % 2 == core] for core in (0, 1)]
        parts = lax.all_to_all(partial, "vir", 0, 0, axis_index_groups=sides)
        return pl.pallas_call(
            finish_kernel,
            out_shape=pltpu.HBM((rows_out, columns), F32),
            in_specs=[vmem] * 3,
            out_specs=vmem,
            compiler_params=params,
            name="unfold",
        )(label_out, keys, parts)

    if len(classes) == 1:
        return contract(outgoing[0])
    branches = [lambda *packed, k=k: contract(packed[k]) for k in range(len(classes))]
    return lax.switch(choice[0], branches, *outgoing)


def solution(mesh):
    return jax.shard_map(
        per_device,
        mesh=mesh,
        in_specs=(
            P(("grp", "vir"), None, None),
            P(("grp", "vir"), None, None),
            P("grp"),
            P(),
            P(),
            P("grp"),
            P("grp", None),
        ),
        out_specs=P(("grp", "vir"), None),
        check_vma=False,
    )
```

```python
import functools

import jax
import jax.numpy as jnp
from jax import lax
from jax.experimental import pallas as pl
from jax.experimental.pallas import tpu as pltpu
from jax.sharding import PartitionSpec as P

BS = 4
MOST = 256
LIMIT = 24 * 1024 * 1024
F32, BF16, I32, I16 = jnp.float32, jnp.bfloat16, jnp.int32, jnp.int16
TOP = 32767.0
STEPS = 256.0
SMALL = 2.0**-126
HALF = MOST // 2
ALIGN = 16
PAD = 16


def irrep_of(index, sizes):
    label = jnp.zeros_like(index)
    end = jnp.int32(0)
    for h in range(sizes.shape[0] - 1):
        end = end + sizes[h]
        label = jnp.where(index >= end, h + 1, label)
    return label


def iota(shape, dim):
    return lax.broadcasted_iota(I32, shape, dim)


def column_keys(columns, sizes, j_irrep):
    count = j_irrep.shape[0]
    column = iota((1, columns), 1)
    j = column % count
    j_label = jnp.zeros_like(column)
    for i in range(count):
        j_label = jnp.where(j == i, j_irrep[i], j_label)
    return irrep_of(column // count, sizes) ^ j_label


def block_place(owner_row, rows):
    blocks = owner_row.shape[1]
    first, second = iota((blocks, blocks), 0), iota((blocks, blocks), 1)
    owner_col = jnp.sum(jnp.where(first == second, owner_row, 0), axis=1, keepdims=True)
    earlier = (owner_col == owner_row) & (first < second)
    rank = jnp.sum(earlier.astype(I32), axis=0, keepdims=True)
    return owner_row * rows + rank * BS


def virtual_place(place, virtuals):
    blocks = place.shape[1]
    e, block = iota((virtuals, blocks), 0), iota((virtuals, blocks), 1)
    start = jnp.sum(jnp.where(e // BS == block, place, 0), axis=1, keepdims=True)
    return start + iota((virtuals, 1), 0) % BS


def wide_flags(partner, sizes):
    wide = jnp.zeros_like(partner)
    for h in range(sizes.shape[0]):
        wide = jnp.where(partner == h, (sizes[h] > HALF).astype(I32), wide)
    return wide


def wide_block(block, wanted, sizes):
    wide = jnp.zeros_like(block ^ wanted)
    for r in range(BS):
        wide = wide | wide_flags(irrep_of(block * BS + r, sizes) ^ wanted, sizes)
    return wide


def slots_needed(wide, owned):
    return wide + (owned - wide + 1) // 2


def slots_of(wide, rank, rank_wide, count_wide):
    rank_narrow = rank - rank_wide
    slot = jnp.where(wide == 1, rank_wide, count_wide + rank_narrow // 2)
    return slot, jnp.where(wide == 1, 0, 1 + rank_narrow % 2)


def pack_kernel(
    rows_out,
    classes,
    sizes_hbm,
    occ_hbm,
    pair,
    owner_hbm,
    t_hbm,
    *refs,
):
    outs, choice = refs[: len(classes)], refs[len(classes)]
    sizes, occ, owner_row, t_vmem, folds, filled, out, in_sems, out_sems = refs[len(classes) + 1 :]
    virtuals = t_hbm.shape[1]
    blocks = owner_row.shape[1]
    chips = outs[0].shape[0] // 2
    quarter = HALF // 2
    pairs = (
        (owner_hbm, owner_row),
        (sizes_hbm, sizes),
        (occ_hbm, occ),
        (t_hbm.at[0], t_vmem),
    )
    copies = [
        pltpu.make_async_copy(source, here, in_sems.at[i])
        for i, (source, here) in enumerate(pairs)
    ]
    for copy in copies:
        copy.start()
    copies[0].wait()
    chip_row = owner_row[...] // 2
    first, second = iota((blocks, blocks), 0), iota((blocks, blocks), 1)
    chip_col = jnp.sum(jnp.where(first == second, chip_row, 0), axis=1, keepdims=True)
    same = chip_col == chip_row
    before = jnp.where(same & (first < second), 1.0, 0.0).astype(BF16)
    same = jnp.where(same, 1.0, 0.0).astype(BF16)
    for copy in copies[1:3]:
        copy.wait()
    wanted = pair[0] ^ occ[lax.axis_index("vir")]
    row = iota((8, blocks), 0)
    wide_all = wide_block(iota((1, blocks), 1), row, sizes)
    own = jnp.sum(jnp.where(row == wanted, wide_all, 0), axis=0, keepdims=True)
    rest = jnp.where(row == 0, own, jnp.where(row == 1, 1, 0))
    tallies = jnp.concatenate([wide_all, rest], axis=0).astype(F32).astype(BF16)
    ahead = jnp.dot(tallies, before, preferred_element_type=F32).astype(I32)
    total = jnp.dot(tallies, same, preferred_element_type=F32).astype(I32)
    owned = total[9:10]

    index = jnp.int32(0)
    if len(classes) > 1:
        used = jnp.int32(0)
        for m in range(occ.shape[0]):
            used = used | (jnp.int32(1) << (pair[0] ^ occ[m]))
        need = slots_needed(total[:8], owned) * ((used >> row) & 1)
        need = jnp.max(need) * BS
        for size in classes[:-1]:
            index = index + (need > size).astype(I32)
    choice[0] = index

    step = ALIGN // BS
    chip = iota((chips, 1), 0)
    lengths = jnp.where(chip == chip_row, slots_needed(total[8:9], owned), 0)
    lengths = (jnp.max(lengths, axis=1, keepdims=True) + (step - 1)) // step
    starts_row = jnp.sum(jnp.where(chip < chip_row, lengths, 0), axis=0, keepdims=True)
    starts = [jnp.sum(jnp.where(chip < q, lengths, 0)) for q in range(chips)]
    slot, kind = slots_of(own, ahead[9:10], ahead[8:9], total[8:9])
    place = starts_row * step + slot
    targets = [jnp.where(kind == 2, -1, place), jnp.where(kind == 1, -1, place)]

    partner = irrep_of(iota((virtuals, 1), 0), sizes) ^ wanted
    partner = jnp.broadcast_to(partner, (virtuals, HALF)).astype(I16)
    label_a = irrep_of(iota((1, virtuals), 1), sizes).astype(I16)
    copies[3].wait()
    halves = [jnp.zeros((virtuals, HALF), BF16) for _ in range(2)]
    for i, k in enumerate(range(0, virtuals, HALF)):
        here = partner == label_a[:, k : k + HALF]
        kept = jnp.where(here, t_vmem[:, k : k + HALF], jnp.zeros((), BF16))
        halves[i % 2] = halves[i % 2] + kept
    for h in range(2):
        folds[h] = halves[h].astype(F32)
    first, second = iota((blocks, blocks), 0), iota((blocks, blocks), 1)
    narrow = jnp.sum(jnp.where(first == second, own, 0), axis=1, keepdims=True) == 0
    blank = jnp.zeros((blocks, quarter), F32)
    sources = [[[], []], [[], []]]
    for r in range(BS):
        both = [folds[h, pl.ds(r, blocks, stride=BS), :] for h in range(2)]
        for h in range(2):
            source = both[h] + jnp.where(narrow, both[1 - h], 0.0)
            if rows_out < quarter:
                old, new = iota((HALF, HALF), 0), iota((HALF, HALF), 1)
                core, x = new // quarter, new % quarter
                lane = x // rows_out * (2 * rows_out) + core * rows_out + x % rows_out
                order = jnp.where(old == lane, 1.0, 0.0).astype(BF16)
                source = jnp.dot(source.astype(BF16), order, preferred_element_type=F32)
            for core in range(2):
                side = source[:, core * quarter : (core + 1) * quarter]
                sources[core][h] += [blank, side] if h else [side, blank]
    count = filled.shape[1] // BS
    slot = iota((count, 1), 0)
    hot = jnp.concatenate([jnp.where(x == slot, 1.0, 0.0) for x in targets], axis=1).astype(BF16)

    def send(k, device):
        start = pl.multiple_of(starts[device // 2] * ALIGN, ALIGN)
        return pltpu.make_async_copy(
            out.at[device % 2, pl.ds(start, classes[k])],
            outs[k].at[device],
            out_sems.at[device],
        )

    def each(core, act):
        for k in range(len(classes)):

            @pl.when(index == k)
            def _(k=k):
                for device in range(core, 2 * chips, 2):
                    act(send(k, device))

    for core in range(2):
        source = [jnp.concatenate(x, axis=1) for x in sources[core]]
        source = jnp.concatenate(source, axis=0).astype(BF16)
        moved = jnp.dot(hot, source, preferred_element_type=F32)
        for r in range(BS):
            part = slice(r * HALF, (r + 1) * HALF)
            filled[core, pl.ds(r, count, stride=BS), :] = moved[:, part]
        out[core, : filled.shape[1]] = filled[core].astype(BF16)
        rest = out.shape[1] - filled.shape[1]
        out[core, filled.shape[1] :] = jnp.zeros((rest, HALF), BF16)
        each(core, lambda copy: copy.start())
    for core in range(2):
        each(core, lambda copy: copy.wait())


def label_kernel(
    rows,
    rows_out,
    sizes,
    occ,
    pair,
    j_irrep,
    owner_row,
    label_row,
    label_k,
    slots,
    kinds,
    label_kept,
    label_out,
    keys,
):
    here = lax.axis_index("vir")
    occupied, lanes = label_k.shape
    virtuals = owner_row.shape[1] * BS
    target = virtual_place(block_place(owner_row[...], rows), virtuals)
    lane = iota((virtuals, lanes), 1)
    source = jnp.where(lane < rows, lane + here * rows, lane - rows + (here ^ 1) * rows)
    virtual = iota((virtuals, lanes), 0)
    e_row = jnp.sum(jnp.where(target == source, virtual + 1, 0), axis=0, keepdims=True) - 1
    label = irrep_of(e_row, sizes)
    label_row[...] = label[:, :rows]
    m_row = iota((occupied, 1), 0)
    wanted = jnp.zeros((occupied, 1), I32)
    for m in range(occupied):
        wanted = jnp.where(m_row == m, pair[0] ^ occ[m], wanted)
    partner = label ^ wanted
    label_k[...] = partner
    first, second = iota((lanes, lanes), 0), iota((lanes, lanes), 1)
    e_col = jnp.sum(jnp.where(first == second, e_row, 0), axis=1, keepdims=True)
    ahead = (e_col >= 0) & (e_col % BS == 0) & (e_col // BS < e_row // BS)
    wide = jnp.where(e_row >= 0, wide_block(jnp.maximum(e_row, 0) // BS, wanted, sizes), 0)
    rank_wide = jnp.dot(
        wide.astype(F32).astype(BF16),
        jnp.where(ahead, 1.0, 0.0).astype(BF16),
        preferred_element_type=F32,
    ).astype(I32)
    rank = jnp.sum(ahead.astype(I32), axis=0, keepdims=True)
    count_wide = jnp.sum(wide, axis=1, keepdims=True) // BS
    slot, kind = slots_of(wide, rank, rank_wide, count_wide)
    slots[...] = jnp.where(e_row >= 0, slot * BS + e_row % BS, -1)
    kinds[...] = kind
    row = iota(label_kept.shape, 0)
    a = row // rows_out * (2 * rows_out) + here % 2 * rows_out + row % rows_out
    label_kept[...] = irrep_of(a, sizes)
    label_out[...] = irrep_of(iota(label_out.shape, 0) + here * rows_out, sizes) ^ pair[0]
    keys[...] = jnp.broadcast_to(column_keys(keys.shape[1], sizes, j_irrep), keys.shape)


def fold_kernel(first, occ, label_row, keys, w, out, folded):
    step, part = pl.program_id(0), pl.program_id(1)
    row_block, m_block, columns = w.shape
    wide = out.shape[2]
    m_row = iota((m_block, 1), 0)
    occ_col = jnp.zeros((m_block, 1), I32)
    for i in range(m_block):
        occ_col = jnp.where(m_row == i, occ[part * m_block + i], occ_col)

    @pl.loop(0, row_block // 4)
    def _(quad):
        for i in range(4):
            row = quad * 4 + i
            label = label_row[first + step * row_block + row]
            allowed = (occ_col ^ label) == keys[:1, :]
            kept = jnp.where(allowed, w[row].astype(F32), 0.0)
            total = kept[:, :wide]
            for k in range(1, columns // wide):
                total = total + kept[:, k * wide : (k + 1) * wide]
            here = pl.ds(pl.multiple_of(row * m_block, m_block), m_block)
            for k in range(wide // 128):
                folded[k, here, :] = total[:, k * 128 : (k + 1) * 128]

    for i in range(m_block):
        for k in range(wide // 128):
            out[i, :, k * 128 : (k + 1) * 128] = folded[
                k, pl.ds(i, row_block, stride=m_block), :
            ].astype(BF16)


def product_kernel(pieces, label_k, slots, kinds, label_kept, packed, *refs):
    own, mate_hbm = refs[:pieces], refs[pieces : 2 * pieces]
    coded, out, t, mate, sems = refs[2 * pieces :]
    occupied, half, lanes = t.shape
    rows = lanes // 2
    kept = out.shape[0]
    size = rows // pieces
    copies = [
        pltpu.make_async_copy(mate_hbm[i], mate.at[:, i * size : (i + 1) * size], sems.at[i])
        for i in range(pieces)
    ]
    for copy in copies:
        copy.start()
    slot = iota((packed.shape[1], 1), 0)
    unpacked = max(1, min(occupied, 8))

    @pl.loop(0, occupied // unpacked)
    def _(step):
        for i in range(unpacked):
            m = step * unpacked + i
            hot = jnp.where(slots[pl.ds(m, 1), :] == slot, 1.0, 0.0).astype(BF16)
            both = lax.dot_general(
                packed[m], hot, (((0,), (0,)), ((), ())), preferred_element_type=F32
            )
            low, high = both[: half // 2], both[half // 2 :]
            kind = kinds[pl.ds(m, 1), :]
            t[m] = jnp.concatenate(
                [jnp.where(kind == 2, high, low), jnp.where(kind == 1, low, high)], axis=0
            ).astype(BF16)

    wide_label = jnp.broadcast_to(label_kept[:, :1], (kept, rows))

    def expand(m, side):
        lane = slice(side * rows, (side + 1) * rows)
        wanted = label_k[pl.ds(m, 1), :][:, lane]
        values = t[m][:, lane].astype(F32)
        return jnp.concatenate(
            [
                jnp.where(wide_label[k : k + half] == wanted, values, 0.0).astype(BF16)
                for k in range(0, kept, half)
            ],
            axis=0,
        )

    def couplings(m, side):
        return mate[m] if side else jnp.concatenate([piece[m] for piece in own], axis=0)

    def arrived(side):
        for copy in copies if side else ():
            copy.wait()

    if rows % 128 == 0:
        for side in range(2):
            arrived(side)
            left = jnp.concatenate([expand(m, side) for m in range(occupied)], axis=1)
            right = jnp.concatenate([couplings(m, side) for m in range(occupied)], axis=0)
            total = jnp.dot(left, right, preferred_element_type=F32)
            out[...] = out[...] + total if side else total
    else:
        arrived(1)
        out[...] = jnp.zeros(out.shape, F32)

        @pl.loop(0, occupied)
        def _(m):
            for side in range(2):
                out[...] += jnp.dot(
                    expand(m, side), couplings(m, side), preferred_element_type=F32
                )

    rows_out = kept // coded.shape[0]
    for chip in range(coded.shape[0]):
        coded[chip] = encode(out[chip * rows_out : (chip + 1) * rows_out, :])


def encode(values):
    row = iota((PAD, 128), 0)
    scales = jnp.zeros((PAD, 128), I32)
    blocks = []
    for i in range(values.shape[1] // 128):
        part = values[:, i * 128 : (i + 1) * 128]
        largest = jnp.maximum(jnp.max(jnp.abs(part), axis=0, keepdims=True), SMALL)
        scale = jnp.floor(jnp.log2(largest) * STEPS) + 2.0
        factor = jnp.exp2(scale * (-0.5 / STEPS))
        blocks.append(jnp.floor(part * factor * (factor * TOP) + 0.5).astype(I32))
        scales = jnp.where(row == i, scale.astype(I32), scales)
    return jnp.concatenate(blocks + [scales], axis=0).astype(I16)


def decode(coded, rows_out):
    values = coded.astype(I32)
    blocks = []
    for i in range((coded.shape[0] - PAD) // rows_out):
        scale = values[coded.shape[0] - PAD + i :][:1].astype(F32)
        factor = jnp.exp2(scale * (0.5 / STEPS))
        part = values[i * rows_out : (i + 1) * rows_out].astype(F32)
        blocks.append(part * (factor * (1.0 / TOP)) * factor)
    return blocks


def finish_kernel(label_out, keys, parts, out):
    chips = parts.shape[0]
    rows_out = out.shape[0]
    total = decode(parts[0], rows_out)
    for q in range(1, chips):
        total = [x + y for x, y in zip(total, decode(parts[q], rows_out))]
    total = jnp.concatenate(total, axis=1)
    wide = total.shape[1]
    for k in range(0, out.shape[1], wide):
        out[:, k : k + wide] = jnp.where(
            label_out[:, :1] == keys[:1, k : k + wide], total, 0.0
        )


in_hbm = functools.partial(pltpu.with_memory_space_constraint, memory_space=pltpu.HBM)
in_vmem = functools.partial(pltpu.with_memory_space_constraint, memory_space=pltpu.VMEM)


def per_device(amplitudes, couplings, occ_irrep, pair_irrep, j_irrep, block_sizes, owner):
    devices = lax.axis_size("vir")
    chips = devices // 2
    virtuals = amplitudes.shape[2]
    rows, occupied, columns = couplings.shape
    wide = columns // virtuals * MOST
    rows_out = virtuals // devices
    kept = virtuals // 2
    lanes = 2 * rows
    blocks = owner.shape[0]
    smem = pl.BlockSpec(memory_space=pltpu.SMEM)
    vmem = pl.BlockSpec(memory_space=pltpu.VMEM)
    hbm = pl.BlockSpec(memory_space=pltpu.HBM)
    params = pltpu.CompilerParams(vmem_limit_bytes=LIMIT)

    classes = [lanes]
    if lanes % 256 == 0:
        classes = [lanes // 16 * part for part in (11, 12, 13, 14, 16)]
    owner_row = owner.reshape(1, blocks)
    *outgoing, choice = pl.pallas_call(
        functools.partial(pack_kernel, rows_out, classes),
        out_shape=[jax.ShapeDtypeStruct((devices, size, HALF), BF16) for size in classes]
        + [jax.ShapeDtypeStruct((1,), I32)],
        in_specs=[hbm, hbm, smem, hbm, hbm],
        out_specs=[hbm] * len(classes) + [smem],
        scratch_shapes=[
            pltpu.SMEM(block_sizes.shape, I32),
            pltpu.SMEM(occ_irrep.shape, I32),
            pltpu.VMEM((1, blocks), I32),
            pltpu.VMEM((virtuals, virtuals), BF16),
            pltpu.VMEM((2, virtuals, HALF), F32),
            pltpu.VMEM((2, virtuals + chips * ALIGN, HALF), F32),
            pltpu.VMEM((2, virtuals + chips * ALIGN + lanes, HALF), BF16),
            pltpu.SemaphoreType.DMA((4,)),
            pltpu.SemaphoreType.DMA((devices,)),
        ],
        compiler_params=params,
        name="pack_amplitudes",
    )(
        in_hbm(block_sizes),
        in_hbm(occ_irrep),
        pair_irrep,
        in_hbm(owner_row),
        in_hbm(amplitudes),
    )

    def contract(packed):
        received = lax.all_to_all(packed, "vir", 0, 0)

        label_row, label_k, slots, kinds, label_kept, label_out, keys = pl.pallas_call(
            functools.partial(label_kernel, rows, rows_out),
            out_shape=(
                jax.ShapeDtypeStruct((1, rows), I32),
                jax.ShapeDtypeStruct((occupied, lanes), I32),
                jax.ShapeDtypeStruct((occupied, lanes), I32),
                jax.ShapeDtypeStruct((occupied, lanes), I32),
                jax.ShapeDtypeStruct((kept, 128), I32),
                jax.ShapeDtypeStruct((rows_out, 128), I32),
                jax.ShapeDtypeStruct((8, columns), I32),
            ),
            in_specs=[smem] * 4 + [vmem],
            out_specs=(vmem,) * 7,
            compiler_params=params,
            name="labels",
        )(block_sizes, occ_irrep, pair_irrep, j_irrep, owner_row)

        row_block, m_block = 16, 16
        pieces = max(1, rows // 32)
        piece_rows = rows // pieces
        w_own, w_mate = [], []
        for piece in range(pieces):
            first = piece * piece_rows
            w_own.append(
                pl.pallas_call(
                    functools.partial(fold_kernel, first),
                    out_shape=jax.ShapeDtypeStruct((occupied, piece_rows, wide), BF16),
                    grid=(piece_rows // row_block, occupied // m_block),
                    in_specs=[smem, smem, vmem]
                    + [
                        pl.BlockSpec(
                            (row_block, m_block, columns),
                            lambda i, j, skip=first // row_block: (skip + i, j, 0),
                        )
                    ],
                    out_specs=pl.BlockSpec((m_block, row_block, wide), lambda i, j: (j, i, 0)),
                    scratch_shapes=[pltpu.VMEM((wide // 128, row_block * m_block, 128), F32)],
                    compiler_params=params,
                    cost_estimate=pl.CostEstimate(
                        flops=4 * piece_rows * occupied * columns,
                        bytes_accessed=3 * piece_rows * occupied * columns,
                        transcendentals=0,
                    ),
                    name="fold_couplings",
                )(occ_irrep, label_row.reshape(rows), keys, in_hbm(couplings))
            )
            w_mate.append(lax.ppermute(w_own[-1], "vir", [(d, d ^ 1) for d in range(devices)]))

        partial = pl.pallas_call(
            functools.partial(product_kernel, pieces),
            out_shape=jax.ShapeDtypeStruct((chips, wide // 128 * rows_out + PAD, 128), I16),
            in_specs=[vmem] * (5 + pieces) + [hbm] * pieces,
            out_specs=vmem,
            scratch_shapes=[
                pltpu.VMEM((kept, wide), F32),
                pltpu.VMEM((occupied, HALF, lanes), BF16),
                pltpu.VMEM((occupied, rows, wide), BF16),
                pltpu.SemaphoreType.DMA((pieces,)),
            ],
            compiler_params=params,
            name="multiply",
        )(
            *[in_vmem(x) for x in (label_k, slots, kinds, label_kept, received, *w_own)],
            *[in_hbm(x) for x in w_mate],
        )
        sides = [[d for d in range(devices) if d % 2 == core] for core in (0, 1)]
        parts = lax.all_to_all(partial, "vir", 0, 0, axis_index_groups=sides)
        return pl.pallas_call(
            finish_kernel,
            out_shape=pltpu.HBM((rows_out, columns), F32),
            in_specs=[vmem] * 3,
            out_specs=vmem,
            compiler_params=params,
            name="unfold",
        )(label_out, keys, parts)

    if len(classes) == 1:
        return contract(outgoing[0])
    branches = [lambda *packed, k=k: contract(packed[k]) for k in range(len(classes))]
    return lax.switch(choice[0], branches, *outgoing)


def solution(mesh):
    return jax.shard_map(
        per_device,
        mesh=mesh,
        in_specs=(
            P(("grp", "vir"), None, None),
            P(("grp", "vir"), None, None),
            P("grp"),
            P(),
            P(),
            P("grp"),
            P("grp", None),
        ),
        out_specs=P(("grp", "vir"), None),
        check_vma=False,
    )
```

```python
import functools

import jax
import jax.numpy as jnp
from jax import lax
from jax.experimental import pallas as pl
from jax.experimental.pallas import tpu as pltpu
from jax.sharding import PartitionSpec as P

BS = 4
MOST = 256
LIMIT = 24 * 1024 * 1024
F32, BF16, I32, I16 = jnp.float32, jnp.bfloat16, jnp.int32, jnp.int16
TOP = 32767.0
STEPS = 256.0
SMALL = 2.0**-126
HALF = MOST // 2
ALIGN = 16
PAD = 16


def irrep_of(index, sizes):
    label = jnp.zeros_like(index)
    end = jnp.int32(0)
    for h in range(sizes.shape[0] - 1):
        end = end + sizes[h]
        label = jnp.where(index >= end, h + 1, label)
    return label


def iota(shape, dim):
    return lax.broadcasted_iota(I32, shape, dim)


def column_keys(columns, sizes, j_irrep):
    count = j_irrep.shape[0]
    column = iota((1, columns), 1)
    j = column % count
    j_label = jnp.zeros_like(column)
    for i in range(count):
        j_label = jnp.where(j == i, j_irrep[i], j_label)
    return irrep_of(column // count, sizes) ^ j_label


def block_place(owner_row, rows):
    blocks = owner_row.shape[1]
    first, second = iota((blocks, blocks), 0), iota((blocks, blocks), 1)
    owner_col = jnp.sum(jnp.where(first == second, owner_row, 0), axis=1, keepdims=True)
    earlier = (owner_col == owner_row) & (first < second)
    rank = jnp.sum(earlier.astype(I32), axis=0, keepdims=True)
    return owner_row * rows + rank * BS


def virtual_place(place, virtuals):
    blocks = place.shape[1]
    e, block = iota((virtuals, blocks), 0), iota((virtuals, blocks), 1)
    start = jnp.sum(jnp.where(e // BS == block, place, 0), axis=1, keepdims=True)
    return start + iota((virtuals, 1), 0) % BS


def wide_flags(partner, sizes):
    wide = jnp.zeros_like(partner)
    for h in range(sizes.shape[0]):
        wide = jnp.where(partner == h, (sizes[h] > HALF).astype(I32), wide)
    return wide


def wide_block(block, wanted, sizes):
    wide = jnp.zeros_like(block ^ wanted)
    for r in range(BS):
        wide = wide | wide_flags(irrep_of(block * BS + r, sizes) ^ wanted, sizes)
    return wide


def slots_needed(wide, owned):
    return wide + (owned - wide + 1) // 2


def slots_of(wide, rank, rank_wide, count_wide):
    rank_narrow = rank - rank_wide
    slot = jnp.where(wide == 1, rank_wide, count_wide + rank_narrow // 2)
    return slot, jnp.where(wide == 1, 0, 1 + rank_narrow % 2)


def pack_kernel(
    rows_out,
    classes,
    sizes_hbm,
    occ_hbm,
    pair,
    owner_hbm,
    t_hbm,
    *refs,
):
    outs, choice = refs[: len(classes)], refs[len(classes)]
    sizes, occ, owner_row, t_vmem, folds, filled, out, in_sems, out_sems = refs[len(classes) + 1 :]
    virtuals = t_hbm.shape[1]
    blocks = owner_row.shape[1]
    chips = outs[0].shape[0] // 2
    quarter = HALF // 2
    pairs = (
        (owner_hbm, owner_row),
        (sizes_hbm, sizes),
        (occ_hbm, occ),
        (t_hbm.at[0], t_vmem),
    )
    copies = [
        pltpu.make_async_copy(source, here, in_sems.at[i])
        for i, (source, here) in enumerate(pairs)
    ]
    for copy in copies:
        copy.start()
    copies[0].wait()
    chip_row = owner_row[...] // 2
    first, second = iota((blocks, blocks), 0), iota((blocks, blocks), 1)
    chip_col = jnp.sum(jnp.where(first == second, chip_row, 0), axis=1, keepdims=True)
    same = chip_col == chip_row
    before = jnp.where(same & (first < second), 1.0, 0.0).astype(BF16)
    same = jnp.where(same, 1.0, 0.0).astype(BF16)
    for copy in copies[1:3]:
        copy.wait()
    wanted = pair[0] ^ occ[lax.axis_index("vir")]
    row = iota((8, blocks), 0)
    wide_all = wide_block(iota((1, blocks), 1), row, sizes)
    own = jnp.sum(jnp.where(row == wanted, wide_all, 0), axis=0, keepdims=True)
    rest = jnp.where(row == 0, own, jnp.where(row == 1, 1, 0))
    tallies = jnp.concatenate([wide_all, rest], axis=0).astype(F32).astype(BF16)
    ahead = jnp.dot(tallies, before, preferred_element_type=F32).astype(I32)
    total = jnp.dot(tallies, same, preferred_element_type=F32).astype(I32)
    owned = total[9:10]

    index = jnp.int32(0)
    if len(classes) > 1:
        used = jnp.int32(0)
        for m in range(occ.shape[0]):
            used = used | (jnp.int32(1) << (pair[0] ^ occ[m]))
        need = slots_needed(total[:8], owned) * ((used >> row) & 1)
        need = jnp.max(need) * BS
        for size in classes[:-1]:
            index = index + (need > size).astype(I32)
    choice[0] = index

    step = ALIGN // BS
    chip = iota((chips, 1), 0)
    lengths = jnp.where(chip == chip_row, slots_needed(total[8:9], owned), 0)
    lengths = (jnp.max(lengths, axis=1, keepdims=True) + (step - 1)) // step
    starts_row = jnp.sum(jnp.where(chip < chip_row, lengths, 0), axis=0, keepdims=True)
    starts = [jnp.sum(jnp.where(chip < q, lengths, 0)) for q in range(chips)]
    slot, kind = slots_of(own, ahead[9:10], ahead[8:9], total[8:9])
    place = starts_row * step + slot
    targets = [jnp.where(kind == 2, -1, place), jnp.where(kind == 1, -1, place)]

    partner = irrep_of(iota((virtuals, 1), 0), sizes) ^ wanted
    partner = jnp.broadcast_to(partner, (virtuals, HALF)).astype(I16)
    label_a = irrep_of(iota((1, virtuals), 1), sizes).astype(I16)
    copies[3].wait()
    halves = [jnp.zeros((virtuals, HALF), BF16) for _ in range(2)]
    for i, k in enumerate(range(0, virtuals, HALF)):
        here = partner == label_a[:, k : k + HALF]
        kept = jnp.where(here, t_vmem[:, k : k + HALF], jnp.zeros((), BF16))
        halves[i % 2] = halves[i % 2] + kept
    for h in range(2):
        folds[h] = halves[h].astype(F32)
    first, second = iota((blocks, blocks), 0), iota((blocks, blocks), 1)
    narrow = jnp.sum(jnp.where(first == second, own, 0), axis=1, keepdims=True) == 0
    blank = jnp.zeros((blocks, quarter), F32)
    sources = [[[], []], [[], []]]
    for r in range(BS):
        both = [folds[h, pl.ds(r, blocks, stride=BS), :] for h in range(2)]
        for h in range(2):
            source = both[h] + jnp.where(narrow, both[1 - h], 0.0)
            if rows_out < quarter:
                old, new = iota((HALF, HALF), 0), iota((HALF, HALF), 1)
                core, x = new // quarter, new % quarter
                lane = x // rows_out * (2 * rows_out) + core * rows_out + x % rows_out
                order = jnp.where(old == lane, 1.0, 0.0).astype(BF16)
                source = jnp.dot(source.astype(BF16), order, preferred_element_type=F32)
            for core in range(2):
                side = source[:, core * quarter : (core + 1) * quarter]
                sources[core][h] += [blank, side] if h else [side, blank]
    count = filled.shape[1] // BS
    slot = iota((count, 1), 0)
    hot = jnp.concatenate([jnp.where(x == slot, 1.0, 0.0) for x in targets], axis=1).astype(BF16)

    def send(k, device):
        start = pl.multiple_of(starts[device // 2] * ALIGN, ALIGN)
        return pltpu.make_async_copy(
            out.at[device % 2, pl.ds(start, classes[k])],
            outs[k].at[device],
            out_sems.at[device],
        )

    def each(core, act):
        for k in range(len(classes)):

            @pl.when(index == k)
            def _(k=k):
                for device in range(core, 2 * chips, 2):
                    act(send(k, device))

    for core in range(2):
        source = [jnp.concatenate(x, axis=1) for x in sources[core]]
        source = jnp.concatenate(source, axis=0).astype(BF16)
        moved = jnp.dot(hot, source, preferred_element_type=F32)
        for r in range(BS):
            part = slice(r * HALF, (r + 1) * HALF)
            filled[core, pl.ds(r, count, stride=BS), :] = moved[:, part]
        out[core, : filled.shape[1]] = filled[core].astype(BF16)
        rest = out.shape[1] - filled.shape[1]
        out[core, filled.shape[1] :] = jnp.zeros((rest, HALF), BF16)
        each(core, lambda copy: copy.start())
    for core in range(2):
        each(core, lambda copy: copy.wait())


def label_kernel(
    rows,
    rows_out,
    sizes,
    occ,
    pair,
    j_irrep,
    owner_row,
    label_row,
    label_k,
    slots,
    kinds,
    label_kept,
    label_out,
    keys,
):
    here = lax.axis_index("vir")
    occupied, lanes = label_k.shape
    virtuals = owner_row.shape[1] * BS
    target = virtual_place(block_place(owner_row[...], rows), virtuals)
    lane = iota((virtuals, lanes), 1)
    source = jnp.where(lane < rows, lane + here * rows, lane - rows + (here ^ 1) * rows)
    virtual = iota((virtuals, lanes), 0)
    e_row = jnp.sum(jnp.where(target == source, virtual + 1, 0), axis=0, keepdims=True) - 1
    label = irrep_of(e_row, sizes)
    label_row[...] = label[:, :rows]
    m_row = iota((occupied, 1), 0)
    wanted = jnp.zeros((occupied, 1), I32)
    for m in range(occupied):
        wanted = jnp.where(m_row == m, pair[0] ^ occ[m], wanted)
    partner = label ^ wanted
    label_k[...] = partner
    first, second = iota((lanes, lanes), 0), iota((lanes, lanes), 1)
    e_col = jnp.sum(jnp.where(first == second, e_row, 0), axis=1, keepdims=True)
    ahead = (e_col >= 0) & (e_col % BS == 0) & (e_col // BS < e_row // BS)
    wide = jnp.where(e_row >= 0, wide_block(jnp.maximum(e_row, 0) // BS, wanted, sizes), 0)
    rank_wide = jnp.dot(
        wide.astype(F32).astype(BF16),
        jnp.where(ahead, 1.0, 0.0).astype(BF16),
        preferred_element_type=F32,
    ).astype(I32)
    rank = jnp.sum(ahead.astype(I32), axis=0, keepdims=True)
    count_wide = jnp.sum(wide, axis=1, keepdims=True) // BS
    slot, kind = slots_of(wide, rank, rank_wide, count_wide)
    slots[...] = jnp.where(e_row >= 0, slot * BS + e_row % BS, -1)
    kinds[...] = kind
    row = iota(label_kept.shape, 0)
    a = row // rows_out * (2 * rows_out) + here % 2 * rows_out + row % rows_out
    label_kept[...] = irrep_of(a, sizes)
    label_out[...] = irrep_of(iota(label_out.shape, 0) + here * rows_out, sizes) ^ pair[0]
    keys[...] = jnp.broadcast_to(column_keys(keys.shape[1], sizes, j_irrep), keys.shape)


def fold_kernel(first, occ, label_row, keys, w, out, folded):
    step, part = pl.program_id(0), pl.program_id(1)
    row_block, m_block, columns = w.shape
    wide = out.shape[2]
    m_row = iota((m_block, 1), 0)
    occ_col = jnp.zeros((m_block, 1), I32)
    for i in range(m_block):
        occ_col = jnp.where(m_row == i, occ[part * m_block + i], occ_col)

    @pl.loop(0, row_block // 4)
    def _(quad):
        for i in range(4):
            row = quad * 4 + i
            label = label_row[first + step * row_block + row]
            allowed = (occ_col ^ label) == keys[:1, :]
            kept = jnp.where(allowed, w[row].astype(F32), 0.0)
            total = kept[:, :wide]
            for k in range(1, columns // wide):
                total = total + kept[:, k * wide : (k + 1) * wide]
            here = pl.ds(pl.multiple_of(row * m_block, m_block), m_block)
            for k in range(wide // 128):
                folded[k, here, :] = total[:, k * 128 : (k + 1) * 128]

    for i in range(m_block):
        for k in range(wide // 128):
            out[i, :, k * 128 : (k + 1) * 128] = folded[
                k, pl.ds(i, row_block, stride=m_block), :
            ].astype(BF16)


def product_kernel(pieces, label_k, slots, kinds, label_kept, packed, *refs):
    own, mate_hbm = refs[:pieces], refs[pieces : 2 * pieces]
    coded, out, t, mate, sems = refs[2 * pieces :]
    occupied, half, lanes = t.shape
    rows = lanes // 2
    kept = out.shape[0]
    size = rows // pieces
    copies = [
        pltpu.make_async_copy(mate_hbm[i], mate.at[:, i * size : (i + 1) * size], sems.at[i])
        for i in range(pieces)
    ]
    for copy in copies:
        copy.start()
    slot = iota((packed.shape[1], 1), 0)
    unpacked = max(1, min(occupied, 8))

    @pl.loop(0, occupied // unpacked)
    def _(step):
        for i in range(unpacked):
            m = step * unpacked + i
            hot = jnp.where(slots[pl.ds(m, 1), :] == slot, 1.0, 0.0).astype(BF16)
            both = lax.dot_general(
                packed[m], hot, (((0,), (0,)), ((), ())), preferred_element_type=F32
            )
            low, high = both[: half // 2], both[half // 2 :]
            kind = kinds[pl.ds(m, 1), :]
            t[m] = jnp.concatenate(
                [jnp.where(kind == 2, high, low), jnp.where(kind == 1, low, high)], axis=0
            ).astype(BF16)

    wide_label = jnp.broadcast_to(label_kept[:, :1], (kept, rows))

    def expand(m, side):
        lane = slice(side * rows, (side + 1) * rows)
        wanted = label_k[pl.ds(m, 1), :][:, lane]
        values = t[m][:, lane].astype(F32)
        return jnp.concatenate(
            [
                jnp.where(wide_label[k : k + half] == wanted, values, 0.0).astype(BF16)
                for k in range(0, kept, half)
            ],
            axis=0,
        )

    def couplings(m, side):
        return mate[m] if side else jnp.concatenate([piece[m] for piece in own], axis=0)

    def arrived(side):
        for copy in copies if side else ():
            copy.wait()

    if rows % 128 == 0:
        for side in range(2):
            arrived(side)
            left = jnp.concatenate([expand(m, side) for m in range(occupied)], axis=1)
            right = jnp.concatenate([couplings(m, side) for m in range(occupied)], axis=0)
            total = jnp.dot(left, right, preferred_element_type=F32)
            out[...] = out[...] + total if side else total
    else:
        arrived(1)
        out[...] = jnp.zeros(out.shape, F32)

        @pl.loop(0, occupied)
        def _(m):
            for side in range(2):
                out[...] += jnp.dot(
                    expand(m, side), couplings(m, side), preferred_element_type=F32
                )

    rows_out = kept // coded.shape[0]
    for chip in range(coded.shape[0]):
        coded[chip] = encode(out[chip * rows_out : (chip + 1) * rows_out, :])


def encode(values):
    row = iota((PAD, 128), 0)
    scales = jnp.zeros((PAD, 128), I32)
    blocks = []
    for i in range(values.shape[1] // 128):
        part = values[:, i * 128 : (i + 1) * 128]
        largest = jnp.maximum(jnp.max(jnp.abs(part), axis=0, keepdims=True), SMALL)
        scale = jnp.floor(jnp.log2(largest) * STEPS) + 2.0
        factor = jnp.exp2(scale * (-0.5 / STEPS))
        blocks.append(jnp.floor(part * factor * (factor * TOP) + 0.5).astype(I32))
        scales = jnp.where(row == i, scale.astype(I32), scales)
    return jnp.concatenate(blocks + [scales], axis=0).astype(I16)


def decode(coded, rows_out):
    values = coded.astype(I32)
    blocks = []
    for i in range((coded.shape[0] - PAD) // rows_out):
        scale = values[coded.shape[0] - PAD + i :][:1].astype(F32)
        factor = jnp.exp2(scale * (0.5 / STEPS))
        part = values[i * rows_out : (i + 1) * rows_out].astype(F32)
        blocks.append(part * (factor * (1.0 / TOP)) * factor)
    return blocks


def finish_kernel(label_out, keys, parts, out):
    chips = parts.shape[0]
    rows_out = out.shape[0]
    total = decode(parts[0], rows_out)
    for q in range(1, chips):
        total = [x + y for x, y in zip(total, decode(parts[q], rows_out))]
    total = jnp.concatenate(total, axis=1)
    wide = total.shape[1]
    for k in range(0, out.shape[1], wide):
        out[:, k : k + wide] = jnp.where(
            label_out[:, :1] == keys[:1, k : k + wide], total, 0.0
        )


in_hbm = functools.partial(pltpu.with_memory_space_constraint, memory_space=pltpu.HBM)
in_vmem = functools.partial(pltpu.with_memory_space_constraint, memory_space=pltpu.VMEM)


def per_device(amplitudes, couplings, occ_irrep, pair_irrep, j_irrep, block_sizes, owner):
    devices = lax.axis_size("vir")
    chips = devices // 2
    virtuals = amplitudes.shape[2]
    rows, occupied, columns = couplings.shape
    wide = columns // virtuals * MOST
    rows_out = virtuals // devices
    kept = virtuals // 2
    lanes = 2 * rows
    blocks = owner.shape[0]
    smem = pl.BlockSpec(memory_space=pltpu.SMEM)
    vmem = pl.BlockSpec(memory_space=pltpu.VMEM)
    hbm = pl.BlockSpec(memory_space=pltpu.HBM)
    params = pltpu.CompilerParams(vmem_limit_bytes=LIMIT)

    classes = [lanes]
    if lanes % 256 == 0:
        classes = [lanes // 16 * part for part in (11, 12, 13, 14, 16)]
    owner_row = owner.reshape(1, blocks)
    *outgoing, choice = pl.pallas_call(
        functools.partial(pack_kernel, rows_out, classes),
        out_shape=[jax.ShapeDtypeStruct((devices, size, HALF), BF16) for size in classes]
        + [pltpu.SMEM((1,), I32)],
        in_specs=[hbm, hbm, smem, hbm, hbm],
        out_specs=[hbm] * len(classes) + [smem],
        scratch_shapes=[
            pltpu.SMEM(block_sizes.shape, I32),
            pltpu.SMEM(occ_irrep.shape, I32),
            pltpu.VMEM((1, blocks), I32),
            pltpu.VMEM((virtuals, virtuals), BF16),
            pltpu.VMEM((2, virtuals, HALF), F32),
            pltpu.VMEM((2, virtuals + chips * ALIGN, HALF), F32),
            pltpu.VMEM((2, virtuals + chips * ALIGN + lanes, HALF), BF16),
            pltpu.SemaphoreType.DMA((4,)),
            pltpu.SemaphoreType.DMA((devices,)),
        ],
        compiler_params=params,
        name="pack_amplitudes",
    )(
        in_hbm(block_sizes),
        in_hbm(occ_irrep),
        pair_irrep,
        in_hbm(owner_row),
        in_hbm(amplitudes),
    )

    def contract(packed):
        received = lax.all_to_all(packed, "vir", 0, 0)

        label_row, label_k, slots, kinds, label_kept, label_out, keys = pl.pallas_call(
            functools.partial(label_kernel, rows, rows_out),
            out_shape=(
                jax.ShapeDtypeStruct((1, rows), I32),
                jax.ShapeDtypeStruct((occupied, lanes), I32),
                jax.ShapeDtypeStruct((occupied, lanes), I32),
                jax.ShapeDtypeStruct((occupied, lanes), I32),
                jax.ShapeDtypeStruct((kept, 128), I32),
                jax.ShapeDtypeStruct((rows_out, 128), I32),
                jax.ShapeDtypeStruct((8, columns), I32),
            ),
            in_specs=[smem] * 4 + [vmem],
            out_specs=(vmem,) * 7,
            compiler_params=params,
            name="labels",
        )(block_sizes, occ_irrep, pair_irrep, j_irrep, owner_row)

        row_block, m_block = 16, 16
        pieces = max(1, rows // 32)
        piece_rows = rows // pieces
        w_own, w_mate = [], []
        for piece in range(pieces):
            first = piece * piece_rows
            w_own.append(
                pl.pallas_call(
                    functools.partial(fold_kernel, first),
                    out_shape=jax.ShapeDtypeStruct((occupied, piece_rows, wide), BF16),
                    grid=(piece_rows // row_block, occupied // m_block),
                    in_specs=[smem, smem, vmem]
                    + [
                        pl.BlockSpec(
                            (row_block, m_block, columns),
                            lambda i, j, skip=first // row_block: (skip + i, j, 0),
                        )
                    ],
                    out_specs=pl.BlockSpec((m_block, row_block, wide), lambda i, j: (j, i, 0)),
                    scratch_shapes=[pltpu.VMEM((wide // 128, row_block * m_block, 128), F32)],
                    compiler_params=params,
                    cost_estimate=pl.CostEstimate(
                        flops=4 * piece_rows * occupied * columns,
                        bytes_accessed=3 * piece_rows * occupied * columns,
                        transcendentals=0,
                    ),
                    name="fold_couplings",
                )(occ_irrep, label_row.reshape(rows), keys, in_hbm(couplings))
            )
            w_mate.append(lax.ppermute(w_own[-1], "vir", [(d, d ^ 1) for d in range(devices)]))

        partial = pl.pallas_call(
            functools.partial(product_kernel, pieces),
            out_shape=jax.ShapeDtypeStruct((chips, wide // 128 * rows_out + PAD, 128), I16),
            in_specs=[vmem] * (5 + pieces) + [hbm] * pieces,
            out_specs=vmem,
            scratch_shapes=[
                pltpu.VMEM((kept, wide), F32),
                pltpu.VMEM((occupied, HALF, lanes), BF16),
                pltpu.VMEM((occupied, rows, wide), BF16),
                pltpu.SemaphoreType.DMA((pieces,)),
            ],
            compiler_params=params,
            name="multiply",
        )(
            *[in_vmem(x) for x in (label_k, slots, kinds, label_kept, received, *w_own)],
            *[in_hbm(x) for x in w_mate],
        )
        sides = [[d for d in range(devices) if d % 2 == core] for core in (0, 1)]
        parts = lax.all_to_all(partial, "vir", 0, 0, axis_index_groups=sides)
        return pl.pallas_call(
            finish_kernel,
            out_shape=pltpu.HBM((rows_out, columns), F32),
            in_specs=[vmem] * 3,
            out_specs=vmem,
            compiler_params=params,
            name="unfold",
        )(label_out, keys, parts)

    if len(classes) == 1:
        return contract(outgoing[0])
    branches = [lambda *packed, k=k: contract(packed[k]) for k in range(len(classes))]
    return lax.switch(choice[0], branches, *outgoing)


def solution(mesh):
    return jax.shard_map(
        per_device,
        mesh=mesh,
        in_specs=(
            P(("grp", "vir"), None, None),
            P(("grp", "vir"), None, None),
            P("grp"),
            P(),
            P(),
            P("grp"),
            P("grp", None),
        ),
        out_specs=P(("grp", "vir"), None),
        check_vma=False,
    )
```

```python
import functools

import jax
import jax.numpy as jnp
from jax import lax
from jax.experimental import pallas as pl
from jax.experimental.pallas import tpu as pltpu
from jax.sharding import PartitionSpec as P

BS = 4
MOST = 256
LIMIT = 24 * 1024 * 1024
F32, BF16, I32, I16 = jnp.float32, jnp.bfloat16, jnp.int32, jnp.int16
TOP = 32767.0
STEPS = 256.0
SMALL = 2.0**-126
HALF = MOST // 2
ALIGN = 16
PAD = 8


def irrep_of(index, sizes):
    label = jnp.zeros_like(index)
    end = jnp.int32(0)
    for h in range(sizes.shape[0] - 1):
        end = end + sizes[h]
        label = jnp.where(index >= end, h + 1, label)
    return label


def iota(shape, dim):
    return lax.broadcasted_iota(I32, shape, dim)


def column_keys(columns, sizes, j_irrep):
    count = j_irrep.shape[0]
    column = iota((1, columns), 1)
    j = column % count
    j_label = jnp.zeros_like(column)
    for i in range(count):
        j_label = jnp.where(j == i, j_irrep[i], j_label)
    return irrep_of(column // count, sizes) ^ j_label


def block_place(owner_row, rows):
    blocks = owner_row.shape[1]
    first, second = iota((blocks, blocks), 0), iota((blocks, blocks), 1)
    owner_col = jnp.sum(jnp.where(first == second, owner_row, 0), axis=1, keepdims=True)
    earlier = (owner_col == owner_row) & (first < second)
    rank = jnp.sum(earlier.astype(I32), axis=0, keepdims=True)
    return owner_row * rows + rank * BS


def virtual_place(place, virtuals):
    blocks = place.shape[1]
    e, block = iota((virtuals, blocks), 0), iota((virtuals, blocks), 1)
    start = jnp.sum(jnp.where(e // BS == block, place, 0), axis=1, keepdims=True)
    return start + iota((virtuals, 1), 0) % BS


def wide_flags(partner, sizes):
    wide = jnp.zeros_like(partner)
    for h in range(sizes.shape[0]):
        wide = jnp.where(partner == h, (sizes[h] > HALF).astype(I32), wide)
    return wide


def wide_block(block, wanted, sizes):
    wide = jnp.zeros_like(block ^ wanted)
    for r in range(BS):
        wide = wide | wide_flags(irrep_of(block * BS + r, sizes) ^ wanted, sizes)
    return wide


def slots_needed(wide, owned):
    return wide + (owned - wide + 1) // 2


def slots_of(wide, rank, rank_wide, count_wide):
    rank_narrow = rank - rank_wide
    slot = jnp.where(wide == 1, rank_wide, count_wide + rank_narrow // 2)
    return slot, jnp.where(wide == 1, 0, 1 + rank_narrow % 2)


def pack_kernel(
    rows_out,
    classes,
    sizes_hbm,
    occ_hbm,
    pair,
    owner_hbm,
    t_hbm,
    *refs,
):
    outs, choice = refs[: len(classes)], refs[len(classes)]
    sizes, occ, owner_row, t_vmem, folds, filled, out, in_sems, out_sems = refs[len(classes) + 1 :]
    virtuals = t_hbm.shape[1]
    blocks = owner_row.shape[1]
    chips = outs[0].shape[0] // 2
    quarter = HALF // 2
    pairs = (
        (owner_hbm, owner_row),
        (sizes_hbm, sizes),
        (occ_hbm, occ),
        (t_hbm.at[0], t_vmem),
    )
    copies = [
        pltpu.make_async_copy(source, here, in_sems.at[i])
        for i, (source, here) in enumerate(pairs)
    ]
    for copy in copies:
        copy.start()
    copies[0].wait()
    chip_row = owner_row[...] // 2
    first, second = iota((blocks, blocks), 0), iota((blocks, blocks), 1)
    chip_col = jnp.sum(jnp.where(first == second, chip_row, 0), axis=1, keepdims=True)
    same = chip_col == chip_row
    before = jnp.where(same & (first < second), 1.0, 0.0).astype(BF16)
    same = jnp.where(same, 1.0, 0.0).astype(BF16)
    for copy in copies[1:3]:
        copy.wait()
    wanted = pair[0] ^ occ[lax.axis_index("vir")]
    row = iota((8, blocks), 0)
    wide_all = wide_block(iota((1, blocks), 1), row, sizes)
    own = jnp.sum(jnp.where(row == wanted, wide_all, 0), axis=0, keepdims=True)
    rest = jnp.where(row == 0, own, jnp.where(row == 1, 1, 0))
    tallies = jnp.concatenate([wide_all, rest], axis=0).astype(F32).astype(BF16)
    partner = irrep_of(iota((virtuals, 1), 0), sizes) ^ wanted
    partner = jnp.broadcast_to(partner, (virtuals, HALF)).astype(I16)
    label_a = irrep_of(iota((1, virtuals), 1), sizes).astype(I16)
    copies[3].wait()
    halves = [jnp.zeros((virtuals, HALF), BF16) for _ in range(2)]
    for i, k in enumerate(range(0, virtuals, HALF)):
        here = partner == label_a[:, k : k + HALF]
        kept = jnp.where(here, t_vmem[:, k : k + HALF], jnp.zeros((), BF16))
        halves[i % 2] = halves[i % 2] + kept
    for h in range(2):
        folds[h] = halves[h].astype(F32)
    ahead = jnp.dot(tallies, before, preferred_element_type=F32).astype(I32)
    total = jnp.dot(tallies, same, preferred_element_type=F32).astype(I32)
    owned = total[9:10]

    index = jnp.int32(0)
    if len(classes) > 1:
        used = jnp.int32(0)
        for m in range(occ.shape[0]):
            used = used | (jnp.int32(1) << (pair[0] ^ occ[m]))
        need = slots_needed(total[:8], owned) * ((used >> row) & 1)
        need = jnp.max(need) * BS
        for size in classes[:-1]:
            index = index + (need > size).astype(I32)
    choice[0] = index

    step = ALIGN // BS
    chip = iota((chips, 1), 0)
    lengths = jnp.where(chip == chip_row, slots_needed(total[8:9], owned), 0)
    lengths = (jnp.max(lengths, axis=1, keepdims=True) + (step - 1)) // step
    starts_row = jnp.sum(jnp.where(chip < chip_row, lengths, 0), axis=0, keepdims=True)
    starts = [jnp.sum(jnp.where(chip < q, lengths, 0)) for q in range(chips)]
    slot, kind = slots_of(own, ahead[9:10], ahead[8:9], total[8:9])
    place = starts_row * step + slot
    targets = [jnp.where(kind == 2, -1, place), jnp.where(kind == 1, -1, place)]

    first, second = iota((blocks, blocks), 0), iota((blocks, blocks), 1)
    narrow = jnp.sum(jnp.where(first == second, own, 0), axis=1, keepdims=True) == 0
    blank = jnp.zeros((blocks, quarter), F32)
    sources = [[[], []], [[], []]]
    for r in range(BS):
        both = [folds[h, pl.ds(r, blocks, stride=BS), :] for h in range(2)]
        for h in range(2):
            source = both[h] + jnp.where(narrow, both[1 - h], 0.0)
            if rows_out < quarter:
                old, new = iota((HALF, HALF), 0), iota((HALF, HALF), 1)
                core, x = new // quarter, new % quarter
                lane = x // rows_out * (2 * rows_out) + core * rows_out + x % rows_out
                order = jnp.where(old == lane, 1.0, 0.0).astype(BF16)
                source = jnp.dot(source.astype(BF16), order, preferred_element_type=F32)
            for core in range(2):
                side = source[:, core * quarter : (core + 1) * quarter]
                sources[core][h] += [blank, side] if h else [side, blank]
    count = filled.shape[1] // BS
    slot = iota((count, 1), 0)
    hot = jnp.concatenate([jnp.where(x == slot, 1.0, 0.0) for x in targets], axis=1).astype(BF16)

    def send(k, device):
        start = pl.multiple_of(starts[device // 2] * ALIGN, ALIGN)
        return pltpu.make_async_copy(
            out.at[device % 2, pl.ds(start, classes[k])],
            outs[k].at[device],
            out_sems.at[device],
        )

    def each(core, act):
        for k in range(len(classes)):

            @pl.when(index == k)
            def _(k=k):
                for device in range(core, 2 * chips, 2):
                    act(send(k, device))

    for core in range(2):
        source = [jnp.concatenate(x, axis=1) for x in sources[core]]
        source = jnp.concatenate(source, axis=0).astype(BF16)
        moved = jnp.dot(hot, source, preferred_element_type=F32)
        for r in range(BS):
            part = slice(r * HALF, (r + 1) * HALF)
            filled[core, pl.ds(r, count, stride=BS), :] = moved[:, part]
        out[core, : filled.shape[1]] = filled[core].astype(BF16)
        rest = out.shape[1] - filled.shape[1]
        out[core, filled.shape[1] :] = jnp.zeros((rest, HALF), BF16)
        each(core, lambda copy: copy.start())
    for core in range(2):
        each(core, lambda copy: copy.wait())


def label_kernel(
    rows,
    rows_out,
    sizes,
    occ,
    pair,
    j_irrep,
    owner_row,
    label_row,
    label_k,
    slots,
    kinds,
    label_kept,
    label_out,
    keys,
):
    here = lax.axis_index("vir")
    occupied, lanes = label_k.shape
    virtuals = owner_row.shape[1] * BS
    target = virtual_place(block_place(owner_row[...], rows), virtuals)
    lane = iota((virtuals, lanes), 1)
    source = jnp.where(lane < rows, lane + here * rows, lane - rows + (here ^ 1) * rows)
    virtual = iota((virtuals, lanes), 0)
    e_row = jnp.sum(jnp.where(target == source, virtual + 1, 0), axis=0, keepdims=True) - 1
    label = irrep_of(e_row, sizes)
    label_row[...] = label[:, :rows]
    m_row = iota((occupied, 1), 0)
    wanted = jnp.zeros((occupied, 1), I32)
    for m in range(occupied):
        wanted = jnp.where(m_row == m, pair[0] ^ occ[m], wanted)
    partner = label ^ wanted
    label_k[...] = partner
    first, second = iota((lanes, lanes), 0), iota((lanes, lanes), 1)
    e_col = jnp.sum(jnp.where(first == second, e_row, 0), axis=1, keepdims=True)
    ahead = (e_col >= 0) & (e_col % BS == 0) & (e_col // BS < e_row // BS)
    wide = jnp.where(e_row >= 0, wide_block(jnp.maximum(e_row, 0) // BS, wanted, sizes), 0)
    rank_wide = jnp.dot(
        wide.astype(F32).astype(BF16),
        jnp.where(ahead, 1.0, 0.0).astype(BF16),
        preferred_element_type=F32,
    ).astype(I32)
    rank = jnp.sum(ahead.astype(I32), axis=0, keepdims=True)
    count_wide = jnp.sum(wide, axis=1, keepdims=True) // BS
    slot, kind = slots_of(wide, rank, rank_wide, count_wide)
    slots[...] = jnp.where(e_row >= 0, slot * BS + e_row % BS, -1)
    kinds[...] = kind
    row = iota(label_kept.shape, 0)
    a = row // rows_out * (2 * rows_out) + here % 2 * rows_out + row % rows_out
    label_kept[...] = irrep_of(a, sizes)
    label_out[...] = irrep_of(iota(label_out.shape, 0) + here * rows_out, sizes) ^ pair[0]
    keys[...] = jnp.broadcast_to(column_keys(keys.shape[1], sizes, j_irrep), keys.shape)


def fold_kernel(first, occ, label_row, keys, w, out, folded):
    step, part = pl.program_id(0), pl.program_id(1)
    row_block, m_block, columns = w.shape
    wide = out.shape[2]
    m_row = iota((m_block, 1), 0)
    occ_col = jnp.zeros((m_block, 1), I32)
    for i in range(m_block):
        occ_col = jnp.where(m_row == i, occ[part * m_block + i], occ_col)

    @pl.loop(0, row_block // 4)
    def _(quad):
        for i in range(4):
            row = quad * 4 + i
            label = label_row[first + step * row_block + row]
            allowed = (occ_col ^ label) == keys[:1, :]
            kept = jnp.where(allowed, w[row].astype(F32), 0.0)
            total = kept[:, :wide]
            for k in range(1, columns // wide):
                total = total + kept[:, k * wide : (k + 1) * wide]
            here = pl.ds(pl.multiple_of(row * m_block, m_block), m_block)
            for k in range(wide // 128):
                folded[k, here, :] = total[:, k * 128 : (k + 1) * 128]

    for i in range(m_block):
        for k in range(wide // 128):
            out[i, :, k * 128 : (k + 1) * 128] = folded[
                k, pl.ds(i, row_block, stride=m_block), :
            ].astype(BF16)


def product_kernel(pieces, label_k, slots, kinds, label_kept, packed, *refs):
    own, mate_hbm = refs[:pieces], refs[pieces : 2 * pieces]
    coded, out, t, mate, sems = refs[2 * pieces :]
    occupied, half, lanes = t.shape
    rows = lanes // 2
    kept = out.shape[0]
    size = rows // pieces
    copies = [
        pltpu.make_async_copy(mate_hbm[i], mate.at[:, i * size : (i + 1) * size], sems.at[i])
        for i in range(pieces)
    ]
    for copy in copies:
        copy.start()
    slot = iota((packed.shape[1], 1), 0)
    unpacked = max(1, min(occupied, 8))

    @pl.loop(0, occupied // unpacked)
    def _(step):
        for i in range(unpacked):
            m = step * unpacked + i
            hot = jnp.where(slots[pl.ds(m, 1), :] == slot, 1.0, 0.0).astype(BF16)
            both = lax.dot_general(
                packed[m], hot, (((0,), (0,)), ((), ())), preferred_element_type=F32
            )
            low, high = both[: half // 2], both[half // 2 :]
            kind = kinds[pl.ds(m, 1), :]
            t[m] = jnp.concatenate(
                [jnp.where(kind == 2, high, low), jnp.where(kind == 1, low, high)], axis=0
            ).astype(BF16)

    wide_label = jnp.broadcast_to(label_kept[:, :1], (kept, rows))

    def expand(m, side):
        lane = slice(side * rows, (side + 1) * rows)
        wanted = label_k[pl.ds(m, 1), :][:, lane]
        values = t[m][:, lane].astype(F32)
        return jnp.concatenate(
            [
                jnp.where(wide_label[k : k + half] == wanted, values, 0.0).astype(BF16)
                for k in range(0, kept, half)
            ],
            axis=0,
        )

    def couplings(m, side):
        return mate[m] if side else jnp.concatenate([piece[m] for piece in own], axis=0)

    def arrived(side):
        for copy in copies if side else ():
            copy.wait()

    if rows % 128 == 0:
        for side in range(2):
            arrived(side)
            left = jnp.concatenate([expand(m, side) for m in range(occupied)], axis=1)
            right = jnp.concatenate([couplings(m, side) for m in range(occupied)], axis=0)
            total = jnp.dot(left, right, preferred_element_type=F32)
            out[...] = out[...] + total if side else total
    else:
        arrived(1)
        out[...] = jnp.zeros(out.shape, F32)

        @pl.loop(0, occupied)
        def _(m):
            for side in range(2):
                out[...] += jnp.dot(
                    expand(m, side), couplings(m, side), preferred_element_type=F32
                )

    rows_out = kept // coded.shape[0]
    for chip in range(coded.shape[0]):
        coded[chip] = encode(out[chip * rows_out : (chip + 1) * rows_out, :])


def encode(values):
    row = iota((PAD, 128), 0)
    scales = jnp.zeros((PAD, 128), I32)
    blocks = []
    for i in range(values.shape[1] // 128):
        part = values[:, i * 128 : (i + 1) * 128]
        largest = jnp.maximum(jnp.max(jnp.abs(part), axis=0, keepdims=True), SMALL)
        scale = jnp.floor(jnp.log2(largest) * STEPS) + 2.0
        factor = jnp.exp2(scale * (-0.5 / STEPS))
        blocks.append(jnp.floor(part * factor * (factor * TOP) + 0.5).astype(I32))
        scales = jnp.where(row == i, scale.astype(I32), scales)
    return jnp.concatenate(blocks + [scales], axis=0).astype(I16)


def decode(coded, rows_out):
    values = coded.astype(I32)
    blocks = []
    for i in range((coded.shape[0] - PAD) // rows_out):
        scale = values[coded.shape[0] - PAD + i :][:1].astype(F32)
        factor = jnp.exp2(scale * (0.5 / STEPS))
        part = values[i * rows_out : (i + 1) * rows_out].astype(F32)
        blocks.append(part * (factor * (1.0 / TOP)) * factor)
    return blocks


def finish_kernel(label_out, keys, parts, out):
    chips = parts.shape[0]
    rows_out = out.shape[0]
    total = decode(parts[0], rows_out)
    for q in range(1, chips):
        total = [x + y for x, y in zip(total, decode(parts[q], rows_out))]
    total = jnp.concatenate(total, axis=1)
    wide = total.shape[1]
    for k in range(0, out.shape[1], wide):
        out[:, k : k + wide] = jnp.where(
            label_out[:, :1] == keys[:1, k : k + wide], total, 0.0
        )


in_hbm = functools.partial(pltpu.with_memory_space_constraint, memory_space=pltpu.HBM)
in_vmem = functools.partial(pltpu.with_memory_space_constraint, memory_space=pltpu.VMEM)


def per_device(amplitudes, couplings, occ_irrep, pair_irrep, j_irrep, block_sizes, owner):
    devices = lax.axis_size("vir")
    chips = devices // 2
    virtuals = amplitudes.shape[2]
    rows, occupied, columns = couplings.shape
    wide = columns // virtuals * MOST
    rows_out = virtuals // devices
    kept = virtuals // 2
    lanes = 2 * rows
    blocks = owner.shape[0]
    smem = pl.BlockSpec(memory_space=pltpu.SMEM)
    vmem = pl.BlockSpec(memory_space=pltpu.VMEM)
    hbm = pl.BlockSpec(memory_space=pltpu.HBM)
    params = pltpu.CompilerParams(vmem_limit_bytes=LIMIT)

    classes = [lanes]
    if lanes % 256 == 0:
        classes = [lanes // 16 * part for part in (11, 12, 13, 14, 16)]
    owner_row = owner.reshape(1, blocks)
    *outgoing, choice = pl.pallas_call(
        functools.partial(pack_kernel, rows_out, classes),
        out_shape=[jax.ShapeDtypeStruct((devices, size, HALF), BF16) for size in classes]
        + [pltpu.SMEM((1,), I32)],
        in_specs=[hbm, hbm, smem, hbm, hbm],
        out_specs=[hbm] * len(classes) + [smem],
        scratch_shapes=[
            pltpu.SMEM(block_sizes.shape, I32),
            pltpu.SMEM(occ_irrep.shape, I32),
            pltpu.VMEM((1, blocks), I32),
            pltpu.VMEM((virtuals, virtuals), BF16),
            pltpu.VMEM((2, virtuals, HALF), F32),
            pltpu.VMEM((2, virtuals + chips * ALIGN, HALF), F32),
            pltpu.VMEM((2, virtuals + chips * ALIGN + lanes, HALF), BF16),
            pltpu.SemaphoreType.DMA((4,)),
            pltpu.SemaphoreType.DMA((devices,)),
        ],
        compiler_params=params,
        name="pack_amplitudes",
    )(
        in_hbm(block_sizes),
        in_hbm(occ_irrep),
        pair_irrep,
        in_hbm(owner_row),
        in_hbm(amplitudes),
    )

    def contract(packed):
        received = lax.all_to_all(packed, "vir", 0, 0)

        label_row, label_k, slots, kinds, label_kept, label_out, keys = pl.pallas_call(
            functools.partial(label_kernel, rows, rows_out),
            out_shape=(
                jax.ShapeDtypeStruct((1, rows), I32),
                jax.ShapeDtypeStruct((occupied, lanes), I32),
                jax.ShapeDtypeStruct((occupied, lanes), I32),
                jax.ShapeDtypeStruct((occupied, lanes), I32),
                jax.ShapeDtypeStruct((kept, 128), I32),
                jax.ShapeDtypeStruct((rows_out, 128), I32),
                jax.ShapeDtypeStruct((8, columns), I32),
            ),
            in_specs=[smem] * 4 + [vmem],
            out_specs=(vmem,) * 7,
            compiler_params=params,
            name="labels",
        )(block_sizes, occ_irrep, pair_irrep, j_irrep, owner_row)

        row_block, m_block = 16, 16
        pieces = max(1, rows // 32)
        piece_rows = rows // pieces
        w_own, w_mate = [], []
        for piece in range(pieces):
            first = piece * piece_rows
            w_own.append(
                pl.pallas_call(
                    functools.partial(fold_kernel, first),
                    out_shape=jax.ShapeDtypeStruct((occupied, piece_rows, wide), BF16),
                    grid=(piece_rows // row_block, occupied // m_block),
                    in_specs=[smem, smem, vmem]
                    + [
                        pl.BlockSpec(
                            (row_block, m_block, columns),
                            lambda i, j, skip=first // row_block: (skip + i, j, 0),
                        )
                    ],
                    out_specs=pl.BlockSpec((m_block, row_block, wide), lambda i, j: (j, i, 0)),
                    scratch_shapes=[pltpu.VMEM((wide // 128, row_block * m_block, 128), F32)],
                    compiler_params=params,
                    cost_estimate=pl.CostEstimate(
                        flops=4 * piece_rows * occupied * columns,
                        bytes_accessed=3 * piece_rows * occupied * columns,
                        transcendentals=0,
                    ),
                    name="fold_couplings",
                )(occ_irrep, label_row.reshape(rows), keys, in_hbm(couplings))
            )
            w_mate.append(lax.ppermute(w_own[-1], "vir", [(d, d ^ 1) for d in range(devices)]))

        partial = pl.pallas_call(
            functools.partial(product_kernel, pieces),
            out_shape=jax.ShapeDtypeStruct((chips, wide // 128 * rows_out + PAD, 128), I16),
            in_specs=[vmem] * (5 + pieces) + [hbm] * pieces,
            out_specs=vmem,
            scratch_shapes=[
                pltpu.VMEM((kept, wide), F32),
                pltpu.VMEM((occupied, HALF, lanes), BF16),
                pltpu.VMEM((occupied, rows, wide), BF16),
                pltpu.SemaphoreType.DMA((pieces,)),
            ],
            compiler_params=params,
            name="multiply",
        )(
            *[in_vmem(x) for x in (label_k, slots, kinds, label_kept, received, *w_own)],
            *[in_hbm(x) for x in w_mate],
        )
        sides = [[d for d in range(devices) if d % 2 == core] for core in (0, 1)]
        parts = lax.all_to_all(partial, "vir", 0, 0, axis_index_groups=sides)
        return pl.pallas_call(
            finish_kernel,
            out_shape=pltpu.HBM((rows_out, columns), F32),
            in_specs=[vmem] * 3,
            out_specs=vmem,
            compiler_params=params,
            name="unfold",
        )(label_out, keys, parts)

    if len(classes) == 1:
        return contract(outgoing[0])
    branches = [lambda *packed, k=k: contract(packed[k]) for k in range(len(classes))]
    return lax.switch(choice[0], branches, *outgoing)


def solution(mesh):
    return jax.shard_map(
        per_device,
        mesh=mesh,
        in_specs=(
            P(("grp", "vir"), None, None),
            P(("grp", "vir"), None, None),
            P("grp"),
            P(),
            P(),
            P("grp"),
            P("grp", None),
        ),
        out_specs=P(("grp", "vir"), None),
        check_vma=False,
    )
```

```python
import functools

import jax
import jax.numpy as jnp
from jax import lax
from jax.experimental import pallas as pl
from jax.experimental.pallas import tpu as pltpu
from jax.sharding import PartitionSpec as P

BS = 4
MOST = 256
LIMIT = 24 * 1024 * 1024
F32, BF16, I32, I16 = jnp.float32, jnp.bfloat16, jnp.int32, jnp.int16
TOP = 32767.0
STEPS = 256.0
SMALL = 2.0**-126
HALF = MOST // 2
ALIGN = 16
PAD = 16


def irrep_of(index, sizes):
    label = jnp.zeros_like(index)
    end = jnp.int32(0)
    for h in range(sizes.shape[0] - 1):
        end = end + sizes[h]
        label = jnp.where(index >= end, h + 1, label)
    return label


def iota(shape, dim):
    return lax.broadcasted_iota(I32, shape, dim)


def column_keys(columns, sizes, j_irrep):
    count = j_irrep.shape[0]
    column = iota((1, columns), 1)
    j = column % count
    j_label = jnp.zeros_like(column)
    for i in range(count):
        j_label = jnp.where(j == i, j_irrep[i], j_label)
    return irrep_of(column // count, sizes) ^ j_label


def block_place(owner_row, rows):
    blocks = owner_row.shape[1]
    first, second = iota((blocks, blocks), 0), iota((blocks, blocks), 1)
    owner_col = jnp.sum(jnp.where(first == second, owner_row, 0), axis=1, keepdims=True)
    earlier = (owner_col == owner_row) & (first < second)
    rank = jnp.sum(earlier.astype(I32), axis=0, keepdims=True)
    return owner_row * rows + rank * BS


def virtual_place(place, virtuals):
    blocks = place.shape[1]
    e, block = iota((virtuals, blocks), 0), iota((virtuals, blocks), 1)
    start = jnp.sum(jnp.where(e // BS == block, place, 0), axis=1, keepdims=True)
    return start + iota((virtuals, 1), 0) % BS


def wide_flags(partner, sizes):
    wide = jnp.zeros_like(partner)
    for h in range(sizes.shape[0]):
        wide = jnp.where(partner == h, (sizes[h] > HALF).astype(I32), wide)
    return wide


def wide_block(block, wanted, sizes):
    wide = jnp.zeros_like(block ^ wanted)
    for r in range(BS):
        wide = wide | wide_flags(irrep_of(block * BS + r, sizes) ^ wanted, sizes)
    return wide


def slots_needed(wide, owned):
    return wide + (owned - wide + 1) // 2


def slots_of(wide, rank, rank_wide, count_wide):
    rank_narrow = rank - rank_wide
    slot = jnp.where(wide == 1, rank_wide, count_wide + rank_narrow // 2)
    return slot, jnp.where(wide == 1, 0, 1 + rank_narrow % 2)


def pack_kernel(
    rows_out,
    classes,
    sizes_hbm,
    occ_hbm,
    pair,
    owner_hbm,
    t_hbm,
    *refs,
):
    outs, choice = refs[: len(classes)], refs[len(classes)]
    sizes, occ, owner_row, t_vmem, folds, filled, out, in_sems, out_sems = refs[len(classes) + 1 :]
    virtuals = t_hbm.shape[1]
    blocks = owner_row.shape[1]
    chips = outs[0].shape[0] // 2
    quarter = HALF // 2
    pairs = (
        (owner_hbm, owner_row),
        (sizes_hbm, sizes),
        (occ_hbm, occ),
        (t_hbm.at[0], t_vmem),
    )
    copies = [
        pltpu.make_async_copy(source, here, in_sems.at[i])
        for i, (source, here) in enumerate(pairs)
    ]
    for copy in copies:
        copy.start()
    copies[0].wait()
    chip_row = owner_row[...] // 2
    first, second = iota((blocks, blocks), 0), iota((blocks, blocks), 1)
    chip_col = jnp.sum(jnp.where(first == second, chip_row, 0), axis=1, keepdims=True)
    same = chip_col == chip_row
    before = jnp.where(same & (first < second), 1.0, 0.0).astype(BF16)
    same = jnp.where(same, 1.0, 0.0).astype(BF16)
    for copy in copies[1:3]:
        copy.wait()
    wanted = pair[0] ^ occ[lax.axis_index("vir")]
    row = iota((8, blocks), 0)
    wide_all = wide_block(iota((1, blocks), 1), row, sizes)
    own = jnp.sum(jnp.where(row == wanted, wide_all, 0), axis=0, keepdims=True)
    rest = jnp.where(row == 0, own, jnp.where(row == 1, 1, 0))
    tallies = jnp.concatenate([wide_all, rest], axis=0).astype(F32).astype(BF16)
    partner = irrep_of(iota((virtuals, 1), 0), sizes) ^ wanted
    partner = jnp.broadcast_to(partner, (virtuals, HALF)).astype(I16)
    label_a = irrep_of(iota((1, virtuals), 1), sizes).astype(I16)
    copies[3].wait()
    halves = [jnp.zeros((virtuals, HALF), BF16) for _ in range(2)]
    for i, k in enumerate(range(0, virtuals, HALF)):
        here = partner == label_a[:, k : k + HALF]
        kept = jnp.where(here, t_vmem[:, k : k + HALF], jnp.zeros((), BF16))
        halves[i % 2] = halves[i % 2] + kept
    for h in range(2):
        folds[h] = halves[h].astype(F32)
    ahead = jnp.dot(tallies, before, preferred_element_type=F32).astype(I32)
    total = jnp.dot(tallies, same, preferred_element_type=F32).astype(I32)
    owned = total[9:10]

    index = jnp.int32(0)
    if len(classes) > 1:
        used = jnp.int32(0)
        for m in range(occ.shape[0]):
            used = used | (jnp.int32(1) << (pair[0] ^ occ[m]))
        need = slots_needed(total[:8], owned) * ((used >> row) & 1)
        need = jnp.max(need) * BS
        for size in classes[:-1]:
            index = index + (need > size).astype(I32)
    choice[0] = index

    step = ALIGN // BS
    chip = iota((chips, 1), 0)
    lengths = jnp.where(chip == chip_row, slots_needed(total[8:9], owned), 0)
    lengths = (jnp.max(lengths, axis=1, keepdims=True) + (step - 1)) // step
    starts_row = jnp.sum(jnp.where(chip < chip_row, lengths, 0), axis=0, keepdims=True)
    starts = [jnp.sum(jnp.where(chip < q, lengths, 0)) for q in range(chips)]
    slot, kind = slots_of(own, ahead[9:10], ahead[8:9], total[8:9])
    place = starts_row * step + slot
    targets = [jnp.where(kind == 2, -1, place), jnp.where(kind == 1, -1, place)]

    first, second = iota((blocks, blocks), 0), iota((blocks, blocks), 1)
    narrow = jnp.sum(jnp.where(first == second, own, 0), axis=1, keepdims=True) == 0
    blank = jnp.zeros((blocks, quarter), F32)
    sources = [[[], []], [[], []]]
    for r in range(BS):
        both = [folds[h, pl.ds(r, blocks, stride=BS), :] for h in range(2)]
        for h in range(2):
            source = both[h] + jnp.where(narrow, both[1 - h], 0.0)
            if rows_out < quarter:
                old, new = iota((HALF, HALF), 0), iota((HALF, HALF), 1)
                core, x = new // quarter, new % quarter
                lane = x // rows_out * (2 * rows_out) + core * rows_out + x % rows_out
                order = jnp.where(old == lane, 1.0, 0.0).astype(BF16)
                source = jnp.dot(source.astype(BF16), order, preferred_element_type=F32)
            for core in range(2):
                side = source[:, core * quarter : (core + 1) * quarter]
                sources[core][h] += [blank, side] if h else [side, blank]
    count = filled.shape[1] // BS
    slot = iota((count, 1), 0)
    hot = jnp.concatenate([jnp.where(x == slot, 1.0, 0.0) for x in targets], axis=1).astype(BF16)

    def send(k, device):
        start = pl.multiple_of(starts[device // 2] * ALIGN, ALIGN)
        return pltpu.make_async_copy(
            out.at[device % 2, pl.ds(start, classes[k])],
            outs[k].at[device],
            out_sems.at[device],
        )

    def each(core, act):
        for k in range(len(classes)):

            @pl.when(index == k)
            def _(k=k):
                for device in range(core, 2 * chips, 2):
                    act(send(k, device))

    for core in range(2):
        source = [jnp.concatenate(x, axis=1) for x in sources[core]]
        source = jnp.concatenate(source, axis=0).astype(BF16)
        moved = jnp.dot(hot, source, preferred_element_type=F32)
        for r in range(BS):
            part = slice(r * HALF, (r + 1) * HALF)
            filled[core, pl.ds(r, count, stride=BS), :] = moved[:, part]
        out[core, : filled.shape[1]] = filled[core].astype(BF16)
        rest = out.shape[1] - filled.shape[1]
        out[core, filled.shape[1] :] = jnp.zeros((rest, HALF), BF16)
        each(core, lambda copy: copy.start())
    for core in range(2):
        each(core, lambda copy: copy.wait())


def label_kernel(
    rows,
    rows_out,
    sizes,
    occ,
    pair,
    j_irrep,
    owner_row,
    label_row,
    label_k,
    slots,
    kinds,
    label_kept,
    label_out,
    keys,
):
    here = lax.axis_index("vir")
    occupied, lanes = label_k.shape
    virtuals = owner_row.shape[1] * BS
    target = virtual_place(block_place(owner_row[...], rows), virtuals)
    lane = iota((virtuals, lanes), 1)
    source = jnp.where(lane < rows, lane + here * rows, lane - rows + (here ^ 1) * rows)
    virtual = iota((virtuals, lanes), 0)
    e_row = jnp.sum(jnp.where(target == source, virtual + 1, 0), axis=0, keepdims=True) - 1
    label = irrep_of(e_row, sizes)
    label_row[...] = label[:, :rows]
    m_row = iota((occupied, 1), 0)
    wanted = jnp.zeros((occupied, 1), I32)
    for m in range(occupied):
        wanted = jnp.where(m_row == m, pair[0] ^ occ[m], wanted)
    partner = label ^ wanted
    label_k[...] = partner
    first, second = iota((lanes, lanes), 0), iota((lanes, lanes), 1)
    e_col = jnp.sum(jnp.where(first == second, e_row, 0), axis=1, keepdims=True)
    ahead = (e_col >= 0) & (e_col % BS == 0) & (e_col // BS < e_row // BS)
    wide = jnp.where(e_row >= 0, wide_block(jnp.maximum(e_row, 0) // BS, wanted, sizes), 0)
    rank_wide = jnp.dot(
        wide.astype(F32).astype(BF16),
        jnp.where(ahead, 1.0, 0.0).astype(BF16),
        preferred_element_type=F32,
    ).astype(I32)
    rank = jnp.sum(ahead.astype(I32), axis=0, keepdims=True)
    count_wide = jnp.sum(wide, axis=1, keepdims=True) // BS
    slot, kind = slots_of(wide, rank, rank_wide, count_wide)
    slots[...] = jnp.where(e_row >= 0, slot * BS + e_row % BS, -1)
    kinds[...] = kind
    row = iota(label_kept.shape, 0)
    a = row // rows_out * (2 * rows_out) + here % 2 * rows_out + row % rows_out
    label_kept[...] = irrep_of(a, sizes)
    label_out[...] = irrep_of(iota(label_out.shape, 0) + here * rows_out, sizes) ^ pair[0]
    keys[...] = jnp.broadcast_to(column_keys(keys.shape[1], sizes, j_irrep), keys.shape)


def fold_kernel(first, occ, label_row, keys, w, out, folded):
    step, part = pl.program_id(0), pl.program_id(1)
    row_block, m_block, columns = w.shape
    wide = out.shape[2]
    m_row = iota((m_block, 1), 0)
    occ_col = jnp.zeros((m_block, 1), I32)
    for i in range(m_block):
        occ_col = jnp.where(m_row == i, occ[part * m_block + i], occ_col)

    @pl.loop(0, row_block // 4)
    def _(quad):
        for i in range(4):
            row = quad * 4 + i
            label = label_row[first + step * row_block + row]
            allowed = (occ_col ^ label) == keys[:1, :]
            kept = jnp.where(allowed, w[row].astype(F32), 0.0)
            total = kept[:, :wide]
            for k in range(1, columns // wide):
                total = total + kept[:, k * wide : (k + 1) * wide]
            here = pl.ds(pl.multiple_of(row * m_block, m_block), m_block)
            for k in range(wide // 128):
                folded[k, here, :] = total[:, k * 128 : (k + 1) * 128]

    for i in range(m_block):
        for k in range(wide // 128):
            out[i, :, k * 128 : (k + 1) * 128] = folded[
                k, pl.ds(i, row_block, stride=m_block), :
            ].astype(BF16)


def product_kernel(pieces, label_k, slots, kinds, label_kept, packed, *refs):
    own, mate_hbm = refs[:pieces], refs[pieces : 2 * pieces]
    coded, out, t, mate, sems = refs[2 * pieces :]
    occupied, half, lanes = t.shape
    rows = lanes // 2
    kept = out.shape[0]
    size = rows // pieces
    copies = [
        pltpu.make_async_copy(mate_hbm[i], mate.at[:, i * size : (i + 1) * size], sems.at[i])
        for i in range(pieces)
    ]
    for copy in copies:
        copy.start()
    slot = iota((packed.shape[1], 1), 0)
    unpacked = max(1, min(occupied, 8))

    @pl.loop(0, occupied // unpacked)
    def _(step):
        for i in range(unpacked):
            m = step * unpacked + i
            hot = jnp.where(slots[pl.ds(m, 1), :] == slot, 1.0, 0.0).astype(BF16)
            both = lax.dot_general(
                packed[m], hot, (((0,), (0,)), ((), ())), preferred_element_type=F32
            )
            low, high = both[: half // 2], both[half // 2 :]
            kind = kinds[pl.ds(m, 1), :]
            t[m] = jnp.concatenate(
                [jnp.where(kind == 2, high, low), jnp.where(kind == 1, low, high)], axis=0
            ).astype(BF16)

    wide_label = jnp.broadcast_to(label_kept[:, :1], (kept, rows))

    def expand(m, side):
        lane = slice(side * rows, (side + 1) * rows)
        wanted = label_k[pl.ds(m, 1), :][:, lane]
        values = t[m][:, lane].astype(F32)
        return jnp.concatenate(
            [
                jnp.where(wide_label[k : k + half] == wanted, values, 0.0).astype(BF16)
                for k in range(0, kept, half)
            ],
            axis=0,
        )

    def couplings(m, side):
        return mate[m] if side else jnp.concatenate([piece[m] for piece in own], axis=0)

    def arrived(side):
        for copy in copies if side else ():
            copy.wait()

    if rows % 128 == 0:
        for side in range(2):
            arrived(side)
            left = jnp.concatenate([expand(m, side) for m in range(occupied)], axis=1)
            right = jnp.concatenate([couplings(m, side) for m in range(occupied)], axis=0)
            total = jnp.dot(left, right, preferred_element_type=F32)
            out[...] = out[...] + total if side else total
    else:
        arrived(1)
        out[...] = jnp.zeros(out.shape, F32)

        @pl.loop(0, occupied)
        def _(m):
            for side in range(2):
                out[...] += jnp.dot(
                    expand(m, side), couplings(m, side), preferred_element_type=F32
                )

    rows_out = kept // coded.shape[0]
    for chip in range(coded.shape[0]):
        coded[chip] = encode(out[chip * rows_out : (chip + 1) * rows_out, :])


def encode(values):
    row = iota((PAD, 128), 0)
    scales = jnp.zeros((PAD, 128), I32)
    blocks = []
    for i in range(values.shape[1] // 128):
        part = values[:, i * 128 : (i + 1) * 128]
        largest = jnp.maximum(jnp.max(jnp.abs(part), axis=0, keepdims=True), SMALL)
        scale = jnp.floor(jnp.log2(largest) * STEPS) + 2.0
        factor = jnp.exp2(scale * (-0.5 / STEPS))
        blocks.append(jnp.floor(part * factor * (factor * TOP) + 0.5).astype(I32))
        scales = jnp.where(row == i, scale.astype(I32), scales)
    return jnp.concatenate(blocks + [scales], axis=0).astype(I16)


def decode(coded, rows_out):
    values = coded.astype(I32)
    blocks = []
    for i in range((coded.shape[0] - PAD) // rows_out):
        scale = values[coded.shape[0] - PAD + i :][:1].astype(F32)
        factor = jnp.exp2(scale * (0.5 / STEPS))
        part = values[i * rows_out : (i + 1) * rows_out].astype(F32)
        blocks.append(part * (factor * (1.0 / TOP)) * factor)
    return blocks


def finish_kernel(label_out, keys, parts, out):
    chips = parts.shape[0]
    rows_out = out.shape[0]
    total = decode(parts[0], rows_out)
    for q in range(1, chips):
        total = [x + y for x, y in zip(total, decode(parts[q], rows_out))]
    total = jnp.concatenate(total, axis=1)
    wide = total.shape[1]
    for k in range(0, out.shape[1], wide):
        out[:, k : k + wide] = jnp.where(
            label_out[:, :1] == keys[:1, k : k + wide], total, 0.0
        )


in_hbm = functools.partial(pltpu.with_memory_space_constraint, memory_space=pltpu.HBM)
in_vmem = functools.partial(pltpu.with_memory_space_constraint, memory_space=pltpu.VMEM)


def per_device(amplitudes, couplings, occ_irrep, pair_irrep, j_irrep, block_sizes, owner):
    devices = lax.axis_size("vir")
    chips = devices // 2
    virtuals = amplitudes.shape[2]
    rows, occupied, columns = couplings.shape
    wide = columns // virtuals * MOST
    rows_out = virtuals // devices
    kept = virtuals // 2
    lanes = 2 * rows
    blocks = owner.shape[0]
    smem = pl.BlockSpec(memory_space=pltpu.SMEM)
    vmem = pl.BlockSpec(memory_space=pltpu.VMEM)
    hbm = pl.BlockSpec(memory_space=pltpu.HBM)
    params = pltpu.CompilerParams(vmem_limit_bytes=LIMIT)

    classes = [lanes]
    if lanes % 256 == 0:
        classes = [lanes // 16 * part for part in (11, 12, 13, 14, 16)]
    owner_row = owner.reshape(1, blocks)
    *outgoing, choice = pl.pallas_call(
        functools.partial(pack_kernel, rows_out, classes),
        out_shape=[jax.ShapeDtypeStruct((devices, size, HALF), BF16) for size in classes]
        + [pltpu.SMEM((1,), I32)],
        in_specs=[hbm, hbm, smem, hbm, hbm],
        out_specs=[hbm] * len(classes) + [smem],
        scratch_shapes=[
            pltpu.SMEM(block_sizes.shape, I32),
            pltpu.SMEM(occ_irrep.shape, I32),
            pltpu.VMEM((1, blocks), I32),
            pltpu.VMEM((virtuals, virtuals), BF16),
            pltpu.VMEM((2, virtuals, HALF), F32),
            pltpu.VMEM((2, virtuals + chips * ALIGN, HALF), F32),
            pltpu.VMEM((2, virtuals + chips * ALIGN + lanes, HALF), BF16),
            pltpu.SemaphoreType.DMA((4,)),
            pltpu.SemaphoreType.DMA((devices,)),
        ],
        compiler_params=params,
        name="pack_amplitudes",
    )(
        in_hbm(block_sizes),
        in_hbm(occ_irrep),
        pair_irrep,
        in_hbm(owner_row),
        in_hbm(amplitudes),
    )

    def contract(packed):
        received = lax.all_to_all(packed, "vir", 0, 0)

        label_row, label_k, slots, kinds, label_kept, label_out, keys = pl.pallas_call(
            functools.partial(label_kernel, rows, rows_out),
            out_shape=(
                jax.ShapeDtypeStruct((1, rows), I32),
                jax.ShapeDtypeStruct((occupied, lanes), I32),
                jax.ShapeDtypeStruct((occupied, lanes), I32),
                jax.ShapeDtypeStruct((occupied, lanes), I32),
                jax.ShapeDtypeStruct((kept, 128), I32),
                jax.ShapeDtypeStruct((rows_out, 128), I32),
                jax.ShapeDtypeStruct((8, columns), I32),
            ),
            in_specs=[smem] * 4 + [vmem],
            out_specs=(vmem,) * 7,
            compiler_params=params,
            name="labels",
        )(block_sizes, occ_irrep, pair_irrep, j_irrep, owner_row)

        row_block, m_block = 16, 16
        pieces = max(1, rows // 32)
        piece_rows = rows // pieces
        w_own, w_mate = [], []
        for piece in range(pieces):
            first = piece * piece_rows
            w_own.append(
                pl.pallas_call(
                    functools.partial(fold_kernel, first),
                    out_shape=jax.ShapeDtypeStruct((occupied, piece_rows, wide), BF16),
                    grid=(piece_rows // row_block, occupied // m_block),
                    in_specs=[smem, smem, vmem]
                    + [
                        pl.BlockSpec(
                            (row_block, m_block, columns),
                            lambda i, j, skip=first // row_block: (skip + i, j, 0),
                        )
                    ],
                    out_specs=pl.BlockSpec((m_block, row_block, wide), lambda i, j: (j, i, 0)),
                    scratch_shapes=[pltpu.VMEM((wide // 128, row_block * m_block, 128), F32)],
                    compiler_params=params,
                    cost_estimate=pl.CostEstimate(
                        flops=4 * piece_rows * occupied * columns,
                        bytes_accessed=3 * piece_rows * occupied * columns,
                        transcendentals=0,
                    ),
                    name="fold_couplings",
                )(occ_irrep, label_row.reshape(rows), keys, in_hbm(couplings))
            )
            w_mate.append(lax.ppermute(w_own[-1], "vir", [(d, d ^ 1) for d in range(devices)]))

        partial = pl.pallas_call(
            functools.partial(product_kernel, pieces),
            out_shape=jax.ShapeDtypeStruct((chips, wide // 128 * rows_out + PAD, 128), I16),
            in_specs=[vmem] * (5 + pieces) + [hbm] * pieces,
            out_specs=vmem,
            scratch_shapes=[
                pltpu.VMEM((kept, wide), F32),
                pltpu.VMEM((occupied, HALF, lanes), BF16),
                pltpu.VMEM((occupied, rows, wide), BF16),
                pltpu.SemaphoreType.DMA((pieces,)),
            ],
            compiler_params=params,
            name="multiply",
        )(
            *[in_vmem(x) for x in (label_k, slots, kinds, label_kept, received, *w_own)],
            *[in_hbm(x) for x in w_mate],
        )
        sides = [[d for d in range(devices) if d % 2 == core] for core in (0, 1)]
        parts = lax.all_to_all(partial, "vir", 0, 0, axis_index_groups=sides)
        return pl.pallas_call(
            finish_kernel,
            out_shape=pltpu.HBM((rows_out, columns), F32),
            in_specs=[vmem] * 3,
            out_specs=vmem,
            compiler_params=params,
            name="unfold",
        )(label_out, keys, parts)

    if len(classes) == 1:
        return contract(outgoing[0])
    branches = [lambda *packed, k=k: contract(packed[k]) for k in range(len(classes))]
    return lax.switch(choice[0], branches, *outgoing)


def solution(mesh):
    return jax.shard_map(
        per_device,
        mesh=mesh,
        in_specs=(
            P(("grp", "vir"), None, None),
            P(("grp", "vir"), None, None),
            P("grp"),
            P(),
            P(),
            P("grp"),
            P("grp", None),
        ),
        out_specs=P(("grp", "vir"), None),
        check_vma=False,
    )
```
